32 devices in a mesh: rows: 8 (over y, x, core), imgs: 4 (over z).
Axes of the slice: x: 2, y: 2, z: 4, core: 2. Of those that a mesh axis runs over, the one named last changes fastest.
Arguments:
- images: bfloat16 [4, 128, 256, 180], P('imgs', 'rows'), may hold values from -6 to 6
- widths: int32 [4], P('imgs'), may hold values from 64 to 256, as said below
- norm1_gain: float32 [180], replicated, may hold values from 0.5 to 1.5
- norm1_bias: float32 [180], replicated, may hold values from -3 to 3
- qkv_weight: bfloat16 [180, 540], replicated, may hold values from -0.4375 to 0.4375
- qv_bias: float32 [360], replicated, may hold values from -3 to 3
- bias_table: float32 [225, 6], replicated, may hold values from -4 to 4
- proj_weight: bfloat16 [180, 180], replicated, may hold values from -1.25 to 1.25
- proj_bias: float32 [180], replicated, may hold values from -3 to 3
- norm2_gain: float32 [180], replicated, may hold values from 0.5 to 1.5
- norm2_bias: float32 [180], replicated, may hold values from -3 to 3
- fc1_weight: bfloat16 [180, 360], replicated, may hold values from -0.4375 to 0.4375
- fc1_bias: float32 [360], replicated, may hold values from -3 to 3
- fc2_weight: bfloat16 [360, 180], replicated, may hold values from -0.4375 to 0.4375
- fc2_bias: float32 [180], replicated, may hold values from -3 to 3
- conv_weight: bfloat16 [3, 3, 180, 180], replicated, may hold values from -0.15625 to 0.15625
- conv_bias: float32 [180], replicated, may hold values from -3 to 3
- cotangent: bfloat16 [4, 128, 256, 180], P('imgs', 'rows'), may hold values from -6 to 6
Outputs:
- result: bfloat16 [4, 128, 256, 180], P('imgs', 'rows')
- input_grad: bfloat16 [4, 128, 256, 180], P('imgs', 'rows')
- norm1_gain_grad: float32 [180], replicated
- norm1_bias_grad: float32 [180], replicated
- qkv_weight_grad: float32 [180, 540], replicated
- qv_bias_grad: float32 [360], replicated
- bias_table_grad: float32 [225, 6], replicated
- proj_weight_grad: float32 [180, 180], replicated
- proj_bias_grad: float32 [180], replicated
- norm2_gain_grad: float32 [180], replicated
- norm2_bias_grad: float32 [180], replicated
- fc1_weight_grad: float32 [180, 360], replicated
- fc1_bias_grad: float32 [360], replicated
- fc2_weight_grad: float32 [360, 180], replicated
- fc2_bias_grad: float32 [180], replicated
- conv_weight_grad: float32 [3, 3, 180, 180], replicated
- conv_bias_grad: float32 [180], replicated
The draws below stay inside these ranges and needn't reach their ends.
Inputs may be any that keep to these rules, and one draw needn't show every extreme that they name: `widths`: every width is a multiple of 8; one image of all is exactly 256 wide.
All inputs are finite; a program needn't handle non-finite values.
Results may differ from the reference program's by a relative error of at most 0.015.
Values may be sent and summed in bfloat16 or wider, within the bound.
A program may use at most 192 MiB of HBM per device.

```python
from functools import partial
import jax
import jax.numpy as jnp
from jax import lax

C = 180
HEADS = 6
HEAD_DIM = 30
HIDDEN_SIZE = 360
WIN = 8
SHIFT = 4
WIDTH = 256
TABLE = 225
HEIGHT = 128
IMGS = 4


def draw_widths(key, part):
    key = jax.random.fold_in(key, 7)
    steps = WIDTH // 8
    least = max(2, WIDTH // 32)
    spread = steps - least + 1
    first, second = jax.random.split(key)
    draws = jax.random.randint(first, (IMGS,), 0, spread).astype(jnp.int32)
    tail = draws * draws * draws // (spread * spread)
    picked = jax.random.randint(second, (), 0, IMGS).astype(jnp.int32)
    chosen = jnp.where(jnp.arange(IMGS).astype(jnp.int32) == picked, steps, least + tail)
    return (chosen * 8).astype(jnp.int32)


def block_scale(stream_key, shape, shards, low, high):
    level = 1.0
    for dim, shards_of in shards:
        steps = jax.random.uniform(jax.random.fold_in(jax.random.fold_in(stream_key, 6), dim), (shards_of,), jnp.float32, low / len(shards), high / len(shards))
        level = level * jnp.repeat(jnp.exp(steps), shape[dim] // shards_of).reshape((-1,) + (1,) * (len(shape) - 1 - dim))
    return level


def scatter_about(stream_key, shape, deviation, bound, pieces=(), kind=jnp.bfloat16):
    drawn = jax.random.normal(stream_key, shape, jnp.float32) * deviation
    if len(pieces) > 0:
        drawn = block_scale(stream_key, shape, pieces, -0.22, 0.18) * drawn
    return jnp.clip(drawn, min=-bound, max=bound).astype(kind)


def setup_inputs(seed: int = 0) -> dict:
    seeds = jax.random.split(jax.random.key(seed), 19)
    images = scatter_about(seeds[0], (IMGS, HEIGHT, WIDTH, C), 1.0, 6.0, ((0, 4), (1, 8)))
    widths = draw_widths(jax.random.fold_in(seeds[18], 71), 0)
    norm1_gain = jnp.clip(1.0 + 0.1 * jax.random.normal(seeds[2], (C,), jnp.float32), 0.5, 1.5)
    norm1_bias = scatter_about(seeds[3], (C,), 0.5, 3.0, (), jnp.float32)
    qkv_weight = scatter_about(seeds[4], (C, 3 * C), C ** -0.5, 0.4375)
    qv_bias = scatter_about(seeds[5], (2 * C,), 0.5, 3.0, (), jnp.float32)
    bias_table = scatter_about(seeds[6], (TABLE, HEADS), 1.0, 4.0, (), jnp.float32)
    proj_weight = scatter_about(seeds[7], (C, C), (C // 8) ** -0.5, 1.25)
    proj_bias = scatter_about(seeds[8], (C,), 0.5, 3.0, (), jnp.float32)
    norm2_gain = jnp.clip(1.0 + 0.1 * jax.random.normal(seeds[9], (C,), jnp.float32), 0.5, 1.5)
    norm2_bias = scatter_about(seeds[10], (C,), 0.5, 3.0, (), jnp.float32)
    fc1_weight = scatter_about(seeds[11], (C, HIDDEN_SIZE), C ** -0.5, 0.4375)
    fc1_bias = scatter_about(seeds[12], (HIDDEN_SIZE,), 0.5, 3.0, (), jnp.float32)
    fc2_weight = scatter_about(seeds[13], (HIDDEN_SIZE, C), (HIDDEN_SIZE // 2) ** -0.5, 0.4375)
    fc2_bias = scatter_about(seeds[14], (C,), 0.5, 3.0, (), jnp.float32)
    conv_weight = scatter_about(seeds[15], (3, 3, C, C), (9 * C) ** -0.5, 0.15625)
    conv_bias = scatter_about(seeds[16], (C,), 0.5, 3.0, (), jnp.float32)
    cotangent = scatter_about(seeds[17], (IMGS, HEIGHT, WIDTH, C), 1.0, 6.0, ((0, 4), (1, 8)))
    return {"images": images, "widths": widths, "norm1_gain": norm1_gain, "norm1_bias": norm1_bias, "qkv_weight": qkv_weight, "qv_bias": qv_bias, "bias_table": bias_table, "proj_weight": proj_weight, "proj_bias": proj_bias, "norm2_gain": norm2_gain, "norm2_bias": norm2_bias, "fc1_weight": fc1_weight, "fc1_bias": fc1_bias, "fc2_weight": fc2_weight, "fc2_bias": fc2_bias, "conv_weight": conv_weight, "conv_bias": conv_bias, "cotangent": cotangent}


@jax.custom_vjp
def low(v):
    return lax.optimization_barrier(v.astype(jnp.bfloat16)).astype(jnp.float32)

@jax.custom_vjp
def low_back(v):
    return v

def low_keep(v):
    return (low(v), None)

def low_pass(kept, grad):
    return (grad,)

def back_keep(v):
    return (v, None)

def back_low(kept, grad):
    return (low(grad),)
low.defvjp(low_keep, low_pass)
low_back.defvjp(back_keep, back_low)

def layer_norm(values, gain, shift):
    mean = lax.optimization_barrier(jnp.mean(values, axis=-1, keepdims=True))
    centred = values - mean
    spread = lax.optimization_barrier(jnp.mean(centred * centred, axis=-1, keepdims=True))
    return centred * lax.rsqrt(spread + 1e-05) * gain + shift

def to_windows(field, side):
    count, height, width, chans = field.shape
    tiles = field.reshape(count, height // side, side, width // side, side, chans)
    return tiles.transpose(0, 1, 3, 2, 4, 5).reshape(count, height // side * (width // side), side * side, chans)

def from_windows(tiles, height, width, side):
    count = tiles.shape[0]
    chans = tiles.shape[-1]
    field = tiles.reshape(count, height // side, width // side, side, side, chans)
    return field.transpose(0, 1, 3, 2, 4, 5).reshape(count, height, width, chans)

def relative_index(side):
    coords = jnp.arange(side * side)
    row_of = coords // side
    col_of = coords % side
    return ((row_of[:, None] - row_of[None, :] + side - 1) * (2 * side - 1) + col_of[:, None] - col_of[None, :] + side - 1).astype(jnp.int32)

def column_index(widths, width, offset):
    columns = jnp.arange(width).astype(jnp.int32)[None, :]
    limit = widths.astype(jnp.int32)[:, None]
    return jnp.where(columns < limit, (columns + offset) % limit, columns).astype(jnp.int32)

def move_columns(field, index):
    return jax.vmap(lambda plane, picks: jnp.take(plane, picks, axis=1))(field, index)

def region_mask(first_row, rows_here, height, widths, width, side, offset):
    glob_rows = first_row + jnp.arange(rows_here)
    row_band = jnp.where(glob_rows < height - side, 0, jnp.where(glob_rows < height - offset, 1, 2))
    columns = jnp.arange(width)[None, :]
    limit = widths.astype(jnp.int32)[:, None]
    col_band = jnp.where(columns < limit - side, 0, jnp.where(columns < limit - offset, 1, 2))
    region = (row_band[None, :, None] * 3 + col_band[:, None, :]).astype(jnp.int32)
    tiles = to_windows(region[:, :, :, None], side)[:, :, :, 0]
    return jnp.where(tiles[:, :, :, None] == tiles[:, :, None, :], 0.0, -100.0).astype(jnp.float32)

def forward(widths, source, norm1_gain, norm1_bias, qkv_weight, qv_bias, bias_table, proj_weight, proj_bias, norm2_gain, norm2_bias, fc1_weight, fc1_bias, fc2_weight, fc2_bias, conv_weight, conv_bias):
    highest = lax.Precision.HIGHEST
    count, height, width, chans = source.shape
    side = WIN
    scale = HEAD_DIM ** (-0.5)
    inside = (jnp.arange(width)[None, :] < widths[:, None]).astype(jnp.float32)[:, None, :, None]
    ahead = column_index(widths, width, SHIFT)
    behind = column_index(widths, width, -SHIFT)
    normed = low_back(low(layer_norm(source, norm1_gain, norm1_bias)))
    shifted = move_columns(jnp.roll(normed, -SHIFT, axis=1), ahead)
    tokens_win = to_windows(shifted, side)
    windows = tokens_win.shape[1]
    qkv_bias = jnp.concatenate([qv_bias[:chans], jnp.zeros((chans,), jnp.float32), qv_bias[chans:]])
    projected = jnp.einsum('bnic,co->bnio', tokens_win, qkv_weight, precision=highest) + qkv_bias
    projected = low_back(low(projected))
    split = projected.reshape(count, windows, side * side, 3, HEADS, HEAD_DIM)
    queries = split[:, :, :, 0]
    keys = split[:, :, :, 1]
    values = split[:, :, :, 2]
    lookup = relative_index(side)
    rel_bias = bias_table[lookup].transpose(2, 0, 1)
    masking = region_mask(0, height, height, widths, width, side, SHIFT)
    scores = jnp.einsum('bnihd,bnjhd->bnhij', queries, keys, precision=highest) * scale
    scores = low_back(scores + rel_bias[None, None] + masking[:, :, None])
    probs = low(jax.nn.softmax(scores, axis=-1))
    mixed = jnp.einsum('bnhij,bnjhd->bnihd', probs, values, precision=highest).reshape(count, windows, side * side, chans)
    mixed = low_back(low(mixed))
    restored = move_columns(jnp.roll(from_windows(mixed, height, width, side), SHIFT, axis=1), behind)
    branch = low_back(jnp.einsum('brwc,co->brwo', restored, proj_weight, precision=highest) + proj_bias)
    first_sum = source + branch
    normed2 = low_back(low(layer_norm(first_sum, norm2_gain, norm2_bias)))
    hidden = low_back(jnp.einsum('brwc,ch->brwh', normed2, fc1_weight, precision=highest) + fc1_bias)
    activated = low_back(low(jax.nn.gelu(hidden, approximate=False)))
    second_sum = first_sum + low_back(jnp.einsum('brwh,hc->brwc', activated, fc2_weight, precision=highest) + fc2_bias)
    layer_low = low(second_sum * inside)
    conv_out = lax.conv_general_dilated(layer_low, conv_weight, (1, 1), ((1, 1), (1, 1)), dimension_numbers=('NHWC', 'HWIO', 'NHWC'), precision=highest)
    return (conv_out + conv_bias + source) * inside

def reference(images, widths, norm1_gain, norm1_bias, qkv_weight, qv_bias, bias_table, proj_weight, proj_bias, norm2_gain, norm2_bias, fc1_weight, fc1_bias, fc2_weight, fc2_bias, conv_weight, conv_bias, cotangent):
    f32 = jnp.float32
    output, pullback = jax.vjp(partial(forward, widths.astype(jnp.int32)), images.astype(f32), norm1_gain.astype(f32), norm1_bias.astype(f32), qkv_weight.astype(f32), qv_bias.astype(f32), bias_table.astype(f32), proj_weight.astype(f32), proj_bias.astype(f32), norm2_gain.astype(f32), norm2_bias.astype(f32), fc1_weight.astype(f32), fc1_bias.astype(f32), fc2_weight.astype(f32), fc2_bias.astype(f32), conv_weight.astype(f32), conv_bias.astype(f32))
    grads = pullback(cotangent.astype(f32))
    return (output.astype(jnp.bfloat16), grads[0].astype(jnp.bfloat16), grads[1], grads[2], grads[3], grads[4], grads[5], grads[6], grads[7], grads[8], grads[9], grads[10], grads[11], grads[12], grads[13], grads[14], grads[15])
```

```python
import functools

import jax
import jax.numpy as jnp
import numpy as np
from jax import lax
from jax.experimental import pallas as pl
from jax.experimental.pallas import tpu as pltpu
from jax.sharding import PartitionSpec as P

HEADS = 6
HEAD_DIM = 30
WIN = 8
SHIFT = 4
C = 180
CP = 256
HID = 360
HP = 384
AREA = WIN * WIN
HI = HEADS * AREA
LOG2E = 1.4426950408889634
SCALE = HEAD_DIM ** (-0.5)

f32 = jnp.float32
bf16 = jnp.bfloat16


def dot(a, b, ca=1, cb=0):
    return lax.dot_general(a, b, (((ca,), (cb,)), ((), ())), preferred_element_type=f32)


def lanes(shape):
    return lax.broadcasted_iota(jnp.int32, shape, len(shape) - 1)


def rows_of(shape):
    return lax.broadcasted_iota(jnp.int32, shape, len(shape) - 2)


def ln_fwd(x, gain, bias):
    real = (lanes((1, CP)) < C).astype(f32)
    mean = jnp.sum(x, axis=-1, keepdims=True) * (1.0 / C)
    xc = (x - mean) * real
    var = jnp.sum(xc * xc, axis=-1, keepdims=True) * (1.0 / C)
    rstd = lax.rsqrt(var + 1e-05)
    xhat = xc * rstd
    return xhat, rstd, xhat * gain + bias


def ln_bwd(dy, xhat, rstd, gain):
    a = dy * gain
    m1 = jnp.sum(a, axis=-1, keepdims=True) * (1.0 / C)
    m2 = jnp.sum(a * xhat, axis=-1, keepdims=True) * (1.0 / C)
    return rstd * (a - m1 - xhat * m2)


def gelu_pair(h):
    z = jnp.abs(h) * 0.7071067811865476
    d = 1.0 + 0.3275911 * z
    t = pl.reciprocal(d, approx=True)
    t = t * (2.0 - d * t)
    e = jnp.exp2(h * h * (-0.5 * LOG2E))
    poly = t * (
        0.254829592 + t * (-0.284496736 + t * (1.421413741 + t * (-1.453152027 + t * 1.061405429)))
    )
    q = 0.5 * poly * e
    phi = jnp.where(h >= 0, 1.0 - q, q)
    return h * phi, phi + h * (e * 0.3989422804014327)


def fold8(v):
    return jnp.sum(v.reshape(v.shape[0] // 8, 8, v.shape[1]), axis=0)


def head_mask(h):
    ln = lanes((1, CP))
    return (ln >= h * HEAD_DIM) & (ln < (h + 1) * HEAD_DIM)


def spread_heads(v):
    return jnp.concatenate(
        [jnp.where(head_mask(h), v, jnp.zeros_like(v)) for h in range(HEADS)], axis=0
    )


def gather_heads(v):
    out = jnp.where(head_mask(0), v[:AREA], 0.0)
    for h in range(1, HEADS):
        out = jnp.where(head_mask(h), v[h * AREA : (h + 1) * AREA], out)
    return out


def main_kernel(
    scal,
    img,
    img_nxt,
    cot,
    cot_nxt,
    wqkv,
    wproj,
    wfc1,
    wfc2,
    wconv,
    vecs,
    extra,
    ll_out,
    gcat,
    ig_out,
    d_qkv,
    d_proj,
    d_fc1,
    d_fc2,
    d_norm,
    d_rel,
    xrow,
    xhat1,
    rstd,
    normed,
    qkv,
    probs,
    mixed,
    xhat2,
    normed2,
    act,
    dgelu,
    winf,
    fgrad,
    do_buf,
    tmp,
):
    nb = scal[0]
    last = scal[1]
    width = nb * WIN
    NW = 256 // WIN
    RM = 256

    def vec(i, n):
        return vecs[i : i + 1, 0:n]

    xrow[:, :, 128:256] = jnp.zeros((16, 256, 128), f32)

    @pl.loop(0, 12)
    def _(r):
        xrow[r, :, 0:C] = img[r + 4].astype(f32)

    @pl.loop(0, 4)
    def _(r):
        xrow[12 + r, :, 0:C] = img_nxt[r].astype(f32)

    tmp[...] = jnp.zeros_like(tmp)
    col_in = rows_of((256, C)) < width

    def put_g(pos, row, flag):
        g = jnp.where(col_in, row.astype(f32), 0.0) * flag
        tmp[8:264, 0:C] = g
        base = pl.multiple_of(pos * 256, 256)
        gcat[pl.ds(base, 256), 0:CP] = tmp[9:265, :].astype(bf16)
        gcat[pl.ds(base, 256), CP : 2 * CP] = tmp[8:264, :].astype(bf16)
        gcat[pl.ds(base, 256), 2 * CP : 3 * CP] = tmp[7:263, :].astype(bf16)

    joined = jnp.where(last == 1, 0.0, 1.0)

    @pl.loop(0, 13)
    def _(r):
        put_g(r, cot[r + 3], 1.0)

    put_g(13, cot_nxt[0], joined)
    put_g(14, cot[15], joined)

    @pl.loop(0, 5)
    def _(r):
        put_g(15 + r, cot_nxt[r], 1.0)

    d_qkv[...] = jnp.zeros_like(d_qkv)
    d_proj[...] = jnp.zeros_like(d_proj)
    d_fc1[...] = jnp.zeros_like(d_fc1)
    d_fc2[...] = jnp.zeros_like(d_fc2)
    d_norm[...] = jnp.zeros_like(d_norm)
    d_rel[...] = jnp.zeros_like(d_rel)

    pos_hi = rows_of((1, WIN, CP)) >= SHIFT

    def rolled(a, b):
        t = jnp.where(pos_hi, a, b)
        return pltpu.roll(t, SHIFT, 1)

    def to_win(ref, band, k):
        nxt = jnp.where(k == nb - 1, 0, jnp.minimum(k + 1, NW - 1))
        rs = pl.ds(pl.multiple_of(band * WIN, WIN), WIN)
        a = ref[rs, pl.ds(pl.multiple_of(k * WIN, WIN), WIN), :]
        b = ref[rs, pl.ds(pl.multiple_of(nxt * WIN, WIN), WIN), :]
        return rolled(a, b).reshape(AREA, CP)

    def from_win(ref, band, k):
        prv = jnp.where(k == 0, nb - 1, k - 1)
        a = ref[pl.ds(pl.multiple_of((band * NW + prv) * AREA, AREA), AREA), :]
        b = ref[pl.ds(pl.multiple_of((band * NW + k) * AREA, AREA), AREA), :]
        return rolled(a.reshape(WIN, WIN, CP), b.reshape(WIN, WIN, CP))

    def win_rows(w):
        return pl.ds(pl.multiple_of(w * AREA, AREA), AREA)

    @pl.loop(0, 8)
    def _(g):
        band = lax.div(g, 4)
        k0 = lax.rem(g, 4) * 8

        @pl.loop(0, 8)
        def _(i):
            x = to_win(xrow, band, k0 + i)
            rs = win_rows(g * 8 + i)
            xhat, rs_, out = ln_fwd(x, vec(0, CP), vec(1, CP))
            winf[rs, :] = x
            xhat1[rs, :] = xhat
            rstd[rs, 0:1] = rs_
            normed[rs, :] = out.astype(bf16)

        gs = pl.ds(pl.multiple_of(g * 512, 512), 512)
        for n in range(3):
            sl = slice(n * CP, (n + 1) * CP)
            qkv[gs, sl] = (dot(normed[gs, :], wqkv[:, sl]) + vecs[2:3, sl]).astype(bf16)

        @pl.loop(0, 8)
        def _(i):
            rs = win_rows(g * 8 + i)
            kk = k0 + i
            q = qkv[rs, 0:CP]
            k = qkv[rs, CP : 2 * CP]
            v = qkv[rs, 2 * CP : 3 * CP]
            which = jnp.where((band == 1) & (last == 1), 2, 0) + jnp.where(kk == nb - 1, 1, 0)
            s = dot(k, spread_heads(q), 1, 1) * (SCALE * LOG2E) + extra[which]
            top = jnp.max(s, axis=0, keepdims=True)
            e = jnp.exp2(s - top)
            total = jnp.sum(e, axis=0, keepdims=True)
            p = (e * (1.0 / total)).astype(bf16)
            probs[rs, :] = p
            o = gather_heads(dot(p, v, 0, 0))
            o = jnp.where(lanes((1, CP)) == C, 1.0, o)
            mixed[rs, :] = o.astype(bf16)

        @pl.loop(0, 512 // RM)
        def _(j):
            rs = pl.ds(pl.multiple_of(g * 512 + j * RM, RM), RM)
            fs = dot(mixed[rs, :], wproj[...]) + vec(3, CP) + winf[rs, :]
            xhat, rs_, out = ln_fwd(fs, vec(4, CP), vec(5, CP))
            xhat2[rs, :] = xhat
            rstd[rs, 1:2] = rs_
            n2 = out.astype(bf16)
            normed2[rs, :] = n2
            hid = dot(n2, wfc1[...]) + vec(6, HP)
            ac, dg = gelu_pair(hid)
            ac = jnp.where(lanes((1, HP)) == HID, 1.0, ac).astype(bf16)
            act[rs, :] = ac
            dgelu[rs, :] = dg.astype(bf16)
            winf[rs, :] = fs + dot(ac, wfc2[...]) + vec(7, CP)

    @pl.loop(0, 64)
    def _(w):
        band = lax.div(w, NW)
        k = lax.rem(w, NW)
        xrow[pl.ds(pl.multiple_of(band * 8, 8), 8), pl.ds(pl.multiple_of(k * 8, 8), 8), :] = from_win(
            winf, band, k
        )

    col_in_p = rows_of((256, CP)) < width

    @pl.loop(0, 16)
    def _(r):
        ll_out[pl.ds(pl.multiple_of(r * 256, 256), 256), :] = jnp.where(
            col_in_p, xrow[r], 0.0
        ).astype(bf16)

    @pl.loop(0, 16)
    def _(r):
        pos = r + 1 + jnp.where(r >= 12, 2, 0)
        acc = None
        for a in range(3):
            d = dot(
                gcat[pl.ds(pl.multiple_of((pos + 1 - a) * 256, 256), 256), :], wconv[a], 1, 1
            )
            acc = d if acc is None else acc + d
        xrow[r] = jnp.where(col_in_p, acc, 0.0)

    @pl.loop(0, 8)
    def _(g):
        band = lax.div(g, 4)
        k0 = lax.rem(g, 4) * 8
        gs = pl.ds(pl.multiple_of(g * 512, 512), 512)

        @pl.loop(0, 8)
        def _(i):
            fgrad[win_rows(i), :] = to_win(xrow, band, k0 + i)

        @pl.loop(0, 512 // RM)
        def _(j):
            ls = pl.ds(pl.multiple_of(j * RM, RM), RM)
            rs = pl.ds(pl.multiple_of(g * 512 + j * RM, RM), RM)
            lg = fgrad[ls, :]
            mg = lg.astype(bf16)
            d_fc2[...] += dot(act[rs, :], mg, 0, 0)
            ag = dot(mg, wfc2[...], 1, 1).astype(bf16).astype(f32)
            hg = (ag * dgelu[rs, :].astype(f32)).astype(bf16)
            d_fc1[...] += dot(normed2[rs, :], hg, 0, 0)
            dn2 = dot(hg, wfc1[...], 1, 1).astype(bf16).astype(f32)
            xhat = xhat2[rs, :]
            d_norm[0:8, :] += fold8(dn2 * xhat)
            d_norm[8:16, :] += fold8(dn2)
            fg = lg + ln_bwd(dn2, xhat, rstd[rs, 1:2], vec(4, CP))
            fgrad[ls, :] = fg
            at = fg.astype(bf16)
            d_proj[...] += dot(mixed[rs, :], at, 0, 0)
            do_buf[ls, :] = dot(at, wproj[...], 1, 1).astype(bf16)

        @pl.loop(0, 8)
        def _(i):
            rs = win_rows(g * 8 + i)
            q = qkv[rs, 0:CP]
            k = qkv[rs, CP : 2 * CP]
            v = qkv[rs, 2 * CP : 3 * CP]
            dobd = spread_heads(do_buf[win_rows(i), :])
            dp = dot(v, dobd, 1, 1)
            pb = probs[rs, :]
            p = pb.astype(f32)
            ds = p * (dp - jnp.sum(p * dp, axis=0, keepdims=True))
            dsb = ds.astype(bf16)
            d_rel[...] += dsb.astype(f32)
            dv = dot(pb, dobd)
            dk = dot(dsb, spread_heads(q)) * SCALE
            dq = gather_heads(dot(dsb, k, 0, 0)) * SCALE
            qkv[rs, 0:CP] = dq.astype(bf16)
            qkv[rs, CP : 2 * CP] = dk.astype(bf16)
            qkv[rs, 2 * CP : 3 * CP] = dv.astype(bf16)

        d_qkv[...] += dot(normed[gs, :], qkv[gs, :], 0, 0)

        @pl.loop(0, 512 // RM)
        def _(j):
            ls = pl.ds(pl.multiple_of(j * RM, RM), RM)
            rs = pl.ds(pl.multiple_of(g * 512 + j * RM, RM), RM)
            dn1 = dot(qkv[rs, :], wqkv[...], 1, 1).astype(bf16).astype(f32)
            xhat = xhat1[rs, :]
            d_norm[16:24, :] += fold8(dn1 * xhat)
            d_norm[24:32, :] += fold8(dn1)
            winf[rs, :] = fgrad[ls, :] + ln_bwd(dn1, xhat, rstd[rs, 0:1], vec(0, CP))

    @pl.loop(0, 64)
    def _(w):
        band = lax.div(w, NW)
        k = lax.rem(w, NW)
        xrow[pl.ds(pl.multiple_of(band * 8, 8), 8), pl.ds(pl.multiple_of(k * 8, 8), 8), :] = from_win(
            winf, band, k
        )

    @pl.loop(0, 16)
    def _(r):
        pos = r + 1 + jnp.where(r >= 12, 2, 0)
        g = gcat[pl.ds(pl.multiple_of(pos * 256, 256), 256), CP : 2 * CP]
        v = jnp.where(col_in_p, xrow[r] + g.astype(f32), 0.0)
        ig_out[r] = v[:, 0:C].astype(bf16)


def conv_kernel(
    scal, ll, ll_top, ll_bot, gcat, img, img_nxt, wconv, vecs, res_out, d_conv, buf, tmp
):
    nb = scal[0]
    last = scal[1]
    width = nb * WIN
    joined = jnp.where(last == 1, 0.0, 1.0).astype(bf16)
    buf[0:256] = ll_top[...]
    buf[256 : 13 * 256] = ll[0 : 12 * 256]
    buf[13 * 256 : 14 * 256] = ll[12 * 256 : 13 * 256] * joined
    buf[14 * 256 : 15 * 256] = ll[11 * 256 : 12 * 256] * joined
    buf[15 * 256 : 19 * 256] = ll[12 * 256 : 16 * 256]
    buf[19 * 256 :] = ll_bot[...]
    d_conv[...] = jnp.zeros_like(d_conv)
    tmp[...] = jnp.zeros_like(tmp)
    col_in = rows_of((256, C)) < width

    @pl.loop(0, 4)
    def _(n):
        start = 1 + 4 * n + jnp.where(n == 3, 2, 0)
        gs = gcat[pl.ds(pl.multiple_of(start * 256, 256), 1024), :]
        for a in range(3):
            xs = buf[pl.ds(pl.multiple_of((start + a - 1) * 256, 256), 1024), :]
            d_conv[a] += dot(xs, gs, 0, 0)

    def out_row(r, source):
        pos = r + 1 + jnp.where(r >= 12, 2, 0)
        acc = None
        for a in range(3):
            d = dot(buf[pl.ds(pl.multiple_of((pos + a - 1) * 256, 256), 256), :], wconv[a])
            acc = d if acc is None else acc + d
        tmp[8:264, :] = acc[:, 0:CP]
        tmp[280:536, :] = acc[:, 2 * CP : 3 * CP]
        out = acc[:, CP : 2 * CP] + tmp[7:263, :] + tmp[281:537, :] + vecs[8:9, 0:CP]
        out = out[:, 0:C] + source.astype(f32)
        res_out[r] = jnp.where(col_in, out, 0.0).astype(bf16)

    @pl.loop(0, 12)
    def _(r):
        out_row(r, img[r + 4])

    @pl.loop(0, 4)
    def _(r):
        out_row(r + 12, img_nxt[r])


def relative_index():
    coords = np.arange(AREA)
    row, col = coords // WIN, coords % WIN
    return (row[:, None] - row[None, :] + WIN - 1) * (2 * WIN - 1) + col[:, None] - col[None, :] + WIN - 1


def score_extra(bias_table):
    hot = jnp.asarray(
        (relative_index().T.reshape(-1)[:, None] == np.arange(225)[None, :]).astype(np.float32)
    )
    rel = jnp.dot(hot, bias_table, precision=lax.Precision.HIGHEST)
    rel = rel.reshape(AREA, AREA, HEADS).transpose(0, 2, 1).reshape(AREA, HI)
    coords = np.arange(AREA)
    yh = coords // WIN >= SHIFT
    xh = coords % WIN >= SHIFT
    ydiff = yh[:, None] != yh[None, :]
    xdiff = xh[:, None] != xh[None, :]
    masks = np.stack([np.zeros_like(ydiff), xdiff, ydiff, ydiff | xdiff])
    masks = np.where(np.tile(masks, (1, 1, HEADS)), -100.0, 0.0).astype(np.float32)
    return (rel[None] + jnp.asarray(masks)) * LOG2E


def rel_to_table(d_rel):
    hot = jnp.asarray(
        (relative_index().T.reshape(-1)[:, None] == np.arange(225)[None, :]).astype(np.float32)
    )
    per = d_rel.reshape(AREA, HEADS, AREA).transpose(0, 2, 1).reshape(AREA * AREA, HEADS)
    return jnp.dot(hot.T, per, precision=lax.Precision.HIGHEST)


def ring(value, axis, steps):
    count = lax.axis_size(axis)
    pairs = [(source, (source + steps) % count) for source in range(count)]
    return lax.ppermute(value, axis, pairs)


VM = pl.BlockSpec(memory_space=pltpu.VMEM)
SM = pl.BlockSpec(memory_space=pltpu.SMEM)


def run_main(scal, img, img_nxt, cot, cot_nxt, wqkv, wproj, wfc1, wfc2, wconv, vecs, extra):
    S = jax.ShapeDtypeStruct
    return pl.pallas_call(
        main_kernel,
        out_shape=(
            S((4096, CP), bf16),
            S((20 * 256, 3 * CP), bf16),
            S((16, 256, C), bf16),
            S((CP, 3 * CP), f32),
            S((CP, CP), f32),
            S((CP, HP), f32),
            S((HP, CP), f32),
            S((32, CP), f32),
            S((AREA, HI), f32),
        ),
        in_specs=[SM] + [VM] * 11,
        out_specs=[VM] * 9,
        scratch_shapes=[
            pltpu.VMEM((16, 256, CP), f32),
            pltpu.VMEM((4096, CP), f32),
            pltpu.VMEM((4096, 2), f32),
            pltpu.VMEM((4096, CP), bf16),
            pltpu.VMEM((4096, 3 * CP), bf16),
            pltpu.VMEM((4096, HI), bf16),
            pltpu.VMEM((4096, CP), bf16),
            pltpu.VMEM((4096, CP), f32),
            pltpu.VMEM((4096, CP), bf16),
            pltpu.VMEM((4096, HP), bf16),
            pltpu.VMEM((4096, HP), bf16),
            pltpu.VMEM((4096, CP), f32),
            pltpu.VMEM((512, CP), f32),
            pltpu.VMEM((512, CP), bf16),
            pltpu.VMEM((272, CP), f32),
        ],
        compiler_params=pltpu.CompilerParams(vmem_limit_bytes=63 * 1024 * 1024),
        name="layer",
    )(scal, img, img_nxt, cot, cot_nxt, wqkv, wproj, wfc1, wfc2, wconv, vecs, extra)


def run_conv(scal, ll, ll_top, ll_bot, gcat, img, img_nxt, wconv, vecs):
    S = jax.ShapeDtypeStruct
    return pl.pallas_call(
        conv_kernel,
        out_shape=(S((16, 256, C), bf16), S((3, CP, 3 * CP), f32)),
        in_specs=[SM] + [VM] * 8,
        out_specs=[VM] * 2,
        scratch_shapes=[pltpu.VMEM((20 * 256, CP), bf16), pltpu.VMEM((544, CP), f32)],
        compiler_params=pltpu.CompilerParams(vmem_limit_bytes=60 * 1024 * 1024),
        name="conv",
    )(scal, ll, ll_top, ll_bot, gcat, img, img_nxt, wconv, vecs)


def prepare(norm1_gain, norm1_bias, qkv_weight, qv_bias, bias_table, proj_weight, proj_bias,
            norm2_gain, norm2_bias, fc1_weight, fc1_bias, fc2_weight, fc2_bias, conv_weight, conv_bias):
    pc = CP - C
    wqkv = jnp.pad(qkv_weight.reshape(C, 3, C), ((0, pc), (0, 0), (0, pc))).reshape(CP, 3 * CP)
    wproj = jnp.pad(proj_weight, ((0, pc), (0, pc)))
    wfc1 = jnp.pad(fc1_weight, ((0, pc), (0, HP - HID)))
    wfc2 = jnp.pad(fc2_weight, ((0, HP - HID), (0, pc)))
    wconv = jnp.pad(conv_weight.transpose(0, 2, 1, 3), ((0, 0), (0, pc), (0, 0), (0, pc)))
    wconv = wconv.reshape(3, CP, 3 * CP)

    def row(v, one=False):
        v = jnp.concatenate([v, jnp.ones((1,), f32)]) if one else v
        return jnp.pad(v, (0, 3 * CP - v.shape[0]))

    zero = jnp.zeros((C,), f32)
    qkvb = jnp.pad(jnp.stack([qv_bias[:C], zero, qv_bias[C:]]), ((0, 0), (0, pc))).reshape(-1)
    vecs = jnp.stack(
        [row(norm1_gain), row(norm1_bias, True), qkvb, row(proj_bias), row(norm2_gain),
         row(norm2_bias, True), row(fc1_bias), row(fc2_bias, True), row(conv_bias)]
        + [jnp.zeros((3 * CP,), f32)] * 7
    )
    return wqkv, wproj, wfc1, wfc2, wconv, vecs, score_extra(bias_table)


def on_device(
    images, widths, norm1_gain, norm1_bias, qkv_weight, qv_bias, bias_table, proj_weight, proj_bias,
    norm2_gain, norm2_bias, fc1_weight, fc1_bias, fc2_weight, fc2_bias, conv_weight, conv_bias, cotangent,
):
    count, rows_here, width, chans = images.shape
    stripes = lax.axis_size("rows")
    img = images.reshape(rows_here, width, chans)
    cot = cotangent.reshape(rows_here, width, chans)
    is_last = (lax.axis_index("rows") == stripes - 1).astype(jnp.int32)
    scal = jnp.stack([lax.div(widths[0], WIN), is_last])
    img_nxt = ring(img[:SHIFT], "rows", -1)
    cot_nxt = ring(cot[: SHIFT + 1], "rows", -1)
    wqkv, wproj, wfc1, wfc2, wconv, vecs, extra = prepare(
        norm1_gain, norm1_bias, qkv_weight, qv_bias, bias_table, proj_weight, proj_bias,
        norm2_gain, norm2_bias, fc1_weight, fc1_bias, fc2_weight, fc2_bias, conv_weight, conv_bias,
    )
    ll, gcat, ig, d_qkv, d_proj, d_fc1, d_fc2, d_norm, d_rel = run_main(
        scal, img, img_nxt, cot, cot_nxt, wqkv, wproj, wfc1, wfc2, wconv, vecs, extra
    )
    ll_bot = ring(ll[:256], "rows", -1)
    ll_top = ring(ll[15 * 256 :], "rows", 1)
    res, d_conv = run_conv(scal, ll, ll_top, ll_bot, gcat, img, img_nxt, wconv, vecs)

    def moved(rows):
        head = ring(rows[rows_here - SHIFT :], "rows", 1)
        return jnp.concatenate([head, rows[: rows_here - SHIFT]], axis=0)[None]

    norms = jnp.sum(d_norm.reshape(4, 8, CP), axis=1)[:, :C]
    dq = d_qkv[: C + 1].reshape(C + 1, 3, CP)[:, :, :C]
    local = (
        norms[2],
        norms[3],
        dq[:C].reshape(C, 3 * C),
        jnp.concatenate([dq[C, 0], dq[C, 2]]),
        rel_to_table(d_rel),
        d_proj[:C, :C],
        d_proj[C, :C],
        norms[0],
        norms[1],
        d_fc1[:C, :HID],
        d_fc1[C, :HID],
        d_fc2[:HID, :C],
        d_fc2[HID, :C],
        d_conv.reshape(3, CP, 3, CP)[:, :C, :, :C].transpose(0, 2, 1, 3),
        d_conv[1, C, CP : CP + C],
    )
    summed = lax.psum(local, ("rows", "imgs"))
    return (moved(res), moved(ig)) + tuple(summed)


def solution(mesh):
    big = P("imgs", "rows", None, None)
    in_specs = (big, P("imgs")) + (P(),) * 15 + (big,)
    out_specs = (big, big) + (P(),) * 15
    return jax.shard_map(
        on_device, mesh=mesh, in_specs=in_specs, out_specs=out_specs, check_vma=False
    )
```

```python
import functools

import jax
import jax.numpy as jnp
import numpy as np
from jax import lax
from jax.experimental import pallas as pl
from jax.experimental.pallas import tpu as pltpu
from jax.sharding import PartitionSpec as P

HEADS = 6
HEAD_DIM = 30
WIN = 8
SHIFT = 4
C = 180
CP = 256
HID = 360
HP = 384
AREA = WIN * WIN
HI = HEADS * AREA
LOG2E = 1.4426950408889634
SCALE = HEAD_DIM ** (-0.5)

CR = 192
FC2_ROWS = 368
A1_FC1 = 9 * CR
A1_FC2 = A1_FC1 + 2 * CR
A1_PROJ = A1_FC2 + FC2_ROWS
A1_USED = A1_PROJ + CR
A2_SMALL = 3 * CR
A2_USED = A2_SMALL + 16

f32 = jnp.float32
bf16 = jnp.bfloat16


def dot(a, b, ca=1, cb=0):
    return lax.dot_general(a, b, (((ca,), (cb,)), ((), ())), preferred_element_type=f32)


def lanes(shape):
    return lax.broadcasted_iota(jnp.int32, shape, len(shape) - 1)


def rows_of(shape):
    return lax.broadcasted_iota(jnp.int32, shape, len(shape) - 2)


def ln_fwd(x, gain, bias):
    real = (lanes((1, CP)) < C).astype(f32)
    mean = jnp.sum(x, axis=-1, keepdims=True) * (1.0 / C)
    xc = (x - mean) * real
    var = jnp.sum(xc * xc, axis=-1, keepdims=True) * (1.0 / C)
    rstd = lax.rsqrt(var + 1e-05)
    xhat = xc * rstd
    return xhat, rstd, xhat * gain + bias


def with_rstd(xhat, rstd):
    high = rstd.astype(bf16).astype(f32)
    lane = lanes((1, CP))
    return jnp.where(lane == 200, high, jnp.where(lane == 201, rstd - high, xhat))


def ln_bwd(dy, xhat, rstd, gain):
    a = dy * gain
    m1 = jnp.sum(a, axis=-1, keepdims=True) * (1.0 / C)
    m2 = jnp.sum(a * xhat, axis=-1, keepdims=True) * (1.0 / C)
    return rstd * (a - m1 - xhat * m2)


def gelu_pair(h):
    z = jnp.abs(h) * 0.7071067811865476
    d = 1.0 + 0.3275911 * z
    t = pl.reciprocal(d, approx=True)
    t = t * (2.0 - d * t)
    e = jnp.exp2(h * h * (-0.5 * LOG2E))
    poly = t * (
        0.254829592 + t * (-0.284496736 + t * (1.421413741 + t * (-1.453152027 + t * 1.061405429)))
    )
    q = 0.5 * poly * e
    phi = jnp.where(h >= 0, 1.0 - q, q)
    return h * phi, phi + h * (e * 0.3989422804014327)


def fold8(v):
    return jnp.sum(v.reshape(v.shape[0] // 8, 8, v.shape[1]), axis=0)


def head_mask(h):
    ln = lanes((1, CP))
    return (ln >= h * HEAD_DIM) & (ln < (h + 1) * HEAD_DIM)


def spread_heads(v):
    return jnp.concatenate(
        [jnp.where(head_mask(h), v, jnp.zeros_like(v)) for h in range(HEADS)], axis=0
    )


def gather_heads(v):
    out = jnp.where(head_mask(0), v[:AREA], 0.0)
    for h in range(1, HEADS):
        out = jnp.where(head_mask(h), v[h * AREA : (h + 1) * AREA], out)
    return out


def column_masks(width):
    return rows_of((256, CP)) < width


class AllReduce:
    def __init__(self, buf, out, r1, r2, r3, ssem, rsem, pr, chips, imgs, zsplit):
        self.buf, self.out, self.r1, self.r2, self.r3 = buf, out, r1, r2, r3
        self.ssem, self.rsem, self.chips, self.imgs = ssem, rsem, chips, imgs
        self.zsplit = zsplit
        rows = lax.axis_index("rows")
        self.core = lax.rem(rows, 2)
        self.chip = lax.div(rows, 2)
        self.z = lax.axis_index("imgs")
        self.piece = pr
        self.group = pr * imgs if zsplit else pr
        self.half = self.group * chips
        self.used = 0

    def copy(self, src, dst, device, n):
        return pltpu.make_async_remote_copy(
            src_ref=src,
            dst_ref=dst,
            send_sem=self.ssem.at[n],
            recv_sem=self.rsem.at[n],
            device_id=device,
            device_id_type=pl.DeviceIdType.MESH,
        )

    def rows(self, ref, start, size):
        return ref.at[pl.ds(pl.multiple_of(start, 16), size)]

    def base_half(self, core):
        return core * self.half

    def base_group(self, chip):
        return self.core * self.half + chip * self.group

    def base_piece(self, z):
        return self.base_group(self.chip) + (z * self.piece if self.zsplit else 0)

    def core_copy(self, ref, dst, n, gather):
        side = self.core if gather else 1 - self.core
        src = self.rows(ref, self.base_half(side), self.half)
        dst = src if dst is None else dst
        return [self.copy(src, dst, {"rows": self.chip * 2 + 1 - self.core}, n)]

    def chip_copies(self, ref, dst, n, gather):
        out = []
        for d in range(1, self.chips):
            to = lax.rem(self.chip + d, self.chips)
            src = self.rows(ref, self.base_group(self.chip if gather else to), self.group)
            to_ref = src if gather else dst.at[pl.ds((d - 1) * self.group, self.group)]
            out.append(self.copy(src, to_ref, {"rows": to * 2 + self.core}, n + d - 1))
        return out

    def img_copies(self, ref, dst, n, gather):
        out = []
        for d in range(1, self.imgs):
            to = lax.rem(self.z + d, self.imgs)
            src = self.rows(ref, self.base_piece(self.z if gather else to), self.piece)
            to_ref = src if gather else dst.at[pl.ds((d - 1) * self.piece, self.piece)]
            out.append(self.copy(src, to_ref, {"imgs": to}, n + d - 1))
        return out

    def start(self, copies):
        for c in copies:
            c.start()
        return copies

    def wait(self, copies):
        for c in copies:
            c.wait()

    def add(self, base, size, extra, count, stride, target):
        step = min(size, 64)
        while size % step:
            step -= 16

        @pl.loop(0, size // step)
        def _(i):
            at = pl.ds(pl.multiple_of(base + i * step, 16), step)
            total = self.buf[at, :].astype(f32)
            for d in range(count):
                total += extra[pl.ds(pl.multiple_of(d * stride + i * step, 16), step), :].astype(f32)
            target[at, :] = total.astype(bf16)

    def step(self, k):
        n2 = 1
        n3 = n2 + self.chips - 1
        n4 = n3 + self.imgs - 1
        n5 = n4 + self.imgs - 1
        n6 = n5 + self.chips - 1
        first = lambda: self.core_copy(self.buf, self.r1, 0, False)
        second = lambda: self.chip_copies(self.buf, self.r2, n2, False)
        third = lambda: self.img_copies(self.buf, self.r3, n3, False)
        fourth = lambda: self.img_copies(self.out, None, n4, True) if self.zsplit else []
        fifth = lambda: self.chip_copies(self.out, None, n5, True)
        sixth = lambda: self.core_copy(self.out, None, n6, True)
        if k == 0:
            self.start(first())
        elif k == 1:
            self.wait(first())
            self.add(self.base_half(self.core), self.half, self.r1, 1, 0, self.buf)
            self.start(second())
        elif k == 2:
            self.wait(second())
            self.add(
                self.base_group(self.chip), self.group, self.r2, self.chips - 1, self.group, self.buf
            )
            self.start(third())
        elif k == 3:
            self.wait(third())
            self.add(
                self.base_piece(self.z), self.piece, self.r3, self.imgs - 1, self.piece, self.out
            )
            self.start(fourth() if self.zsplit else fifth())
        elif k == 4:
            if self.zsplit:
                self.wait(fourth())
                self.start(fifth())
        elif k == 5:
            self.wait(fifth())
            self.start(sixth())
        elif k == 6:
            self.wait(sixth())


def all_reduce_sems(chips, imgs):
    return 2 * (1 + chips - 1 + imgs - 1)


def layer_kernel(
    chips,
    imgs,
    piece1,
    piece2,
    scal,
    img,
    cot,
    wqkv,
    wproj,
    wfc1,
    wfc2,
    wconv,
    vecs,
    extra,
    res_out,
    ig_out,
    o_qkv,
    o_proj,
    o_fc1,
    o_fc2,
    o_conv,
    o_vec,
    d_qkv,
    d_proj,
    d_fc1,
    d_fc2,
    d_conv,
    d_norm,
    d_rel,
    io1,
    io2,
    xband,
    gband,
    gcat,
    llbuf,
    xhat1,
    normed,
    qkv,
    probs,
    mixed,
    xhat2,
    normed2,
    act,
    dgelu,
    winf,
    fgrad,
    do_buf,
    edge,
    tmp,
    a1_buf,
    a1_out,
    a1_r1,
    a1_r2,
    a1_r3,
    a2_buf,
    a2_out,
    a2_r1,
    a2_r2,
    a2_r3,
    lsem,
    hs,
    hr,
    a1_s,
    a1_r,
    a2_s,
    a2_r,
):
    stripes = 2 * chips
    rank = lax.axis_index("rows")
    core = lax.rem(rank, 2)
    up = lax.rem(rank + stripes - 1, stripes)
    down = lax.rem(rank + 1, stripes)
    ar1 = AllReduce(a1_buf, a1_out, a1_r1, a1_r2, a1_r3, a1_s, a1_r, piece1, chips, imgs, True)
    ar2 = AllReduce(a2_buf, a2_out, a2_r1, a2_r2, a2_r3, a2_s, a2_r, piece2, chips, imgs, False)

    barrier = pltpu.get_barrier_semaphore()
    peers = [{"rows": up}, {"rows": down}]
    peers += [{"rows": lax.rem(rank + 2 * d, stripes)} for d in range(1, chips)]
    peers += [{"imgs": lax.rem(ar1.z + d, imgs)} for d in range(1, imgs)]
    for peer in peers:
        pl.semaphore_signal(barrier, inc=1, device_id=peer, device_id_type=pl.DeviceIdType.MESH)
    pl.semaphore_wait(barrier, len(peers))

    def remote(src, dst, to, n):
        return pltpu.make_async_remote_copy(
            src_ref=src,
            dst_ref=dst,
            send_sem=hs.at[n],
            recv_sem=hr.at[n],
            device_id={"rows": to},
            device_id_type=pl.DeviceIdType.MESH,
        )

    send_img = remote(img.at[pl.ds(0, 4)], io2.at[pl.ds(16, 4)], up, 0)
    send_cot = remote(cot.at[pl.ds(0, 5)], io1.at[pl.ds(16, 5)], up, 1)
    send_cot.start()
    send_img.start()
    load_cot = pltpu.make_async_copy(cot, io1.at[pl.ds(0, 16)], lsem.at[0])
    load_img = pltpu.make_async_copy(img, io2.at[pl.ds(0, 16)], lsem.at[1])
    load_cot.start()
    load_img.start()

    nb = scal[0]
    width = nb * WIN
    is_last = rank == stripes - 1
    joined = jnp.where(is_last, 0.0, 1.0)
    NW = 256 // WIN
    RM = 256

    def vec(i, n):
        return vecs[i : i + 1, 0:n]

    def row_at(pos, count=1):
        return pl.ds(pl.multiple_of(pos * 256, 256), count * 256)

    xband[:, :, 128:256] = jnp.zeros((8, 256, 128), f32)
    tmp[...] = jnp.zeros_like(tmp)
    for ref in (d_qkv, d_proj, d_fc1, d_fc2, d_conv, d_norm, d_rel):
        ref[...] = jnp.zeros_like(ref)
    a1_buf[A1_USED:, :] = jnp.zeros((a1_buf.shape[0] - A1_USED, CP), bf16)
    a2_buf[A2_USED:, :] = jnp.zeros((a2_buf.shape[0] - A2_USED, CP), bf16)

    col_in = rows_of((256, C)) < width
    col_in_p = rows_of((256, CP)) < width

    def put_g(pos, row, flag):
        g = jnp.where(col_in, row.astype(f32), 0.0) * flag
        tmp[8:264, 0:C] = g
        at = row_at(pos)
        gcat[at, 0:CP] = tmp[9:265, :].astype(bf16)
        gcat[at, CP : 2 * CP] = tmp[8:264, :].astype(bf16)
        gcat[at, 2 * CP : 3 * CP] = tmp[7:263, :].astype(bf16)

    load_cot.wait()

    @pl.loop(0, 13)
    def _(r):
        put_g(r, io1[r + 3], 1.0)

    put_g(14, io1[15], joined)
    load_img.wait()

    pos_hi = rows_of((1, WIN, CP)) >= SHIFT

    def rolled(a, b):
        t = jnp.where(pos_hi, a, b)
        return pltpu.roll(t, SHIFT, 1)

    def to_win(ref, k):
        nxt = jnp.minimum(k + 1, NW - 1)
        a = ref[:, pl.ds(pl.multiple_of(k * WIN, WIN), WIN), :]
        b = ref[:, pl.ds(pl.multiple_of(nxt * WIN, WIN), WIN), :]
        b = jnp.where(k == nb - 1, ref[:, 0:WIN, :], b)
        return rolled(a, b).reshape(AREA, CP)

    def from_win(ref, band):
        def block(k):
            at = pl.multiple_of((band * NW + k) * AREA, AREA)
            return ref[pl.ds(at, AREA), :].reshape(WIN, WIN, CP)

        @pl.loop(0, NW, unroll=4)
        def _(k):
            b = block(k)
            edge[...] = jnp.where(k == nb - 1, b, edge[...])
            xband[:, pl.ds(pl.multiple_of(k * WIN, WIN), WIN), :] = rolled(
                block(jnp.maximum(k - 1, 0)), b
            )

        xband[:, 0:WIN, :] = rolled(edge[...], block(0))

    def win_rows(w):
        return pl.ds(pl.multiple_of(w * AREA, AREA), AREA)

    @pl.loop(0, 2)
    def _(band):
        @pl.when(band == 1)
        def _():
            send_cot.wait()
            send_img.wait()
            put_g(13, io1[16], joined)

            @pl.loop(0, 5)
            def _(r):
                put_g(15 + r, io1[16 + r], 1.0)

        @pl.loop(0, 8)
        def _(y):
            xband[y, :, 0:C] = io2[band * 8 + y + 4].astype(f32)

        @pl.loop(0, 8)
        def _(y):
            r = band * 8 + y
            pos = r + 1 + jnp.where(r >= 12, 2, 0)
            acc = None
            for a in range(3):
                d = dot(gcat[row_at(pos + 1 - a), :], wconv[a], 1, 1)
                acc = d if acc is None else acc + d
            gband[y] = jnp.where(col_in_p, acc, 0.0)

        @pl.loop(0, 4)
        def _(gg):
            g = band * 4 + gg
            k0 = gg * 8
            gs = pl.ds(pl.multiple_of(g * 512, 512), 512)

            @pl.loop(0, 8, unroll=4)
            def _(i):
                x = to_win(xband, k0 + i)
                rs = win_rows(g * 8 + i)
                xhat, rs_, out = ln_fwd(x, vec(0, CP), vec(1, CP))
                winf[rs, :] = x
                xhat1[rs, :] = with_rstd(xhat, rs_).astype(bf16)
                normed[rs, :] = out.astype(bf16)
                fgrad[rs, :] = to_win(gband, k0 + i)

            for n in range(3):
                sl = slice(n * CP, (n + 1) * CP)
                qkv[gs, sl] = (dot(normed[gs, :], wqkv[:, sl]) + vecs[2:3, sl]).astype(bf16)

            @pl.loop(0, 8, unroll=4)
            def _(i):
                rs = win_rows(g * 8 + i)
                kk = k0 + i
                q = qkv[rs, 0:CP]
                k = qkv[rs, CP : 2 * CP]
                v = qkv[rs, 2 * CP : 3 * CP]
                which = jnp.where((band == 1) & is_last, 2, 0)
                more = jnp.where(kk == nb - 1, extra[which + 1], extra[which])
                s = dot(k, spread_heads(q), 1, 1) * (SCALE * LOG2E) + more
                top = jnp.max(s, axis=0, keepdims=True)
                e = jnp.exp2(s - top)
                total = jnp.sum(e, axis=0, keepdims=True)
                p = (e * (1.0 / total)).astype(bf16)
                probs[rs, :] = p
                o = gather_heads(dot(p, v, 0, 0))
                o = jnp.where(lanes((1, CP)) == C, 1.0, o)
                mixed[win_rows(i), :] = o.astype(bf16)

            @pl.loop(0, 512 // RM)
            def _(j):
                ls = pl.ds(pl.multiple_of(j * RM, RM), RM)
                rs = pl.ds(pl.multiple_of(g * 512 + j * RM, RM), RM)
                fs = dot(mixed[ls, :], wproj[...]) + vec(3, CP) + winf[rs, :]
                xhat, rs_, out = ln_fwd(fs, vec(4, CP), vec(5, CP))
                xhat2[ls, :] = xhat
                n2 = out.astype(bf16)
                normed2[ls, :] = n2
                hid = dot(n2, wfc1[...]) + vec(6, HP)
                ac, dg = gelu_pair(hid)
                ac = jnp.where(lanes((1, HP)) == HID, 1.0, ac).astype(bf16)
                act[ls, :] = ac
                dgelu[ls, :] = dg.astype(bf16)
                winf[rs, :] = fs + dot(ac, wfc2[...]) + vec(7, CP)
                lg = fgrad[rs, :]
                mg = lg.astype(bf16)
                d_fc2[...] += dot(act[ls, 0:FC2_ROWS], mg, 0, 0)
                ag = dot(mg, wfc2[...], 1, 1).astype(bf16).astype(f32)
                hg = (ag * dgelu[ls, :].astype(f32)).astype(bf16)
                d_fc1[...] += dot(normed2[ls, 0:CR], hg, 0, 0)
                dn2 = dot(hg, wfc1[...], 1, 1).astype(bf16).astype(f32)
                xh = xhat2[ls, :]
                d_norm[0:8, :] += fold8(dn2 * xh)
                d_norm[8:16, :] += fold8(dn2)
                fg = lg + ln_bwd(dn2, xh, rs_, vec(4, CP))
                fgrad[rs, :] = fg
                at = fg.astype(bf16)
                d_proj[...] += dot(mixed[ls, 0:CR], at, 0, 0)
                do_buf[rs, :] = dot(at, wproj[...], 1, 1).astype(bf16)

    @pl.loop(0, 2)
    def _(band):
        from_win(winf, band)

        @pl.loop(0, 8)
        def _(y):
            r = band * 8 + y
            pos = r + 1 + jnp.where(r >= 12, 2, 0)
            llbuf[row_at(pos), :] = jnp.where(col_in_p, xband[y], 0.0).astype(bf16)

    send_up = remote(llbuf.at[pl.ds(256, 256)], llbuf.at[pl.ds(19 * 256, 256)], up, 2)
    send_down = remote(llbuf.at[pl.ds(18 * 256, 256)], llbuf.at[pl.ds(0, 256)], down, 3)
    send_up.start()
    send_down.start()
    joined_low = joined.astype(bf16)
    llbuf[13 * 256 : 14 * 256, :] = llbuf[15 * 256 : 16 * 256, :] * joined_low
    llbuf[14 * 256 : 15 * 256, :] = llbuf[12 * 256 : 13 * 256, :] * joined_low

    def wgrad_rows(n):
        start = 1 + 4 * n + jnp.where(n == 3, 2, 0)
        gs = gcat[row_at(start, 4), :]
        for a in range(3):
            d_conv[a] += dot(llbuf[row_at(start + a - 1, 4), 0:CR], gs, 0, 0)

    @pl.loop(1, 3)
    def _(n):
        wgrad_rows(n)

    send_up.wait()
    send_down.wait()

    @pl.loop(0, 2)
    def _(n):
        wgrad_rows(n * 3)

    for a in range(3):
        for b in range(3):
            at = (a * 3 + b) * CR
            a1_buf[at : at + CR, :] = d_conv[a, :, b * CP : (b + 1) * CP].astype(bf16)
    a1_buf[A1_FC1 : A1_FC1 + CR, :] = d_fc1[:, 0:CP].astype(bf16)
    a1_buf[A1_FC1 + CR : A1_FC1 + 2 * CR, 0:128] = d_fc1[:, CP:HP].astype(bf16)
    a1_buf[A1_FC1 + CR : A1_FC1 + 2 * CR, 128:256] = jnp.zeros((CR, 128), bf16)
    a1_buf[A1_FC2 : A1_FC2 + FC2_ROWS, :] = d_fc2[...].astype(bf16)
    a1_buf[A1_PROJ : A1_PROJ + CR, :] = d_proj[...].astype(bf16)
    ar1.step(0)

    def conv_rows(lo, hi):
        @pl.loop(lo, hi)
        def _(r):
            pos = r + 1 + jnp.where(r >= 12, 2, 0)
            acc = None
            for a in range(3):
                d = dot(llbuf[row_at(pos + a - 1), :], wconv[a])
                acc = d if acc is None else acc + d
            tmp[8:264, :] = acc[:, 0:CP]
            tmp[280:536, :] = acc[:, 2 * CP : 3 * CP]
            out = acc[:, CP : 2 * CP] + tmp[7:263, :] + tmp[281:537, :] + vec(8, CP)
            out = out[:, 0:C] + io2[r + 4].astype(f32)
            io1[r] = jnp.where(col_in, out, 0.0).astype(bf16)

    tmp[...] = jnp.zeros_like(tmp)
    conv_rows(12, 16)
    send_res = remote(io1.at[pl.ds(12, 4)], res_out.at[pl.ds(0, 4)], down, 4)
    send_res.start()
    conv_rows(0, 6)
    ar1.step(1)
    conv_rows(6, 12)
    ar1.step(2)
    store_res = pltpu.make_async_copy(io1.at[pl.ds(0, 12)], res_out.at[pl.ds(4, 12)], lsem.at[2])
    store_res.start()

    @pl.loop(0, 8)
    def _(g):
        gs = pl.ds(pl.multiple_of(g * 512, 512), 512)

        @pl.loop(0, 8, unroll=4)
        def _(i):
            rs = win_rows(g * 8 + i)
            q = qkv[rs, 0:CP]
            k = qkv[rs, CP : 2 * CP]
            v = qkv[rs, 2 * CP : 3 * CP]
            dobd = spread_heads(do_buf[rs, :])
            dp = dot(v, dobd, 1, 1)
            pb = probs[rs, :]
            p = pb.astype(f32)
            ds = p * (dp - jnp.sum(p * dp, axis=0, keepdims=True))
            dsb = ds.astype(bf16)
            d_rel[...] += dsb.astype(f32)
            dv = dot(pb, dobd)
            dk = dot(dsb, spread_heads(q)) * SCALE
            dq = gather_heads(dot(dsb, k, 0, 0)) * SCALE
            qkv[rs, 0:CP] = dq.astype(bf16)
            qkv[rs, CP : 2 * CP] = dk.astype(bf16)
            qkv[rs, 2 * CP : 3 * CP] = dv.astype(bf16)

        d_qkv[...] += dot(normed[gs, 0:CR], qkv[gs, :], 0, 0)

        @pl.loop(0, 512 // RM)
        def _(j):
            rs = pl.ds(pl.multiple_of(g * 512 + j * RM, RM), RM)
            dn1 = dot(qkv[rs, :], wqkv[...], 1, 1).astype(bf16).astype(f32)
            xhat = xhat1[rs, :].astype(f32)
            d_norm[16:24, :] += fold8(dn1 * xhat)
            d_norm[24:32, :] += fold8(dn1)
            fgrad[rs, :] = fgrad[rs, :] + ln_bwd(dn1, xhat, xhat[:, 200:201] + xhat[:, 201:202], vec(0, CP))

        @pl.when(g == 0)
        def _():
            ar1.step(3)

        @pl.when(g == 1)
        def _():
            ar1.step(4)

        @pl.when(g == 3)
        def _():
            ar1.step(5)

        @pl.when(g == 5)
        def _():
            ar1.step(6)

    for n in range(3):
        a2_buf[n * CR : (n + 1) * CR, :] = d_qkv[:, n * CP : (n + 1) * CP].astype(bf16)
    norms = jnp.sum(d_norm[...].reshape(4, 8, CP), axis=1)
    small = jnp.concatenate([norms, table_sum(d_rel[...]), jnp.zeros((4, CP), f32)], axis=0)
    a2_buf[A2_SMALL : A2_SMALL + 16, :] = small.astype(bf16)
    ar2.step(0)

    def grad_rows(band):
        from_win(fgrad, band)

        @pl.loop(0, 8)
        def _(y):
            r = band * 8 + y
            pos = r + 1 + jnp.where(r >= 12, 2, 0)
            v = xband[y] + gcat[row_at(pos), CP : 2 * CP].astype(f32)
            io2[r] = jnp.where(col_in_p, v, 0.0)[:, 0:C].astype(bf16)

    grad_rows(1)
    send_ig = remote(io2.at[pl.ds(12, 4)], ig_out.at[pl.ds(0, 4)], down, 5)
    send_ig.start()
    ar2.step(1)
    grad_rows(0)
    store_ig = pltpu.make_async_copy(io2.at[pl.ds(0, 12)], ig_out.at[pl.ds(4, 12)], lsem.at[3])
    store_ig.start()
    ar2.step(2)

    for a in range(3):
        for b in range(3):
            at = (a * 3 + b) * CR
            o_conv[a, b] = a1_out[at : at + CR, :].astype(f32)[0:C, 0:C]
    o_fc1[:, 0:CP] = a1_out[A1_FC1 : A1_FC1 + CR, :].astype(f32)[0:C, :]
    o_fc1[:, CP:HID] = a1_out[A1_FC1 + CR : A1_FC1 + 2 * CR, :].astype(f32)[0:C, 0 : HID - CP]
    o_fc2[...] = a1_out[A1_FC2 : A1_FC2 + FC2_ROWS, :].astype(f32)[0:HID, 0:C]
    o_proj[...] = a1_out[A1_PROJ : A1_PROJ + CR, :].astype(f32)[0:C, 0:C]
    o_vec[0:8, :] = a1_out[A1_FC1 + 176 : A1_FC1 + 192, :].astype(f32)[0:8]
    o_vec[8:16, :] = a1_out[A1_FC1 + CR + 176 : A1_FC1 + CR + 192, :].astype(f32)[0:8]
    o_vec[16:24, :] = a1_out[A1_FC2 + 352 : A1_FC2 + 368, :].astype(f32)[8:16]
    o_vec[24:32, :] = a1_out[A1_PROJ + 176 : A1_PROJ + 192, :].astype(f32)[0:8]
    o_vec[32:40, :] = a1_out[4 * CR + 176 : 4 * CR + 192, :].astype(f32)[0:8]
    ar2.step(3)
    ar2.step(5)
    ar2.step(6)
    for n in range(3):
        o_qkv[:, n * C : (n + 1) * C] = a2_out[n * CR : (n + 1) * CR, :].astype(f32)[0:C, 0:C]
    o_vec[40:48, :] = a2_out[176:192, :].astype(f32)[0:8]
    o_vec[48:56, :] = a2_out[2 * CR + 176 : 2 * CR + 192, :].astype(f32)[0:8]
    o_vec[56:72, :] = a2_out[A2_SMALL : A2_SMALL + 16, :].astype(f32)
    send_res.wait()
    send_ig.wait()
    store_res.wait()
    store_ig.wait()


def table_sum(d_rel):
    row = lax.broadcasted_iota(jnp.int32, (AREA, CP), 0)
    lane = lax.broadcasted_iota(jnp.int32, (AREA, CP), 1)
    put = (lane == row + lax.div(row, WIN) * (WIN - 1)).astype(bf16)
    heads = []
    for h in range(HEADS):
        v = d_rel[:, h * AREA : (h + 1) * AREA]
        v1 = v.astype(bf16)
        v2 = (v - v1.astype(f32)).astype(bf16)
        wide = dot(v1, put) + dot(v2, put)
        total = None
        for y in range(WIN):
            part = pltpu.roll(wide[y * WIN : (y + 1) * WIN, :], 112 - 15 * y, 1)
            total = part if total is None else total + part
        heads.append(total)
    out = None
    for x in range(WIN):
        rows = jnp.concatenate([t[x : x + 1] for t in heads] + [jnp.zeros((2, CP), f32)], axis=0)
        rows = pltpu.roll(rows, CP - x, 1) if x else rows
        out = rows if out is None else out + rows
    return out


def relative_index():
    coords = np.arange(AREA)
    row, col = coords // WIN, coords % WIN
    return (row[:, None] - row[None, :] + WIN - 1) * (2 * WIN - 1) + col[:, None] - col[None, :] + WIN - 1


def score_extra(bias_table):
    hot = jnp.asarray(
        (relative_index().T.reshape(-1)[:, None] == np.arange(225)[None, :]).astype(np.float32)
    )
    rel = jnp.dot(hot, bias_table, precision=lax.Precision.HIGHEST)
    rel = rel.reshape(AREA, AREA, HEADS).transpose(0, 2, 1).reshape(AREA, HI)
    coords = np.arange(AREA)
    yh = coords // WIN >= SHIFT
    xh = coords % WIN >= SHIFT
    ydiff = yh[:, None] != yh[None, :]
    xdiff = xh[:, None] != xh[None, :]
    masks = np.stack([np.zeros_like(ydiff), xdiff, ydiff, ydiff | xdiff])
    masks = np.where(np.tile(masks, (1, 1, HEADS)), -100.0, 0.0).astype(np.float32)
    return (rel[None] + jnp.asarray(masks)) * LOG2E


VM = pl.BlockSpec(memory_space=pltpu.VMEM)
SM = pl.BlockSpec(memory_space=pltpu.SMEM)
HB = pl.BlockSpec(memory_space=pl.ANY)


def up_to(n, m):
    return (n + m - 1) // m * m


def run_layer(stripes, imgs, scal, img, cot, wqkv, wproj, wfc1, wfc2, wconv, vecs, extra):
    S = jax.ShapeDtypeStruct
    V = pltpu.VMEM
    chips = stripes // 2
    piece1 = up_to(-(-A1_USED // (stripes * imgs)), 16)
    piece2 = up_to(-(-A2_USED // stripes), 16)
    half1 = piece1 * imgs * chips
    half2 = piece2 * chips
    sems = 2 * (chips + imgs - 1)
    dma = pltpu.SemaphoreType.DMA
    return pl.pallas_call(
        functools.partial(layer_kernel, chips, imgs, piece1, piece2),
        out_shape=(
            S((16, 256, C), bf16),
            S((16, 256, C), bf16),
            S((C, 3 * C), f32),
            S((C, C), f32),
            S((C, HID), f32),
            S((HID, C), f32),
            S((3, 3, C, C), f32),
            S((72, CP), f32),
        ),
        in_specs=[SM, HB, HB] + [VM] * 7,
        out_specs=[HB] * 2 + [VM] * 6,
        scratch_shapes=[
            V((CR, 3 * CP), f32),
            V((CR, CP), f32),
            V((CR, HP), f32),
            V((FC2_ROWS, CP), f32),
            V((3, CR, 3 * CP), f32),
            V((32, CP), f32),
            V((AREA, HI), f32),
            V((21, 256, C), bf16),
            V((20, 256, C), bf16),
            V((8, 256, CP), f32),
            V((8, 256, CP), f32),
            V((20 * 256, 3 * CP), bf16),
            V((20 * 256, CP), bf16),
            V((4096, CP), bf16),
            V((4096, CP), bf16),
            V((4096, 3 * CP), bf16),
            V((4096, HI), bf16),
            V((512, CP), bf16),
            V((512, CP), f32),
            V((512, CP), bf16),
            V((512, HP), bf16),
            V((512, HP), bf16),
            V((4096, CP), f32),
            V((4096, CP), f32),
            V((4096, CP), bf16),
            V((WIN, WIN, CP), f32),
            V((544, CP), f32),
            V((2 * half1, CP), bf16),
            V((2 * half1, CP), bf16),
            V((half1, CP), bf16),
            V(((chips - 1) * piece1 * imgs, CP), bf16),
            V(((imgs - 1) * piece1, CP), bf16),
            V((2 * half2, CP), bf16),
            V((2 * half2, CP), bf16),
            V((half2, CP), bf16),
            V(((chips - 1) * piece2, CP), bf16),
            V(((imgs - 1) * piece2, CP), bf16),
            dma((4,)),
            dma((6,)),
            dma((6,)),
            dma((sems,)),
            dma((sems,)),
            dma((sems,)),
            dma((sems,)),
        ],
        compiler_params=pltpu.CompilerParams(
            vmem_limit_bytes=63 * 1024 * 1024, collective_id=0, has_side_effects=True
        ),
        name="layer",
    )(scal, img, cot, wqkv, wproj, wfc1, wfc2, wconv, vecs, extra)


def prepare(norm1_gain, norm1_bias, qkv_weight, qv_bias, bias_table, proj_weight, proj_bias,
            norm2_gain, norm2_bias, fc1_weight, fc1_bias, fc2_weight, fc2_bias, conv_weight, conv_bias):
    pc = CP - C
    wqkv = jnp.pad(qkv_weight.reshape(C, 3, C), ((0, pc), (0, 0), (0, pc))).reshape(CP, 3 * CP)
    wproj = jnp.pad(proj_weight, ((0, pc), (0, pc)))
    wfc1 = jnp.pad(fc1_weight, ((0, pc), (0, HP - HID)))
    wfc2 = jnp.pad(fc2_weight, ((0, HP - HID), (0, pc)))
    wconv = jnp.pad(conv_weight.transpose(0, 2, 1, 3), ((0, 0), (0, pc), (0, 0), (0, pc)))
    wconv = wconv.reshape(3, CP, 3 * CP)

    def row(v, one=False):
        v = jnp.concatenate([v, jnp.ones((1,), f32)]) if one else v
        return jnp.pad(v, (0, 3 * CP - v.shape[0]))

    zero = jnp.zeros((C,), f32)
    qkvb = jnp.pad(jnp.stack([qv_bias[:C], zero, qv_bias[C:]]), ((0, 0), (0, pc))).reshape(-1)
    vecs = jnp.stack(
        [row(norm1_gain), row(norm1_bias, True), qkvb, row(proj_bias), row(norm2_gain),
         row(norm2_bias, True), row(fc1_bias), row(fc2_bias, True), row(conv_bias)]
        + [jnp.zeros((3 * CP,), f32)] * 7
    )
    return wqkv, wproj, wfc1, wfc2, wconv, vecs, score_extra(bias_table)


def on_device(
    images, widths, norm1_gain, norm1_bias, qkv_weight, qv_bias, bias_table, proj_weight, proj_bias,
    norm2_gain, norm2_bias, fc1_weight, fc1_bias, fc2_weight, fc2_bias, conv_weight, conv_bias, cotangent,
):
    count, rows_here, width, chans = images.shape
    img = images.reshape(rows_here, width, chans)
    cot = cotangent.reshape(rows_here, width, chans)
    scal = lax.div(widths, WIN)
    wqkv, wproj, wfc1, wfc2, wconv, vecs, extra = prepare(
        norm1_gain, norm1_bias, qkv_weight, qv_bias, bias_table, proj_weight, proj_bias,
        norm2_gain, norm2_bias, fc1_weight, fc1_bias, fc2_weight, fc2_bias, conv_weight, conv_bias,
    )
    res, ig, g_qkv, g_proj, g_fc1, g_fc2, g_conv, v = run_layer(
        lax.axis_size("rows"), lax.axis_size("imgs"),
        scal, img, cot, wqkv, wproj, wfc1, wfc2, wconv, vecs, extra,
    )
    return (
        res[None],
        ig[None],
        v[58, :C],
        v[59, :C],
        g_qkv,
        jnp.concatenate([v[44, :C], v[52, :C]]),
        v[60 : 60 + HEADS, :225].T,
        g_proj,
        v[28, :C],
        v[56, :C],
        v[57, :C],
        g_fc1,
        jnp.concatenate([v[4], v[12, : HID - CP]]),
        g_fc2,
        v[16, :C],
        g_conv,
        v[36, :C],
    )


def solution(mesh):
    big = P("imgs", "rows", None, None)
    in_specs = (big, P("imgs")) + (P(),) * 15 + (big,)
    out_specs = (big, big) + (P(),) * 15
    return jax.shard_map(
        on_device, mesh=mesh, in_specs=in_specs, out_specs=out_specs, check_vma=False
    )
```

```python
import functools

import jax
import jax.numpy as jnp
import numpy as np
from jax import lax
from jax.experimental import pallas as pl
from jax.experimental.pallas import tpu as pltpu
from jax.sharding import PartitionSpec as P

HEADS = 6
HEAD_DIM = 30
WIN = 8
SHIFT = 4
C = 180
CP = 256
HID = 360
HP = 384
AREA = WIN * WIN
HI = HEADS * AREA
LOG2E = 1.4426950408889634
SCALE = HEAD_DIM ** (-0.5)

CR = 192
FC2_ROWS = 368
A1_FC1 = 9 * CR
A1_FC2 = A1_FC1 + 2 * CR
A1_PROJ = A1_FC2 + FC2_ROWS
A1_USED = A1_PROJ + CR
A2_SMALL = 3 * CR
A2_USED = A2_SMALL + 16

f32 = jnp.float32
bf16 = jnp.bfloat16


def dot(a, b, ca=1, cb=0):
    return lax.dot_general(a, b, (((ca,), (cb,)), ((), ())), preferred_element_type=f32)


def lanes(shape):
    return lax.broadcasted_iota(jnp.int32, shape, len(shape) - 1)


def rows_of(shape):
    return lax.broadcasted_iota(jnp.int32, shape, len(shape) - 2)


def ln_fwd(x, gain, bias):
    real = (lanes((1, CP)) < C).astype(f32)
    mean = jnp.sum(x, axis=-1, keepdims=True) * (1.0 / C)
    xc = (x - mean) * real
    var = jnp.sum(xc * xc, axis=-1, keepdims=True) * (1.0 / C)
    rstd = lax.rsqrt(var + 1e-05)
    xhat = xc * rstd
    return xhat, rstd, xhat * gain + bias


def with_rstd(xhat, rstd):
    high = rstd.astype(bf16).astype(f32)
    lane = lanes((1, CP))
    return jnp.where(lane == 200, high, jnp.where(lane == 201, rstd - high, xhat))


def ln_bwd(dy, xhat, rstd, gain):
    a = dy * gain
    m1 = jnp.sum(a, axis=-1, keepdims=True) * (1.0 / C)
    m2 = jnp.sum(a * xhat, axis=-1, keepdims=True) * (1.0 / C)
    return rstd * (a - m1 - xhat * m2)


def gelu_pair(h):
    z = jnp.abs(h) * 0.7071067811865476
    d = 1.0 + 0.3275911 * z
    t = pl.reciprocal(d, approx=True)
    t = t * (2.0 - d * t)
    e = jnp.exp2(h * h * (-0.5 * LOG2E))
    poly = t * (
        0.254829592 + t * (-0.284496736 + t * (1.421413741 + t * (-1.453152027 + t * 1.061405429)))
    )
    q = 0.5 * poly * e
    phi = jnp.where(h >= 0, 1.0 - q, q)
    return h * phi, phi + h * (e * 0.3989422804014327)


def fold8(v):
    return jnp.sum(v.reshape(v.shape[0] // 8, 8, v.shape[1]), axis=0)


HP_DIM = 32


def by_rows(f, step, *arrays):
    rows = arrays[0].shape[0]
    parts = [f(*[a[i : i + step] for a in arrays]) for i in range(0, rows, step)]
    if not isinstance(parts[0], tuple):
        return jnp.concatenate(parts, axis=0)
    return tuple(jnp.concatenate(p, axis=0) for p in zip(*parts))


def added(values):
    return functools.reduce(jnp.add, values)


def head_mask(h):
    ln = lanes((1, 128))
    return (ln >= h * HP_DIM) & (ln < (h + 1) * HP_DIM)


def spread_heads(v, count):
    return jnp.concatenate(
        [jnp.where(head_mask(h), v, jnp.zeros_like(v)) for h in range(count)], axis=0
    )


def gather_heads(v, count):
    out = jnp.where(head_mask(0), v[:AREA], 0.0)
    for h in range(1, count):
        out = jnp.where(head_mask(h), v[h * AREA : (h + 1) * AREA], out)
    return out


GROUPS = ((0, 4), (4, 2))


def column_masks(width):
    return rows_of((256, CP)) < width


class AllReduce:
    def __init__(self, buf, out, r1, r2, r3, ssem, rsem, pr, chips, imgs, zsplit):
        self.buf, self.out, self.r1, self.r2, self.r3 = buf, out, r1, r2, r3
        self.ssem, self.rsem, self.chips, self.imgs = ssem, rsem, chips, imgs
        self.zsplit = zsplit
        rows = lax.axis_index("rows")
        self.core = lax.rem(rows, 2)
        self.chip = lax.div(rows, 2)
        self.z = lax.axis_index("imgs")
        self.piece = pr
        self.group = pr * imgs if zsplit else pr
        self.half = self.group * chips
        self.used = 0

    def copy(self, src, dst, device, n):
        return pltpu.make_async_remote_copy(
            src_ref=src,
            dst_ref=dst,
            send_sem=self.ssem.at[n],
            recv_sem=self.rsem.at[n],
            device_id=device,
            device_id_type=pl.DeviceIdType.MESH,
        )

    def rows(self, ref, start, size):
        return ref.at[pl.ds(pl.multiple_of(start, 16), size)]

    def base_half(self, core):
        return core * self.half

    def base_group(self, chip):
        return self.core * self.half + chip * self.group

    def base_piece(self, z):
        return self.base_group(self.chip) + (z * self.piece if self.zsplit else 0)

    def core_copy(self, ref, dst, n, gather):
        side = self.core if gather else 1 - self.core
        src = self.rows(ref, self.base_half(side), self.half)
        dst = src if dst is None else dst
        return [self.copy(src, dst, {"rows": self.chip * 2 + 1 - self.core}, n)]

    def chip_copies(self, ref, dst, n, gather):
        out = []
        for d in range(1, self.chips):
            to = lax.rem(self.chip + d, self.chips)
            src = self.rows(ref, self.base_group(self.chip if gather else to), self.group)
            to_ref = src if gather else dst.at[pl.ds((d - 1) * self.group, self.group)]
            out.append(self.copy(src, to_ref, {"rows": to * 2 + self.core}, n + d - 1))
        return out

    def img_copies(self, ref, dst, n, gather):
        out = []
        for d in range(1, self.imgs):
            to = lax.rem(self.z + d, self.imgs)
            src = self.rows(ref, self.base_piece(self.z if gather else to), self.piece)
            to_ref = src if gather else dst.at[pl.ds((d - 1) * self.piece, self.piece)]
            out.append(self.copy(src, to_ref, {"imgs": to}, n + d - 1))
        return out

    def start(self, copies):
        for c in copies:
            c.start()
        return copies

    def wait(self, copies):
        for c in copies:
            c.wait()

    def add(self, base, size, extra, count, stride, target):
        step = min(size, 64)
        while size % step:
            step -= 16

        @pl.loop(0, size // step)
        def _(i):
            at = pl.ds(pl.multiple_of(base + i * step, 16), step)
            total = self.buf[at, :].astype(f32)
            for d in range(count):
                total += extra[pl.ds(pl.multiple_of(d * stride + i * step, 16), step), :].astype(f32)
            target[at, :] = total.astype(bf16)

    def step(self, k):
        n2 = 1
        n3 = n2 + self.chips - 1
        n4 = n3 + self.imgs - 1
        n5 = n4 + self.imgs - 1
        n6 = n5 + self.chips - 1
        first = lambda: self.core_copy(self.buf, self.r1, 0, False)
        second = lambda: self.chip_copies(self.buf, self.r2, n2, False)
        third = lambda: self.img_copies(self.buf, self.r3, n3, False)
        fourth = lambda: self.img_copies(self.out, None, n4, True) if self.zsplit else []
        fifth = lambda: self.chip_copies(self.out, None, n5, True)
        sixth = lambda: self.core_copy(self.out, None, n6, True)
        if k == 0:
            self.start(first())
        elif k == 1:
            self.wait(first())
            self.add(self.base_half(self.core), self.half, self.r1, 1, 0, self.buf)
            self.start(second())
        elif k == 2:
            self.wait(second())
            self.add(
                self.base_group(self.chip), self.group, self.r2, self.chips - 1, self.group, self.buf
            )
            self.start(third())
        elif k == 3:
            self.wait(third())
            self.add(
                self.base_piece(self.z), self.piece, self.r3, self.imgs - 1, self.piece, self.out
            )
            self.start(fourth() if self.zsplit else fifth())
        elif k == 4:
            if self.zsplit:
                self.wait(fourth())
                self.start(fifth())
        elif k == 5:
            self.wait(fifth())
            self.start(sixth())
        elif k == 6:
            self.wait(sixth())


def all_reduce_sems(chips, imgs):
    return 2 * (1 + chips - 1 + imgs - 1)


def layer_kernel(
    chips,
    imgs,
    piece1,
    piece2,
    scal,
    img,
    cot,
    wqkv,
    wproj,
    wfc1,
    wfc2,
    wconv,
    vecs,
    extra,
    res_out,
    ig_out,
    o_qkv,
    o_proj,
    o_fc1,
    o_fc2,
    o_conv,
    o_vec,
    d_qkv,
    d_proj,
    d_fc1,
    d_fc2,
    d_conv,
    d_norm,
    d_rel,
    io1,
    io2,
    xband,
    gband,
    gcat,
    llbuf,
    xhat1,
    normed,
    qkv,
    probs,
    mixed,
    winf,
    fgrad,
    do_buf,
    edge,
    tmp,
    a1_buf,
    a1_out,
    a1_r1,
    a1_r2,
    a1_r3,
    a2_buf,
    a2_out,
    a2_r1,
    a2_r2,
    a2_r3,
    lsem,
    hs,
    hr,
    a1_s,
    a1_r,
    a2_s,
    a2_r,
):
    stripes = 2 * chips
    rank = lax.axis_index("rows")
    core = lax.rem(rank, 2)
    up = lax.rem(rank + stripes - 1, stripes)
    down = lax.rem(rank + 1, stripes)
    ar1 = AllReduce(a1_buf, a1_out, a1_r1, a1_r2, a1_r3, a1_s, a1_r, piece1, chips, imgs, True)
    ar2 = AllReduce(a2_buf, a2_out, a2_r1, a2_r2, a2_r3, a2_s, a2_r, piece2, chips, imgs, False)

    barrier = pltpu.get_barrier_semaphore()
    peers = [{"rows": up}, {"rows": down}]
    peers += [{"rows": lax.rem(rank + 2 * d, stripes)} for d in range(1, chips)]
    peers += [{"imgs": lax.rem(ar1.z + d, imgs)} for d in range(1, imgs)]
    for peer in peers:
        pl.semaphore_signal(barrier, inc=1, device_id=peer, device_id_type=pl.DeviceIdType.MESH)
    pl.semaphore_wait(barrier, len(peers))

    def remote(src, dst, to, n):
        return pltpu.make_async_remote_copy(
            src_ref=src,
            dst_ref=dst,
            send_sem=hs.at[n],
            recv_sem=hr.at[n],
            device_id={"rows": to},
            device_id_type=pl.DeviceIdType.MESH,
        )

    send_img = remote(img.at[pl.ds(0, 4)], io2.at[pl.ds(16, 4)], up, 0)
    send_cot = remote(cot.at[pl.ds(0, 5)], io1.at[pl.ds(16, 5)], up, 1)
    send_cot.start()
    send_img.start()
    load_cot = pltpu.make_async_copy(cot, io1.at[pl.ds(0, 16)], lsem.at[0])
    load_img = pltpu.make_async_copy(img, io2.at[pl.ds(0, 16)], lsem.at[1])
    load_cot.start()
    load_img.start()

    nb = scal[0]
    width = nb * WIN
    is_last = rank == stripes - 1
    joined = jnp.where(is_last, 0.0, 1.0)
    NW = 256 // WIN
    RM = 256

    def vec(i, n):
        return vecs[i : i + 1, 0:n]

    def row_at(pos, count=1):
        return pl.ds(pl.multiple_of(pos * 256, 256), count * 256)

    xband[:, :, 128:256] = jnp.zeros((8, 256, 128), f32)
    tmp[...] = jnp.zeros_like(tmp)
    for ref in (d_qkv, d_proj, d_fc1, d_fc2, d_conv, d_norm, d_rel):
        ref[...] = jnp.zeros_like(ref)
    a1_buf[A1_USED:, :] = jnp.zeros((a1_buf.shape[0] - A1_USED, CP), bf16)
    a2_buf[A2_USED:, :] = jnp.zeros((a2_buf.shape[0] - A2_USED, CP), bf16)

    col_in = rows_of((256, C)) < width
    col_in_p = rows_of((256, CP)) < width

    def put_g(pos, row, flag):
        g = jnp.where(col_in, row.astype(f32), 0.0) * flag
        tmp[8:264, 0:C] = g
        at = row_at(pos)
        gcat[at, 0:CP] = tmp[9:265, :].astype(bf16)
        gcat[at, CP : 2 * CP] = tmp[8:264, :].astype(bf16)
        gcat[at, 2 * CP : 3 * CP] = tmp[7:263, :].astype(bf16)

    load_cot.wait()

    @pl.loop(0, 13)
    def _(r):
        put_g(r, io1[r + 3], 1.0)

    put_g(14, io1[15], joined)
    load_img.wait()

    pos_hi = rows_of((1, WIN, CP)) >= SHIFT

    def rolled(a, b):
        t = jnp.where(pos_hi, a, b)
        return pltpu.roll(t, SHIFT, 1)

    def to_win(ref, k):
        nxt = jnp.minimum(k + 1, NW - 1)
        a = ref[:, pl.ds(pl.multiple_of(k * WIN, WIN), WIN), :]
        b = ref[:, pl.ds(pl.multiple_of(nxt * WIN, WIN), WIN), :]
        b = jnp.where(k == nb - 1, ref[:, 0:WIN, :], b)
        return rolled(a, b).reshape(AREA, CP)

    def from_win(ref, band):
        def block(k):
            at = pl.multiple_of((band * NW + k) * AREA, AREA)
            return ref[pl.ds(at, AREA), :].reshape(WIN, WIN, CP)

        @pl.loop(0, NW, unroll=4)
        def _(k):
            b = block(k)
            edge[...] = jnp.where(k == nb - 1, b, edge[...])
            xband[:, pl.ds(pl.multiple_of(k * WIN, WIN), WIN), :] = rolled(
                block(jnp.maximum(k - 1, 0)), b
            )

        xband[:, 0:WIN, :] = rolled(edge[...], block(0))

    def win_rows(w):
        return pl.ds(pl.multiple_of(w * AREA, AREA), AREA)

    @pl.loop(0, 2)
    def _(band):
        @pl.when(band == 1)
        def _():
            send_cot.wait()
            send_img.wait()
            put_g(13, io1[16], joined)

            @pl.loop(0, 5)
            def _(r):
                put_g(15 + r, io1[16 + r], 1.0)

        @pl.loop(0, 8)
        def _(y):
            xband[y, :, 0:C] = io2[band * 8 + y + 4].astype(f32)

        @pl.loop(0, 8)
        def _(y):
            r = band * 8 + y
            pos = r + 1 + jnp.where(r >= 12, 2, 0)
            acc = None
            for a in range(3):
                d = dot(gcat[row_at(pos + 1 - a), :], wconv[a], 1, 1)
                acc = d if acc is None else acc + d
            gband[y] = jnp.where(col_in_p, acc, 0.0)

        @pl.loop(0, 4)
        def _(gg):
            g = band * 4 + gg
            k0 = gg * 8
            gs = pl.ds(pl.multiple_of(g * 512, 512), 512)

            xs = [to_win(xband, k0 + w) for w in range(8)]
            for w in range(8):
                winf[win_rows(g * 8 + w), :] = xs[w]
                fgrad[win_rows(g * 8 + w), :] = to_win(gband, k0 + w)
                xhat, rs_, ln_out = ln_fwd(xs[w], vec(0, CP), vec(1, CP))
                xhat1[win_rows(g * 8 + w), :] = with_rstd(xhat, rs_).astype(bf16)
                normed[win_rows(g * 8 + w), :] = ln_out.astype(bf16)

            for n in range(3):
                sl = slice(n * CP, (n + 1) * CP)
                qkv[gs, sl] = (dot(normed[gs, :], wqkv[:, sl]) + vecs[2:3, sl]).astype(bf16)

            i = 0
            if True:
                which = jnp.where((band == 1) & is_last, 2, 0)
                jobs = []
                for w in range(8):
                    rs = win_rows(g * 8 + i * 8 + w)
                    edge_win = k0 + i * 8 + w == nb - 1
                    for n, (h0, count) in enumerate(GROUPS):
                        jobs.append((rs, w, edge_win, n, count, slice(h0 * AREA, (h0 + count) * AREA)))
                qs = [qkv[rs, n * 128 : (n + 1) * 128] for rs, w, ew, n, count, hl in jobs]
                ks = [qkv[rs, CP + n * 128 : CP + (n + 1) * 128] for rs, w, ew, n, count, hl in jobs]
                vs = [qkv[rs, 2 * CP + n * 128 : 2 * CP + (n + 1) * 128] for rs, w, ew, n, count, hl in jobs]
                ss = [dot(k, spread_heads(q, job[4]), 1, 1) for q, k, job in zip(qs, ks, jobs)]
                ps = []
                for s, (rs, w, ew, n, count, hl) in zip(ss, jobs):
                    more = jnp.where(ew, extra[which + 1, :, hl], extra[which, :, hl])
                    s = s * (SCALE * LOG2E) + more
                    top = jnp.max(s, axis=0, keepdims=True)
                    e = jnp.exp2(s - top)
                    total = jnp.sum(e, axis=0, keepdims=True)
                    ps.append((e * (1.0 / total)).astype(bf16))
                os = [gather_heads(dot(p, v, 0, 0), job[4]) for p, v, job in zip(ps, vs, jobs)]
                for p, o, (rs, w, ew, n, count, hl) in zip(ps, os, jobs):
                    probs[rs, hl] = p
                    if n == 0:
                        o = jnp.where(lanes((1, 128)) == HEAD_DIM, 1.0, o)
                    mixed[win_rows(i * 8 + w), n * 128 : (n + 1) * 128] = o.astype(bf16)

            parts = range(0, 512, 256)
            at_rows = [pl.ds(pl.multiple_of(g * 512 + r, 256), 256) for r in parts]
            mixes = [mixed[r : r + 256, :] for r in parts]
            firsts = [dot(m, wproj[...]) + vec(3, CP) + winf[rs, :] for m, rs in zip(mixes, at_rows)]

            def norm2(v):
                xhat, rs_, ln_out = ln_fwd(v, vec(4, CP), vec(5, CP))
                return xhat, rs_, ln_out.astype(bf16)

            def activate(v):
                ac, dg = gelu_pair(v + vec(6, HP))
                return jnp.where(lanes((1, HP)) == HID, 1.0, ac).astype(bf16), dg.astype(bf16)

            norms = [by_rows(norm2, 64, v) for v in firsts]
            n2s = [n[2] for n in norms]
            acts = [by_rows(activate, 64, dot(n2, wfc1[...])) for n2 in n2s]
            for fs, (ac, dg), rs in zip(firsts, acts, at_rows):
                winf[rs, :] = fs + dot(ac, wfc2[...]) + vec(7, CP)
            lgs = [fgrad[rs, :] for rs in at_rows]
            mgs = [lg.astype(bf16) for lg in lgs]
            hgs = [
                (dot(mg, wfc2[...], 1, 1).astype(bf16).astype(f32) * dg.astype(f32)).astype(bf16)
                for mg, (ac, dg) in zip(mgs, acts)
            ]
            dns = [dot(hg, wfc1[...], 1, 1).astype(bf16) for hg in hgs]

            def back2(dn2, xh, rs_, lg):
                dn2 = dn2.astype(f32)
                fg = lg + ln_bwd(dn2, xh, rs_, vec(4, CP))
                return fg, fg.astype(bf16), fold8(dn2 * xh), fold8(dn2)

            backs = [
                by_rows(back2, 64, dn, n[0], n[1], lg) for dn, n, lg in zip(dns, norms, lgs)
            ]
            ats = [b[1] for b in backs]
            for b, rs in zip(backs, at_rows):
                fgrad[rs, :] = b[0]
                do_buf[rs, :] = dot(b[1], wproj[...], 1, 1).astype(bf16)
            d_norm[0:8, :] += added([fold8(b[2]) for b in backs])
            d_norm[8:16, :] += added([fold8(b[3]) for b in backs])
            join = lambda vs: jnp.concatenate(vs, axis=0)
            mg = join(mgs)
            d_fc2[...] += dot(join([ac for ac, dg in acts])[:, 0:FC2_ROWS], mg, 0, 0)
            d_fc1[...] += dot(join(n2s)[:, 0:CR], join(hgs), 0, 0)
            d_proj[...] += dot(mixed[:, 0:CR], join(ats), 0, 0)

    @pl.loop(0, 2)
    def _(band):
        from_win(winf, band)

        @pl.loop(0, 8)
        def _(y):
            r = band * 8 + y
            pos = r + 1 + jnp.where(r >= 12, 2, 0)
            llbuf[row_at(pos), :] = jnp.where(col_in_p, xband[y], 0.0).astype(bf16)

    send_up = remote(llbuf.at[pl.ds(256, 256)], llbuf.at[pl.ds(19 * 256, 256)], up, 2)
    send_down = remote(llbuf.at[pl.ds(18 * 256, 256)], llbuf.at[pl.ds(0, 256)], down, 3)
    send_up.start()
    send_down.start()
    joined_low = joined.astype(bf16)
    llbuf[13 * 256 : 14 * 256, :] = llbuf[15 * 256 : 16 * 256, :] * joined_low
    llbuf[14 * 256 : 15 * 256, :] = llbuf[12 * 256 : 13 * 256, :] * joined_low

    def wgrad_rows(n):
        start = 1 + 4 * n + jnp.where(n == 3, 2, 0)
        gs = gcat[row_at(start, 4), :]
        for a in range(3):
            d_conv[a] += dot(llbuf[row_at(start + a - 1, 4), 0:CR], gs, 0, 0)

    @pl.loop(1, 3)
    def _(n):
        wgrad_rows(n)

    send_up.wait()
    send_down.wait()

    @pl.loop(0, 2)
    def _(n):
        wgrad_rows(n * 3)

    for a in range(3):
        for b in range(3):
            at = (a * 3 + b) * CR
            a1_buf[at : at + CR, :] = d_conv[a, :, b * CP : (b + 1) * CP].astype(bf16)
    a1_buf[A1_FC1 : A1_FC1 + CR, :] = d_fc1[:, 0:CP].astype(bf16)
    a1_buf[A1_FC1 + CR : A1_FC1 + 2 * CR, 0:128] = d_fc1[:, CP:HP].astype(bf16)
    a1_buf[A1_FC1 + CR : A1_FC1 + 2 * CR, 128:256] = jnp.zeros((CR, 128), bf16)
    a1_buf[A1_FC2 : A1_FC2 + FC2_ROWS, :] = d_fc2[...].astype(bf16)
    a1_buf[A1_PROJ : A1_PROJ + CR, :] = d_proj[...].astype(bf16)
    ar1.step(0)

    @pl.loop(0, 8)
    def _(g):
        gs = pl.ds(pl.multiple_of(g * 512, 512), 512)

        i = 0
        if True:
            jobs = []
            for w in range(8):
                rs = win_rows(g * 8 + i * 8 + w)
                for n, (h0, count) in enumerate(GROUPS):
                    jobs.append((rs, n, count, slice(h0 * AREA, (h0 + count) * AREA)))
            qs = [qkv[rs, n * 128 : (n + 1) * 128] for rs, n, count, hl in jobs]
            ks = [qkv[rs, CP + n * 128 : CP + (n + 1) * 128] for rs, n, count, hl in jobs]
            vs = [qkv[rs, 2 * CP + n * 128 : 2 * CP + (n + 1) * 128] for rs, n, count, hl in jobs]
            dos = [spread_heads(do_buf[rs, n * 128 : (n + 1) * 128], count) for rs, n, count, hl in jobs]
            pbs = [probs[rs, hl] for rs, n, count, hl in jobs]
            dps = [dot(v, d, 1, 1) for v, d in zip(vs, dos)]
            dvs = [dot(p, d) for p, d in zip(pbs, dos)]
            dss = []
            for dp, pb in zip(dps, pbs):
                p = pb.astype(f32)
                dss.append((p * (dp - jnp.sum(p * dp, axis=0, keepdims=True))).astype(bf16))
            dks = [dot(ds, spread_heads(q, job[2])) * SCALE for ds, q, job in zip(dss, qs, jobs)]
            dqs = [gather_heads(dot(ds, k, 0, 0), job[2]) * SCALE for ds, k, job in zip(dss, ks, jobs)]
            for n, (h0, count) in enumerate(GROUPS):
                hl = slice(h0 * AREA, (h0 + count) * AREA)
                d_rel[:, hl] += functools.reduce(jnp.add, [d.astype(f32) for d in dss[n::2]])
            for dq, dk, dv, (rs, n, count, hl) in zip(dqs, dks, dvs, jobs):
                qkv[rs, n * 128 : (n + 1) * 128] = dq.astype(bf16)
                qkv[rs, CP + n * 128 : CP + (n + 1) * 128] = dk.astype(bf16)
                qkv[rs, 2 * CP + n * 128 : 2 * CP + (n + 1) * 128] = dv.astype(bf16)

        d_qkv[...] += dot(normed[gs, 0:CR], qkv[gs, :], 0, 0)

        dn1 = dot(qkv[gs, :], wqkv[...], 1, 1).astype(bf16)

        def back1(dn, xhat, fg):
            dn, xhat = dn.astype(f32), xhat.astype(f32)
            out = fg + ln_bwd(dn, xhat, xhat[:, 200:201] + xhat[:, 201:202], vec(0, CP))
            return out, fold8(dn * xhat), fold8(dn)

        back = by_rows(back1, 64, dn1, xhat1[gs, :], fgrad[gs, :])
        fgrad[gs, :] = back[0]
        d_norm[16:24, :] += fold8(back[1])
        d_norm[24:32, :] += fold8(back[2])

        for k, at in enumerate((0, 2, 4, 6)):

            @pl.when(g == at)
            def _(k=k):
                ar1.step(k + 1)

    for n in range(3):
        a2_buf[n * CR : (n + 1) * CR, :] = d_qkv[:, n * CP : (n + 1) * CP].astype(bf16)
    norms = jnp.sum(d_norm[...].reshape(4, 8, CP), axis=1)
    small = jnp.concatenate([norms, table_sum(d_rel[...]), jnp.zeros((4, CP), f32)], axis=0)
    a2_buf[A2_SMALL : A2_SMALL + 16, :] = small.astype(bf16)
    ar2.step(0)

    def grad_rows(band):
        from_win(fgrad, band)

        @pl.loop(0, 8)
        def _(y):
            r = band * 8 + y
            pos = r + 1 + jnp.where(r >= 12, 2, 0)
            v = xband[y] + gcat[row_at(pos), CP : 2 * CP].astype(f32)
            io2[r] = jnp.where(col_in_p, v, 0.0)[:, 0:C].astype(bf16)

    def conv_rows(lo, hi):
        @pl.loop(lo, hi)
        def _(r):
            pos = r + 1 + jnp.where(r >= 12, 2, 0)
            acc = None
            for a in range(3):
                d = dot(llbuf[row_at(pos + a - 1), :], wconv[a])
                acc = d if acc is None else acc + d
            tmp[8:264, :] = acc[:, 0:CP]
            tmp[280:536, :] = acc[:, 2 * CP : 3 * CP]
            out = acc[:, CP : 2 * CP] + tmp[7:263, :] + tmp[281:537, :] + vec(8, CP)
            out = out[:, 0:C] + io2[r + 4].astype(f32)
            io1[r] = jnp.where(col_in, out, 0.0).astype(bf16)

    conv_rows(12, 16)
    send_res = remote(io1.at[pl.ds(12, 4)], res_out.at[pl.ds(0, 4)], down, 4)
    send_res.start()
    ar1.step(5)
    ar2.step(1)
    conv_rows(0, 8)
    ar2.step(2)
    ar1.step(6)
    conv_rows(8, 12)
    store_res = pltpu.make_async_copy(io1.at[pl.ds(0, 12)], res_out.at[pl.ds(4, 12)], lsem.at[2])
    store_res.start()
    grad_rows(1)
    send_ig = remote(io2.at[pl.ds(12, 4)], ig_out.at[pl.ds(0, 4)], down, 5)
    send_ig.start()
    ar2.step(3)
    grad_rows(0)
    store_ig = pltpu.make_async_copy(io2.at[pl.ds(0, 12)], ig_out.at[pl.ds(4, 12)], lsem.at[3])
    store_ig.start()
    ar2.step(5)

    for a in range(3):
        for b in range(3):
            at = (a * 3 + b) * CR
            o_conv[a, b] = a1_out[at : at + CR, :].astype(f32)[0:C, 0:C]
    o_fc1[:, 0:CP] = a1_out[A1_FC1 : A1_FC1 + CR, :].astype(f32)[0:C, :]
    o_fc1[:, CP:HID] = a1_out[A1_FC1 + CR : A1_FC1 + 2 * CR, :].astype(f32)[0:C, 0 : HID - CP]
    o_fc2[...] = a1_out[A1_FC2 : A1_FC2 + FC2_ROWS, :].astype(f32)[0:HID, 0:C]
    for h in range(HEADS):
        at = A1_PROJ + h * HP_DIM
        o_proj[h * HEAD_DIM : (h + 1) * HEAD_DIM, :] = a1_out[at : at + HP_DIM, :].astype(f32)[
            0:HEAD_DIM, 0:C
        ]
    o_vec[0:8, :] = a1_out[A1_FC1 + 176 : A1_FC1 + 192, :].astype(f32)[0:8]
    o_vec[8:16, :] = a1_out[A1_FC1 + CR + 176 : A1_FC1 + CR + 192, :].astype(f32)[0:8]
    o_vec[16:24, :] = a1_out[A1_FC2 + 352 : A1_FC2 + 368, :].astype(f32)[8:16]
    o_vec[24:32, :] = a1_out[A1_PROJ + 16 : A1_PROJ + 32, :].astype(f32)[8:16]
    o_vec[32:40, :] = a1_out[4 * CR + 176 : 4 * CR + 192, :].astype(f32)[0:8]
    ar2.step(6)
    wide = lax.broadcasted_iota(jnp.int32, (CP, CP), 0)
    dense = lax.broadcasted_iota(jnp.int32, (CP, CP), 1)
    heads_out = (wide == dense + lax.div(dense, HEAD_DIM) * (HP_DIM - HEAD_DIM)) & (dense < C)
    heads_out = heads_out.astype(bf16)
    for n in range(3):
        o_qkv[:, n * C : (n + 1) * C] = dot(a2_out[n * CR : (n + 1) * CR, :], heads_out)[0:C, 0:C]
    o_vec[40:48, :] = dot(a2_out[176:192, :], heads_out)[0:8]
    o_vec[48:56, :] = dot(a2_out[2 * CR + 176 : 2 * CR + 192, :], heads_out)[0:8]
    o_vec[56:72, :] = a2_out[A2_SMALL : A2_SMALL + 16, :].astype(f32)
    send_res.wait()
    send_ig.wait()
    store_res.wait()
    store_ig.wait()


def table_sum(d_rel):
    row = lax.broadcasted_iota(jnp.int32, (AREA, CP), 0)
    lane = lax.broadcasted_iota(jnp.int32, (AREA, CP), 1)
    put = (lane == row + lax.div(row, WIN) * (WIN - 1)).astype(bf16)
    heads = []
    for h in range(HEADS):
        v = d_rel[:, h * AREA : (h + 1) * AREA]
        v1 = v.astype(bf16)
        v2 = (v - v1.astype(f32)).astype(bf16)
        wide = dot(v1, put) + dot(v2, put)
        total = None
        for y in range(WIN):
            part = pltpu.roll(wide[y * WIN : (y + 1) * WIN, :], 112 - 15 * y, 1)
            total = part if total is None else total + part
        heads.append(total)
    out = None
    for x in range(WIN):
        rows = jnp.concatenate([t[x : x + 1] for t in heads] + [jnp.zeros((2, CP), f32)], axis=0)
        rows = pltpu.roll(rows, CP - x, 1) if x else rows
        out = rows if out is None else out + rows
    return out


def relative_index():
    coords = np.arange(AREA)
    row, col = coords // WIN, coords % WIN
    return (row[:, None] - row[None, :] + WIN - 1) * (2 * WIN - 1) + col[:, None] - col[None, :] + WIN - 1


def score_extra(bias_table):
    hot = jnp.asarray(
        (relative_index().T.reshape(-1)[:, None] == np.arange(225)[None, :]).astype(np.float32)
    )
    rel = jnp.dot(hot, bias_table, precision=lax.Precision.HIGHEST)
    rel = rel.reshape(AREA, AREA, HEADS).transpose(0, 2, 1).reshape(AREA, HI)
    coords = np.arange(AREA)
    yh = coords // WIN >= SHIFT
    xh = coords % WIN >= SHIFT
    ydiff = yh[:, None] != yh[None, :]
    xdiff = xh[:, None] != xh[None, :]
    masks = np.stack([np.zeros_like(ydiff), xdiff, ydiff, ydiff | xdiff])
    masks = np.where(np.tile(masks, (1, 1, HEADS)), -100.0, 0.0).astype(np.float32)
    return (rel[None] + jnp.asarray(masks)) * LOG2E


VM = pl.BlockSpec(memory_space=pltpu.VMEM)
SM = pl.BlockSpec(memory_space=pltpu.SMEM)
HB = pl.BlockSpec(memory_space=pl.ANY)


def up_to(n, m):
    return (n + m - 1) // m * m


def run_layer(stripes, imgs, scal, img, cot, wqkv, wproj, wfc1, wfc2, wconv, vecs, extra):
    S = jax.ShapeDtypeStruct
    V = pltpu.VMEM
    chips = stripes // 2
    piece1 = up_to(-(-A1_USED // (stripes * imgs)), 16)
    piece2 = up_to(-(-A2_USED // stripes), 16)
    half1 = piece1 * imgs * chips
    half2 = piece2 * chips
    sems = 2 * (chips + imgs - 1)
    dma = pltpu.SemaphoreType.DMA
    return pl.pallas_call(
        functools.partial(layer_kernel, chips, imgs, piece1, piece2),
        out_shape=(
            S((16, 256, C), bf16),
            S((16, 256, C), bf16),
            S((C, 3 * C), f32),
            S((C, C), f32),
            S((C, HID), f32),
            S((HID, C), f32),
            S((3, 3, C, C), f32),
            S((72, CP), f32),
        ),
        in_specs=[SM, HB, HB] + [VM] * 7,
        out_specs=[HB] * 2 + [VM] * 6,
        scratch_shapes=[
            V((CR, 3 * CP), f32),
            V((CR, CP), f32),
            V((CR, HP), f32),
            V((FC2_ROWS, CP), f32),
            V((3, CR, 3 * CP), f32),
            V((32, CP), f32),
            V((AREA, HI), f32),
            V((21, 256, C), bf16),
            V((20, 256, C), bf16),
            V((8, 256, CP), f32),
            V((8, 256, CP), f32),
            V((20 * 256, 3 * CP), bf16),
            V((20 * 256, CP), bf16),
            V((4096, CP), bf16),
            V((4096, CP), bf16),
            V((4096, 3 * CP), bf16),
            V((4096, HI), bf16),
            V((512, CP), bf16),
            V((4096, CP), f32),
            V((4096, CP), f32),
            V((4096, CP), bf16),
            V((WIN, WIN, CP), f32),
            V((544, CP), f32),
            V((2 * half1, CP), bf16),
            V((2 * half1, CP), bf16),
            V((half1, CP), bf16),
            V(((chips - 1) * piece1 * imgs, CP), bf16),
            V(((imgs - 1) * piece1, CP), bf16),
            V((2 * half2, CP), bf16),
            V((2 * half2, CP), bf16),
            V((half2, CP), bf16),
            V(((chips - 1) * piece2, CP), bf16),
            V(((imgs - 1) * piece2, CP), bf16),
            dma((4,)),
            dma((6,)),
            dma((6,)),
            dma((sems,)),
            dma((sems,)),
            dma((sems,)),
            dma((sems,)),
        ],
        compiler_params=pltpu.CompilerParams(
            vmem_limit_bytes=63 * 1024 * 1024, collective_id=0, has_side_effects=True
        ),
        name="layer",
    )(scal, img, cot, wqkv, wproj, wfc1, wfc2, wconv, vecs, extra)


def prepare(norm1_gain, norm1_bias, qkv_weight, qv_bias, bias_table, proj_weight, proj_bias,
            norm2_gain, norm2_bias, fc1_weight, fc1_bias, fc2_weight, fc2_bias, conv_weight, conv_bias):
    pc = CP - C
    hp = HP_DIM - HEAD_DIM
    wqkv = jnp.pad(qkv_weight.reshape(C, 3, HEADS, HEAD_DIM), ((0, pc), (0, 0), (0, 2), (0, hp)))
    wqkv = wqkv.reshape(CP, 3 * CP)
    wproj = jnp.pad(proj_weight.reshape(HEADS, HEAD_DIM, C), ((0, 2), (0, hp), (0, pc))).reshape(CP, CP)
    wfc1 = jnp.pad(fc1_weight, ((0, pc), (0, HP - HID)))
    wfc2 = jnp.pad(fc2_weight, ((0, HP - HID), (0, pc)))
    wconv = jnp.pad(conv_weight.transpose(0, 2, 1, 3), ((0, 0), (0, pc), (0, 0), (0, pc)))
    wconv = wconv.reshape(3, CP, 3 * CP)

    def row(v, one=False):
        v = jnp.concatenate([v, jnp.ones((1,), f32)]) if one else v
        return jnp.pad(v, (0, 3 * CP - v.shape[0]))

    zero = jnp.zeros((C,), f32)
    qkvb = jnp.stack([qv_bias[:C], zero, qv_bias[C:]]).reshape(3, HEADS, HEAD_DIM)
    qkvb = jnp.pad(qkvb, ((0, 0), (0, 2), (0, hp))).reshape(-1)
    vecs = jnp.stack(
        [row(norm1_gain), row(norm1_bias, True), qkvb, row(proj_bias), row(norm2_gain),
         row(norm2_bias, True), row(fc1_bias), row(fc2_bias, True), row(conv_bias)]
        + [jnp.zeros((3 * CP,), f32)] * 7
    )
    return wqkv, wproj, wfc1, wfc2, wconv, vecs, score_extra(bias_table)


def on_device(
    images, widths, norm1_gain, norm1_bias, qkv_weight, qv_bias, bias_table, proj_weight, proj_bias,
    norm2_gain, norm2_bias, fc1_weight, fc1_bias, fc2_weight, fc2_bias, conv_weight, conv_bias, cotangent,
):
    count, rows_here, width, chans = images.shape
    img = images.reshape(rows_here, width, chans)
    cot = cotangent.reshape(rows_here, width, chans)
    scal = lax.div(widths, WIN)
    wqkv, wproj, wfc1, wfc2, wconv, vecs, extra = prepare(
        norm1_gain, norm1_bias, qkv_weight, qv_bias, bias_table, proj_weight, proj_bias,
        norm2_gain, norm2_bias, fc1_weight, fc1_bias, fc2_weight, fc2_bias, conv_weight, conv_bias,
    )
    res, ig, g_qkv, g_proj, g_fc1, g_fc2, g_conv, v = run_layer(
        lax.axis_size("rows"), lax.axis_size("imgs"),
        scal, img, cot, wqkv, wproj, wfc1, wfc2, wconv, vecs, extra,
    )
    return (
        res[None],
        ig[None],
        v[58, :C],
        v[59, :C],
        g_qkv,
        jnp.concatenate([v[44, :C], v[52, :C]]),
        v[60 : 60 + HEADS, :225].T,
        g_proj,
        v[30, :C],
        v[56, :C],
        v[57, :C],
        g_fc1,
        jnp.concatenate([v[4], v[12, : HID - CP]]),
        g_fc2,
        v[16, :C],
        g_conv,
        v[36, :C],
    )


def solution(mesh):
    big = P("imgs", "rows", None, None)
    in_specs = (big, P("imgs")) + (P(),) * 15 + (big,)
    out_specs = (big, big) + (P(),) * 15
    return jax.shard_map(
        on_device, mesh=mesh, in_specs=in_specs, out_specs=out_specs, check_vma=False
    )
```

```python
import functools

import jax
import jax.numpy as jnp
import numpy as np
from jax import lax
from jax.experimental import pallas as pl
from jax.experimental.pallas import tpu as pltpu
from jax.sharding import PartitionSpec as P

HEADS = 6
HEAD_DIM = 30
WIN = 8
SHIFT = 4
C = 180
CP = 256
HID = 360
HP = 384
AREA = WIN * WIN
HI = HEADS * AREA
LOG2E = 1.4426950408889634
SCALE = HEAD_DIM ** (-0.5)

CR = 192
A_USED = 5 * CR
B_SMALL = 5 * CR
B_USED = B_SMALL + 32
C_MIX = 9 * CR
C_FC1 = C_MIX + 5 * CR
C_USED = C_FC1 + 2 * CR

f32 = jnp.float32
bf16 = jnp.bfloat16


def dot(a, b, ca=1, cb=0):
    return lax.dot_general(a, b, (((ca,), (cb,)), ((), ())), preferred_element_type=f32)


def lanes(shape):
    return lax.broadcasted_iota(jnp.int32, shape, len(shape) - 1)


def rows_of(shape):
    return lax.broadcasted_iota(jnp.int32, shape, len(shape) - 2)


def ln_fwd(x, gain, bias):
    real = (lanes((1, CP)) < C).astype(f32)
    mean = jnp.sum(x, axis=-1, keepdims=True) * (1.0 / C)
    xc = (x - mean) * real
    var = jnp.sum(xc * xc, axis=-1, keepdims=True) * (1.0 / C)
    rstd = lax.rsqrt(var + 1e-05)
    xhat = xc * rstd
    return xhat, rstd, xhat * gain + bias


def with_rstd(xhat, rstd):
    high = rstd.astype(bf16).astype(f32)
    lane = lanes((1, CP))
    return jnp.where(lane == 200, high, jnp.where(lane == 201, rstd - high, xhat))


def ln_bwd(dy, xhat, rstd, gain):
    a = dy * gain
    m1 = jnp.sum(a, axis=-1, keepdims=True) * (1.0 / C)
    m2 = jnp.sum(a * xhat, axis=-1, keepdims=True) * (1.0 / C)
    return rstd * (a - m1 - xhat * m2)


def gelu_pair(h):
    z = jnp.abs(h) * 0.7071067811865476
    d = 1.0 + 0.3275911 * z
    t = pl.reciprocal(d, approx=True)
    t = t * (2.0 - d * t)
    e = jnp.exp2(h * h * (-0.5 * LOG2E))
    poly = t * (
        0.254829592 + t * (-0.284496736 + t * (1.421413741 + t * (-1.453152027 + t * 1.061405429)))
    )
    q = 0.5 * poly * e
    phi = jnp.where(h >= 0, 1.0 - q, q)
    return h * phi, phi + h * (e * 0.3989422804014327)


def fold8(v):
    return jnp.sum(v.reshape(v.shape[0] // 8, 8, v.shape[1]), axis=0)


HP_DIM = 32


def by_rows(f, step, *arrays):
    rows = arrays[0].shape[0]
    parts = [f(*[a[i : i + step] for a in arrays]) for i in range(0, rows, step)]
    if not isinstance(parts[0], tuple):
        return jnp.concatenate(parts, axis=0)
    return tuple(jnp.concatenate(p, axis=0) for p in zip(*parts))


def added(values):
    return functools.reduce(jnp.add, values)


def head_mask(h):
    ln = lanes((1, 128))
    return (ln >= h * HP_DIM) & (ln < (h + 1) * HP_DIM)


def spread_heads(v, count):
    return jnp.concatenate(
        [jnp.where(head_mask(h), v, jnp.zeros_like(v)) for h in range(count)], axis=0
    )


def gather_heads(v, count):
    out = jnp.where(head_mask(0), v[:AREA], 0.0)
    for h in range(1, count):
        out = jnp.where(head_mask(h), v[h * AREA : (h + 1) * AREA], out)
    return out


GROUPS = ((0, 4), (4, 2))


def column_masks(width):
    return rows_of((256, CP)) < width


TURNS = ((1, (("a", 2), ("c", 1))), (2, (("a", 3),)), (5, (("c", 2), ("a", 4))))


class AllReduce:
    def __init__(self, buf, out, r1, r2, r3, ssem, rsem, pr, chips, imgs, zsplit):
        self.buf, self.out, self.r1, self.r2, self.r3 = buf, out, r1, r2, r3
        self.ssem, self.rsem, self.chips, self.imgs = ssem, rsem, chips, imgs
        self.zsplit = zsplit
        rows = lax.axis_index("rows")
        self.core = lax.rem(rows, 2)
        self.chip = lax.div(rows, 2)
        self.z = lax.axis_index("imgs")
        self.piece = pr
        self.group = pr * imgs if zsplit else pr
        self.half = self.group * chips
        self.used = 0

    def copy(self, src, dst, device, n):
        return pltpu.make_async_remote_copy(
            src_ref=src,
            dst_ref=dst,
            send_sem=self.ssem.at[n],
            recv_sem=self.rsem.at[n],
            device_id=device,
            device_id_type=pl.DeviceIdType.MESH,
        )

    def rows(self, ref, start, size):
        return ref.at[pl.ds(pl.multiple_of(start, 16), size)]

    def base_half(self, core):
        return core * self.half

    def base_group(self, chip):
        return self.core * self.half + chip * self.group

    def base_piece(self, z):
        return self.base_group(self.chip) + (z * self.piece if self.zsplit else 0)

    def core_copy(self, ref, dst, n, gather):
        side = self.core if gather else 1 - self.core
        src = self.rows(ref, self.base_half(side), self.half)
        dst = src if dst is None else dst
        return [self.copy(src, dst, {"rows": self.chip * 2 + 1 - self.core}, n)]

    def chip_copies(self, ref, dst, n, gather):
        out = []
        for d in range(1, self.chips):
            to = lax.rem(self.chip + d, self.chips)
            src = self.rows(ref, self.base_group(self.chip if gather else to), self.group)
            to_ref = src if gather else dst.at[pl.ds((d - 1) * self.group, self.group)]
            out.append(self.copy(src, to_ref, {"rows": to * 2 + self.core}, n + d - 1))
        return out

    def img_copies(self, ref, dst, n, gather):
        out = []
        for d in range(1, self.imgs):
            to = lax.rem(self.z + d, self.imgs)
            src = self.rows(ref, self.base_piece(self.z if gather else to), self.piece)
            to_ref = src if gather else dst.at[pl.ds((d - 1) * self.piece, self.piece)]
            out.append(self.copy(src, to_ref, {"imgs": to}, n + d - 1))
        return out

    def start(self, copies):
        for c in copies:
            c.start()
        return copies

    def wait(self, copies):
        for c in copies:
            c.wait()

    def add(self, base, size, extra, count, stride, target):
        step = min(size, 64)
        while size % step:
            step -= 16

        @pl.loop(0, size // step)
        def _(i):
            at = pl.ds(pl.multiple_of(base + i * step, 16), step)
            total = self.buf[at, :].astype(f32)
            for d in range(count):
                total += extra[pl.ds(pl.multiple_of(d * stride + i * step, 16), step), :].astype(f32)
            target[at, :] = total.astype(bf16)

    def step(self, k):
        n2 = 1
        n3 = n2 + self.chips - 1
        n4 = n3 + self.imgs - 1
        n5 = n4 + self.imgs - 1
        n6 = n5 + self.chips - 1
        first = lambda: self.core_copy(self.buf, self.r1, 0, False)
        second = lambda: self.chip_copies(self.buf, self.r2, n2, False)
        third = lambda: self.img_copies(self.buf, self.r3, n3, False)
        fourth = lambda: self.img_copies(self.out, None, n4, True) if self.zsplit else []
        fifth = lambda: self.chip_copies(self.out, None, n5, True)
        sixth = lambda: self.core_copy(self.out, None, n6, True)
        if k == 0:
            self.start(first())
        elif k == 1:
            self.wait(first())
            self.add(self.base_half(self.core), self.half, self.r1, 1, 0, self.buf)
            self.start(second())
        elif k == 2:
            self.wait(second())
            self.add(
                self.base_group(self.chip), self.group, self.r2, self.chips - 1, self.group, self.buf
            )
            self.start(third())
        elif k == 3:
            self.wait(third())
            self.add(
                self.base_piece(self.z), self.piece, self.r3, self.imgs - 1, self.piece, self.out
            )
            self.start(fourth() if self.zsplit else fifth())
        elif k == 4:
            if self.zsplit:
                self.wait(fourth())
                self.start(fifth())
        elif k == 5:
            self.wait(fifth())
            self.start(sixth())
        elif k == 6:
            self.wait(sixth())


def all_reduce_sems(chips, imgs):
    return 2 * (1 + chips - 1 + imgs - 1)


def layer_kernel(
    chips,
    imgs,
    pieces,
    scal,
    img,
    cot,
    r_qkv,
    r_proj,
    r_fc1,
    r_fc2t,
    r_conv,
    r_table,
    r_n1g,
    r_n1b,
    r_qvb,
    r_pb,
    r_n2g,
    r_n2b,
    r_f1b,
    r_f2b,
    r_cb,
    res_out,
    ig_out,
    a_out,
    b_out,
    c_out,
    wqkv,
    wproj,
    wfc1,
    wfc2t,
    wconv,
    vecs,
    extra,
    d_qkv,
    d_proj,
    d_fc1,
    d_fc2,
    d_conv,
    d_norm,
    d_rel,
    io1,
    io2,
    xband,
    gband,
    gcat,
    llbuf,
    xhat1,
    normed,
    qkv,
    probs,
    mixed,
    winf,
    fgrad,
    do_buf,
    ig_rows,
    edge,
    tmp,
    a_buf,
    a_r1,
    a_r2,
    a_r3,
    b_buf,
    b_r1,
    b_r2,
    b_r3,
    c_buf,
    c_r1,
    c_r2,
    c_r3,
    lsem,
    hs,
    hr,
    a_s,
    a_r,
    b_s,
    b_r,
    c_s,
    c_r,
):
    stripes = 2 * chips
    rank = lax.axis_index("rows")
    core = lax.rem(rank, 2)
    up = lax.rem(rank + stripes - 1, stripes)
    down = lax.rem(rank + 1, stripes)
    pa, pb, pc = pieces
    ara = AllReduce(a_buf, a_out, a_r1, a_r2, a_r3, a_s, a_r, pa, chips, imgs, True)
    arb = AllReduce(b_buf, b_out, b_r1, b_r2, b_r3, b_s, b_r, pb, chips, imgs, False)
    arc = AllReduce(c_buf, c_out, c_r1, c_r2, c_r3, c_s, c_r, pc, chips, imgs, True)

    barrier = pltpu.get_barrier_semaphore()
    peers = [{"rows": up}, {"rows": down}]
    peers += [{"rows": lax.rem(rank + 2 * d, stripes)} for d in range(1, chips)]
    peers += [{"imgs": lax.rem(ara.z + d, imgs)} for d in range(1, imgs)]
    for peer in peers:
        pl.semaphore_signal(barrier, inc=1, device_id=peer, device_id_type=pl.DeviceIdType.MESH)
    pl.semaphore_wait(barrier, len(peers))

    def remote(src, dst, to, n):
        return pltpu.make_async_remote_copy(
            src_ref=src,
            dst_ref=dst,
            send_sem=hs.at[n],
            recv_sem=hr.at[n],
            device_id={"rows": to},
            device_id_type=pl.DeviceIdType.MESH,
        )

    send_img = remote(img.at[pl.ds(0, 4)], io2.at[pl.ds(16, 4)], up, 0)
    send_cot = remote(cot.at[pl.ds(0, 5)], io1.at[pl.ds(16, 5)], up, 1)
    send_cot.start()
    send_img.start()
    load_cot = pltpu.make_async_copy(cot, io1.at[pl.ds(0, 16)], lsem.at[0])
    load_img = pltpu.make_async_copy(img, io2.at[pl.ds(0, 16)], lsem.at[1])
    load_cot.start()
    load_img.start()

    nb = scal[0]
    width = nb * WIN
    is_last = rank == stripes - 1
    joined = jnp.where(is_last, 0.0, 1.0)
    NW = 256 // WIN
    RM = 256

    def vec(i, n):
        return vecs[i : i + 1, 0:n]

    def row_at(pos, count=1):
        return pl.ds(pl.multiple_of(pos * 256, 256), count * 256)

    tmp[...] = jnp.zeros_like(tmp)
    for ref in (d_qkv, d_proj, d_fc1, d_fc2, d_conv, d_norm, d_rel):
        ref[...] = jnp.zeros_like(ref)
    for ref, size in ((a_buf, A_USED), (b_buf, B_USED), (c_buf, C_USED)):
        if ref.shape[0] > size:
            ref[size:, :] = jnp.zeros((ref.shape[0] - size, 128), bf16)

    col_in = rows_of((256, C)) < width
    col_in_p = rows_of((256, CP)) < width

    def put_g(pos, row, flag):
        g = jnp.where(col_in, row.astype(f32), 0.0) * flag
        tmp[8:264, 0:C] = g
        at = row_at(pos)
        gcat[at, 0:CP] = tmp[9:265, :].astype(bf16)
        gcat[at, CP : 2 * CP] = tmp[8:264, :].astype(bf16)
        gcat[at, 2 * CP : 3 * CP] = tmp[7:263, :].astype(bf16)

    def iota(shape, dim):
        return lax.broadcasted_iota(jnp.int32, shape, dim)

    def padded(v):
        return jnp.concatenate([v.astype(f32), jnp.zeros((CR - C, v.shape[1]), f32)], axis=0).astype(bf16)

    for ref in (wqkv, wproj, wfc1, wfc2t, wconv, vecs):
        ref[...] = jnp.zeros_like(ref)
    part = iota((3 * C, 3 * CP), 1)
    lane = part & (CP - 1)
    place = (part >> 8) * C + (lane >> 5) * HEAD_DIM + (lane & 31)
    used = ((lane & 31) < HEAD_DIM) & (lane < HEADS * HP_DIM)
    spread = (used & (iota((3 * C, 3 * CP), 0) == place)).astype(bf16)
    wqkv[0:CR, :] = padded(dot(r_qkv[...], spread))
    lane = iota((CP, C), 0)
    place = (lane >> 5) * HEAD_DIM + (lane & 31)
    used = ((lane & 31) < HEAD_DIM) & (lane < HEADS * HP_DIM)
    wproj[:, 0:C] = dot((used & (iota((CP, C), 1) == place)).astype(bf16), r_proj[...]).astype(bf16)
    wfc1[0:CR, 0:HID] = padded(r_fc1[...])
    wfc2t[0:CR, 0:HID] = padded(r_fc2t[...])
    for a in range(3):
        for b in range(3):
            wconv[a, 0:CR, b * CP : b * CP + C] = padded(r_conv[a, b])
    for n, ref in ((0, r_n1g), (1, r_n1b), (3, r_pb), (4, r_n2g), (5, r_n2b), (6, r_f1b), (7, r_f2b), (8, r_cb)):
        vecs[n : n + 1, 0 : ref.shape[0]] = ref[...].reshape(1, ref.shape[0])
    for n in (1, 5, 7):
        vecs[n : n + 1, C : C + 1] = jnp.ones((1, 1), f32)
    qvb = r_qvb[...].reshape(1, 2 * C)
    for h in range(HEADS):
        at = h * HP_DIM
        vecs[2:3, at : at + HEAD_DIM] = qvb[:, h * HEAD_DIM : (h + 1) * HEAD_DIM]
        vecs[2:3, 2 * CP + at : 2 * CP + at + HEAD_DIM] = qvb[
            :, C + h * HEAD_DIM : C + (h + 1) * HEAD_DIM
        ]
    score_terms(r_table[...], extra)

    load_cot.wait()

    @pl.loop(0, 13)
    def _(r):
        put_g(r, io1[r + 3], 1.0)

    put_g(14, io1[15], joined)
    load_img.wait()

    pos_hi = rows_of((1, WIN, CP)) >= SHIFT

    def rolled(a, b):
        t = jnp.where(pos_hi, a, b)
        return pltpu.roll(t, SHIFT, 1)

    def to_win(ref, k):
        nxt = jnp.minimum(k + 1, NW - 1)
        a = ref[:, pl.ds(pl.multiple_of(k * WIN, WIN), WIN), :]
        b = ref[:, pl.ds(pl.multiple_of(nxt * WIN, WIN), WIN), :]
        b = jnp.where(k == nb - 1, ref[:, 0:WIN, :], b)
        return rolled(a, b).reshape(AREA, CP)

    def from_win(ref, band):
        def block(k):
            at = pl.multiple_of((band * NW + k) * AREA, AREA)
            return ref[pl.ds(at, AREA), :].reshape(WIN, WIN, CP)

        @pl.loop(0, NW, unroll=4)
        def _(k):
            b = block(k)
            edge[...] = jnp.where(k == nb - 1, b, edge[...])
            xband[:, pl.ds(pl.multiple_of(k * WIN, WIN), WIN), :] = rolled(
                block(jnp.maximum(k - 1, 0)), b
            )

        xband[:, 0:WIN, :] = rolled(edge[...], block(0))

    def win_rows(w):
        return pl.ds(pl.multiple_of(w * AREA, AREA), AREA)

    @pl.loop(0, 2)
    def _(band):
        @pl.when(band == 1)
        def _():
            send_cot.wait()
            send_img.wait()
            put_g(13, io1[16], joined)

            @pl.loop(0, 5)
            def _(r):
                put_g(15 + r, io1[16 + r], 1.0)

        xband[:, :, 128:256] = jnp.zeros((8, 256, 128), f32)

        @pl.loop(0, 8)
        def _(y):
            xband[y, :, 0:C] = io2[band * 8 + y + 4].astype(f32)

        @pl.loop(0, 8)
        def _(y):
            r = band * 8 + y
            pos = r + 1 + jnp.where(r >= 12, 2, 0)
            acc = None
            for a in range(3):
                d = dot(gcat[row_at(pos + 1 - a), :], wconv[a], 1, 1)
                acc = d if acc is None else acc + d
            gband[y] = jnp.where(col_in_p, acc, 0.0)

        @pl.loop(0, 4)
        def _(gg):
            g = band * 4 + gg
            k0 = gg * 8
            gs = pl.ds(pl.multiple_of(g * 512, 512), 512)

            xs = [to_win(xband, k0 + w) for w in range(8)]
            for w in range(8):
                winf[win_rows(gg * 8 + w), :] = xs[w]
                fgrad[win_rows(g * 8 + w), :] = to_win(gband, k0 + w)
                xhat, rs_, ln_out = ln_fwd(xs[w], vec(0, CP), vec(1, CP))
                xhat1[win_rows(g * 8 + w), :] = with_rstd(xhat, rs_).astype(bf16)
                normed[win_rows(g * 8 + w), :] = ln_out.astype(bf16)

            for n in range(3):
                sl = slice(n * CP, (n + 1) * CP)
                qkv[gs, sl] = (dot(normed[gs, :], wqkv[:, sl]) + vecs[2:3, sl]).astype(bf16)

            i = 0
            if True:
                which = jnp.where((band == 1) & is_last, 2, 0)
                jobs = []
                for w in range(8):
                    rs = win_rows(g * 8 + i * 8 + w)
                    edge_win = k0 + i * 8 + w == nb - 1
                    for n, (h0, count) in enumerate(GROUPS):
                        jobs.append((rs, w, edge_win, n, count, slice(h0 * AREA, (h0 + count) * AREA)))
                qs = [qkv[rs, n * 128 : (n + 1) * 128] for rs, w, ew, n, count, hl in jobs]
                ks = [qkv[rs, CP + n * 128 : CP + (n + 1) * 128] for rs, w, ew, n, count, hl in jobs]
                vs = [qkv[rs, 2 * CP + n * 128 : 2 * CP + (n + 1) * 128] for rs, w, ew, n, count, hl in jobs]
                ss = [dot(k, spread_heads(q, job[4]), 1, 1) for q, k, job in zip(qs, ks, jobs)]
                ps = []
                for s, (rs, w, ew, n, count, hl) in zip(ss, jobs):
                    more = jnp.where(ew, extra[which + 1, :, hl], extra[which, :, hl])
                    s = s * (SCALE * LOG2E) + more
                    top = jnp.max(s, axis=0, keepdims=True)
                    e = jnp.exp2(s - top)
                    total = jnp.sum(e, axis=0, keepdims=True)
                    ps.append((e * (1.0 / total)).astype(bf16))
                os = [gather_heads(dot(p, v, 0, 0), job[4]) for p, v, job in zip(ps, vs, jobs)]
                for p, o, (rs, w, ew, n, count, hl) in zip(ps, os, jobs):
                    probs[rs, hl] = p
                    if n == 0:
                        o = jnp.where(lanes((1, 128)) == HEAD_DIM, 1.0, o)
                    mixed[win_rows(i * 8 + w), n * 128 : (n + 1) * 128] = o.astype(bf16)

            parts = range(0, 512, 256)
            at_rows = [pl.ds(pl.multiple_of(g * 512 + r, 256), 256) for r in parts]
            in_band = [pl.ds(pl.multiple_of(gg * 512 + r, 256), 256) for r in parts]
            mixes = [mixed[r : r + 256, :] for r in parts]
            firsts = [dot(m, wproj[...]) + vec(3, CP) + winf[rs, :] for m, rs in zip(mixes, in_band)]

            def norm2(v):
                xhat, rs_, ln_out = ln_fwd(v, vec(4, CP), vec(5, CP))
                return xhat, rs_, ln_out.astype(bf16)

            def activate(v):
                ac, dg = gelu_pair(v + vec(6, HP))
                return jnp.where(lanes((1, HP)) == HID, 1.0, ac).astype(bf16), dg.astype(bf16)

            norms = [by_rows(norm2, 64, v) for v in firsts]
            n2s = [n[2] for n in norms]
            acts = [by_rows(activate, 64, dot(n2, wfc1[...])) for n2 in n2s]
            for fs, (ac, dg), rs in zip(firsts, acts, in_band):
                winf[rs, :] = fs + dot(ac, wfc2t[...], 1, 1) + vec(7, CP)
            lgs = [fgrad[rs, :] for rs in at_rows]
            mgs = [lg.astype(bf16) for lg in lgs]
            hgs = [
                (dot(mg, wfc2t[...]).astype(bf16).astype(f32) * dg.astype(f32)).astype(bf16)
                for mg, (ac, dg) in zip(mgs, acts)
            ]
            dns = [dot(hg, wfc1[...], 1, 1).astype(bf16) for hg in hgs]

            def back2(dn2, xh, rs_, lg):
                dn2 = dn2.astype(f32)
                fg = lg + ln_bwd(dn2, xh, rs_, vec(4, CP))
                return fg, fg.astype(bf16), fold8(dn2 * xh), fold8(dn2)

            backs = [
                by_rows(back2, 64, dn, n[0], n[1], lg) for dn, n, lg in zip(dns, norms, lgs)
            ]
            ats = [b[1] for b in backs]
            for b, rs in zip(backs, at_rows):
                fgrad[rs, :] = b[0]
                do_buf[rs, :] = dot(b[1], wproj[...], 1, 1).astype(bf16)
            d_norm[0:8, :] += added([fold8(b[2]) for b in backs])
            d_norm[8:16, :] += added([fold8(b[3]) for b in backs])
            join = lambda vs: jnp.concatenate(vs, axis=0)
            mg = join(mgs)
            d_fc2[...] += dot(mg[:, 0:CR], join([ac for ac, dg in acts]), 0, 0)
            d_norm[32:40, :] += fold8(mg.astype(f32))
            d_fc1[...] += dot(join(n2s)[:, 0:CR], join(hgs), 0, 0)
            d_proj[...] += dot(mixed[:, 0:CR], join(ats), 0, 0)

        from_win(winf, 0)

        @pl.loop(0, 8)
        def _(y):
            r = band * 8 + y
            pos = r + 1 + jnp.where(r >= 12, 2, 0)
            llbuf[row_at(pos), :] = jnp.where(col_in_p, xband[y], 0.0).astype(bf16)

    send_up = remote(llbuf.at[pl.ds(256, 256)], llbuf.at[pl.ds(19 * 256, 256)], up, 2)
    send_down = remote(llbuf.at[pl.ds(18 * 256, 256)], llbuf.at[pl.ds(0, 256)], down, 3)
    send_up.start()
    send_down.start()
    joined_low = joined.astype(bf16)
    llbuf[13 * 256 : 14 * 256, :] = llbuf[15 * 256 : 16 * 256, :] * joined_low
    llbuf[14 * 256 : 15 * 256, :] = llbuf[12 * 256 : 13 * 256, :] * joined_low

    def wgrad_rows(n):
        start = 1 + 4 * n + jnp.where(n == 3, 2, 0)
        gs = gcat[row_at(start, 4), :]
        for a in range(3):
            d_conv[a] += dot(llbuf[row_at(start + a - 1, 4), 0:CR], gs, 0, 0)

    low_lanes = lanes((1, 128)) < 64

    def mix(p, q):
        return jnp.where(low_lanes, p, pltpu.roll(q, 64, 1)).astype(bf16)

    a_buf[0:CR, :] = d_fc1[:, CP:HP].astype(bf16)
    for n in range(3):
        a_buf[(n + 1) * CR : (n + 2) * CR, :] = d_fc2[:, n * 128 : (n + 1) * 128].astype(bf16)
    a_buf[4 * CR : 5 * CR, :] = d_proj[:, 0:128].astype(bf16)
    ara.step(0)

    @pl.loop(1, 3)
    def _(n):
        wgrad_rows(n)

    send_up.wait()
    send_down.wait()
    ara.step(1)

    @pl.loop(0, 2)
    def _(n):
        wgrad_rows(n * 3)

    tails = []
    for a in range(3):
        for b in range(3):
            at = (a * 3 + b) * CR
            c_buf[at : at + CR, :] = d_conv[a, :, b * CP : b * CP + 128].astype(bf16)
            tails.append((d_conv, a, slice(b * CP + 128, (b + 1) * CP)))
    tails = [ref[a, :, ln] for ref, a, ln in tails] + [d_proj[:, 128:256]]
    for n in range(5):
        at = C_MIX + n * CR
        c_buf[at : at + CR, :] = mix(tails[2 * n], tails[2 * n + 1])
    for n in range(2):
        at = C_FC1 + n * CR
        c_buf[at : at + CR, :] = d_fc1[:, n * 128 : (n + 1) * 128].astype(bf16)
    arc.step(0)

    def conv_rows(lo, hi):
        @pl.loop(lo, hi)
        def _(r):
            pos = r + 1 + jnp.where(r >= 12, 2, 0)
            acc = None
            for a in range(3):
                d = dot(llbuf[row_at(pos + a - 1), :], wconv[a])
                acc = d if acc is None else acc + d
            tmp[8:264, :] = acc[:, 0:CP]
            tmp[280:536, :] = acc[:, 2 * CP : 3 * CP]
            out = acc[:, CP : 2 * CP] + tmp[7:263, :] + tmp[281:537, :] + vec(8, CP)
            out = out[:, 0:C] + io2[r + 4].astype(f32)
            io1[r] = jnp.where(col_in, out, 0.0).astype(bf16)

    def grad_rows(band):
        from_win(fgrad, band)

        @pl.loop(0, 8)
        def _(y):
            r = band * 8 + y
            pos = r + 1 + jnp.where(r >= 12, 2, 0)
            v = xband[y] + gcat[row_at(pos), CP : 2 * CP].astype(f32)
            ig_rows[r] = jnp.where(col_in_p, v, 0.0)[:, 0:C].astype(bf16)

    conv_rows(12, 16)
    send_res = remote(io1.at[pl.ds(12, 4)], res_out.at[pl.ds(0, 4)], down, 4)
    send_res.start()
    send_ig = remote(ig_rows.at[pl.ds(12, 4)], ig_out.at[pl.ds(0, 4)], down, 5)

    @pl.loop(0, 8)
    def _(turn):
        g = lax.rem(turn + 4, 8)
        gs = pl.ds(pl.multiple_of(g * 512, 512), 512)

        i = 0
        if True:
            jobs = []
            for w in range(8):
                rs = win_rows(g * 8 + i * 8 + w)
                for n, (h0, count) in enumerate(GROUPS):
                    jobs.append((rs, n, count, slice(h0 * AREA, (h0 + count) * AREA)))
            qs = [qkv[rs, n * 128 : (n + 1) * 128] for rs, n, count, hl in jobs]
            ks = [qkv[rs, CP + n * 128 : CP + (n + 1) * 128] for rs, n, count, hl in jobs]
            vs = [qkv[rs, 2 * CP + n * 128 : 2 * CP + (n + 1) * 128] for rs, n, count, hl in jobs]
            dos = [spread_heads(do_buf[rs, n * 128 : (n + 1) * 128], count) for rs, n, count, hl in jobs]
            pbs = [probs[rs, hl] for rs, n, count, hl in jobs]
            dps = [dot(v, d, 1, 1) for v, d in zip(vs, dos)]
            dvs = [dot(p, d) for p, d in zip(pbs, dos)]
            dss = []
            for dp, pb in zip(dps, pbs):
                p = pb.astype(f32)
                dss.append((p * (dp - jnp.sum(p * dp, axis=0, keepdims=True))).astype(bf16))
            dks = [dot(ds, spread_heads(q, job[2])) * SCALE for ds, q, job in zip(dss, qs, jobs)]
            dqs = [gather_heads(dot(ds, k, 0, 0), job[2]) * SCALE for ds, k, job in zip(dss, ks, jobs)]
            for n, (h0, count) in enumerate(GROUPS):
                hl = slice(h0 * AREA, (h0 + count) * AREA)
                d_rel[:, hl] += functools.reduce(jnp.add, [d.astype(f32) for d in dss[n::2]])
            for dq, dk, dv, (rs, n, count, hl) in zip(dqs, dks, dvs, jobs):
                qkv[rs, n * 128 : (n + 1) * 128] = dq.astype(bf16)
                qkv[rs, CP + n * 128 : CP + (n + 1) * 128] = dk.astype(bf16)
                qkv[rs, 2 * CP + n * 128 : 2 * CP + (n + 1) * 128] = dv.astype(bf16)

        d_qkv[...] += dot(normed[gs, 0:CR], qkv[gs, :], 0, 0)

        dn1 = dot(qkv[gs, :], wqkv[...], 1, 1).astype(bf16)

        def back1(dn, xhat, fg):
            dn, xhat = dn.astype(f32), xhat.astype(f32)
            out = fg + ln_bwd(dn, xhat, xhat[:, 200:201] + xhat[:, 201:202], vec(0, CP))
            return out, fold8(dn * xhat), fold8(dn)

        back = by_rows(back1, 64, dn1, xhat1[gs, :], fgrad[gs, :])
        fgrad[gs, :] = back[0]
        d_norm[16:24, :] += fold8(back[1])
        d_norm[24:32, :] += fold8(back[2])

        for at, steps in TURNS:

            @pl.when(turn == at)
            def _(steps=steps):
                for which, k in steps:
                    {"a": ara, "c": arc}[which].step(k)

        @pl.when(turn == 3)
        def _():
            grad_rows(1)
            send_ig.start()

    for n in range(3):
        b_buf[n * CR : (n + 1) * CR, :] = d_qkv[:, n * CP : n * CP + 128].astype(bf16)
    b_buf[3 * CR : 4 * CR, :] = mix(d_qkv[:, 128:256], d_qkv[:, CP + 128 : 2 * CP])
    b_buf[4 * CR : 5 * CR, :] = mix(d_qkv[:, 2 * CP + 128 : 3 * CP], d_qkv[:, 2 * CP + 128 : 3 * CP])
    sums = jnp.sum(d_norm[...].reshape(5, 8, CP), axis=1)
    small = jnp.concatenate([table_sum(d_rel[...]), sums, jnp.zeros((3, CP), f32)], axis=0)
    b_buf[B_SMALL : B_SMALL + 16, :] = small[:, 0:128].astype(bf16)
    b_buf[B_SMALL + 16 : B_SMALL + 32, :] = small[:, 128:256].astype(bf16)
    arb.step(0)
    ara.step(5)
    arc.step(3)
    conv_rows(0, 4)
    arb.step(1)
    ara.step(6)
    conv_rows(4, 8)
    arc.step(4)
    conv_rows(8, 12)
    store_res = pltpu.make_async_copy(io1.at[pl.ds(0, 12)], res_out.at[pl.ds(4, 12)], lsem.at[2])
    store_res.start()
    arb.step(2)
    grad_rows(0)
    store_ig = pltpu.make_async_copy(ig_rows.at[pl.ds(0, 12)], ig_out.at[pl.ds(4, 12)], lsem.at[3])
    store_ig.start()
    arb.step(3)
    arc.step(5)
    arb.step(5)
    arc.step(6)
    arb.step(6)
    send_res.wait()
    send_ig.wait()
    store_res.wait()
    store_ig.wait()


def finish_kernel(
    a_ref, b_ref, c_ref, o_n1g, o_n1b, o_qkv, o_qvb, o_table, o_proj, o_pb, o_n2g, o_n2b, o_fc1, o_f1b, o_fc2t,
    o_f2b, o_conv, o_cb,
):
    def block(ref, at, rows=CR):
        return ref[at : at + rows, :].astype(f32)

    def halves(v):
        return v, pltpu.roll(v, 64, 1)

    tails = []
    for n in range(5):
        tails += halves(block(c_ref, C_MIX + n * CR))
    for a in range(3):
        for b in range(3):
            v = jnp.concatenate([block(c_ref, (a * 3 + b) * CR), tails[a * 3 + b]], axis=1)
            o_conv[a, b] = v[0:C, 0:C]
            if a == 1 and b == 1:
                o_cb[...] = v[C : C + 1, 0:C].reshape(C)
    fc1 = [block(c_ref, C_FC1), block(c_ref, C_FC1 + CR), block(a_ref, 0)]
    fc1 = jnp.concatenate(fc1, axis=1)
    o_fc1[...] = fc1[0:C, 0:HID]
    o_f1b[...] = fc1[C : C + 1, 0:HID].reshape(HID)
    fc2 = jnp.concatenate([block(a_ref, (n + 1) * CR) for n in range(3)], axis=1)
    o_fc2t[...] = fc2[0:C, 0:HID]
    proj = jnp.concatenate([block(a_ref, 4 * CR), tails[9]], axis=1)
    for h in range(HEADS):
        at = h * HP_DIM
        o_proj[h * HEAD_DIM : (h + 1) * HEAD_DIM, :] = proj[at : at + HEAD_DIM, 0:C]
    o_pb[...] = proj[HEAD_DIM : HEAD_DIM + 1, 0:C].reshape(C)
    wide = lax.broadcasted_iota(jnp.int32, (CP, CP), 0)
    dense = lax.broadcasted_iota(jnp.int32, (CP, CP), 1)
    heads_out = (wide == dense + lax.div(dense, HEAD_DIM) * (HP_DIM - HEAD_DIM)) & (dense < C)
    heads_out = heads_out.astype(bf16)
    rest = halves(block(b_ref, 3 * CR)) + halves(block(b_ref, 4 * CR))
    for n in range(3):
        v = jnp.concatenate([block(b_ref, n * CR), rest[n]], axis=1).astype(bf16)
        v = dot(v, heads_out)
        o_qkv[:, n * C : (n + 1) * C] = v[0:C, 0:C]
        if n != 1:
            o_qvb[n // 2 * C : (n // 2 + 1) * C] = v[C : C + 1, 0:C].reshape(C)
    small = jnp.concatenate([block(b_ref, B_SMALL, 16), block(b_ref, B_SMALL + 16, 16)], axis=1)
    o_table[...] = small[0:HEADS, 0 : o_table.shape[1]]
    for n, ref in ((8, o_n2g), (9, o_n2b), (10, o_n1g), (11, o_n1b), (12, o_f2b)):
        ref[...] = small[n : n + 1, 0:C].reshape(C)


def score_terms(table, extra):
    table = jnp.concatenate([table * LOG2E, jnp.zeros((2, table.shape[1]), f32)], axis=0)
    table = jnp.concatenate([table, jnp.zeros((8, CP - table.shape[1]), f32)], axis=1)
    shifted = [pltpu.roll(table, x, 1) if x else table for x in range(WIN)]
    row = lax.broadcasted_iota(jnp.int32, (AREA, CP), 0)
    lane = lax.broadcasted_iota(jnp.int32, (AREA, CP), 1)
    put = (lane == row + (row >> 3) * (WIN - 1)).astype(bf16)
    shape = (AREA, AREA)
    j = lax.broadcasted_iota(jnp.int32, shape, 0)
    i = lax.broadcasted_iota(jnp.int32, shape, 1)
    rows_differ = ((j >> 5) & 1) != ((i >> 5) & 1)
    cols_differ = ((j >> 2) & 1) != ((i >> 2) & 1)
    masks = [None, cols_differ, rows_differ, rows_differ | cols_differ]
    for h in range(HEADS):
        base = jnp.concatenate([t[h : h + 1] for t in shifted], axis=0)
        wide = jnp.concatenate(
            [pltpu.roll(base, CP - (112 - 15 * y), 1) for y in range(WIN)], axis=0
        )
        high = wide.astype(bf16)
        rest = wide - high.astype(f32)
        mid = rest.astype(bf16)
        low = (rest - mid.astype(f32)).astype(bf16)
        term = dot(high, put, 1, 1) + dot(mid, put, 1, 1) + dot(low, put, 1, 1)
        for n, mask in enumerate(masks):
            value = term if mask is None else term + jnp.where(mask, -100.0 * LOG2E, 0.0)
            extra[n, :, h * AREA : (h + 1) * AREA] = value


def table_sum(d_rel):
    row = lax.broadcasted_iota(jnp.int32, (AREA, CP), 0)
    lane = lax.broadcasted_iota(jnp.int32, (AREA, CP), 1)
    put = (lane == row + lax.div(row, WIN) * (WIN - 1)).astype(bf16)
    heads = []
    for h in range(HEADS):
        v = d_rel[:, h * AREA : (h + 1) * AREA]
        v1 = v.astype(bf16)
        v2 = (v - v1.astype(f32)).astype(bf16)
        wide = dot(v1, put) + dot(v2, put)
        total = None
        for y in range(WIN):
            part = pltpu.roll(wide[y * WIN : (y + 1) * WIN, :], 112 - 15 * y, 1)
            total = part if total is None else total + part
        heads.append(total)
    out = None
    for x in range(WIN):
        rows = jnp.concatenate([t[x : x + 1] for t in heads] + [jnp.zeros((2, CP), f32)], axis=0)
        rows = pltpu.roll(rows, CP - x, 1) if x else rows
        out = rows if out is None else out + rows
    return out


VM = pl.BlockSpec(memory_space=pltpu.VMEM)
SM = pl.BlockSpec(memory_space=pltpu.SMEM)
HB = pl.BlockSpec(memory_space=pl.ANY)


def up_to(n, m):
    return (n + m - 1) // m * m


def run_layer(stripes, imgs, *operands):
    S = jax.ShapeDtypeStruct
    V = pltpu.VMEM
    chips = stripes // 2
    dma = pltpu.SemaphoreType.DMA
    sems = 2 * (chips + imgs - 1)
    pieces, buffers, outs = [], [], []
    for used, zsplit in ((A_USED, True), (B_USED, False), (C_USED, True)):
        parts = stripes * imgs if zsplit else stripes
        piece = up_to(-(-used // parts), 16)
        group = piece * imgs if zsplit else piece
        pieces.append(piece)
        outs.append(S((stripes * group, 128), bf16))
        buffers += [
            V((stripes * group, 128), bf16),
            V((chips * group, 128), bf16),
            V(((chips - 1) * group, 128), bf16),
            V(((imgs - 1) * piece, 128), bf16),
        ]
    return pl.pallas_call(
        functools.partial(layer_kernel, chips, imgs, tuple(pieces)),
        out_shape=(S((16, 256, C), bf16), S((16, 256, C), bf16), *outs),
        in_specs=[SM, HB, HB] + [VM] * 15,
        out_specs=[HB] * 2 + [VM] * 3,
        scratch_shapes=[
            V((CP, 3 * CP), bf16),
            V((CP, CP), bf16),
            V((CP, HP), bf16),
            V((CP, HP), bf16),
            V((3, CP, 3 * CP), bf16),
            V((16, 3 * CP), f32),
            V((4, AREA, HI), f32),
            V((CR, 3 * CP), f32),
            V((CR, CP), f32),
            V((CR, HP), f32),
            V((CR, HP), f32),
            V((3, CR, 3 * CP), f32),
            V((40, CP), f32),
            V((AREA, HI), f32),
            V((21, 256, C), bf16),
            V((20, 256, C), bf16),
            V((8, 256, CP), f32),
            V((8, 256, CP), f32),
            V((20 * 256, 3 * CP), bf16),
            V((20 * 256, CP), bf16),
            V((4096, CP), bf16),
            V((4096, CP), bf16),
            V((4096, 3 * CP), bf16),
            V((4096, HI), bf16),
            V((512, CP), bf16),
            V((2048, CP), f32),
            V((4096, CP), f32),
            V((4096, CP), bf16),
            V((16, 256, C), bf16),
            V((WIN, WIN, CP), f32),
            V((544, CP), f32),
            *buffers,
            dma((4,)),
            dma((6,)),
            dma((6,)),
        ]
        + [dma((sems,))] * 6,
        compiler_params=pltpu.CompilerParams(
            vmem_limit_bytes=63 * 1024 * 1024, collective_id=0, has_side_effects=True
        ),
        name="layer",
    )(*operands)


def run_finish(a, b, c, table):
    S = jax.ShapeDtypeStruct
    return pl.pallas_call(
        finish_kernel,
        out_shape=(
            S((C,), f32),
            S((C,), f32),
            S((C, 3 * C), f32),
            S((2 * C,), f32),
            S((HEADS, table), f32),
            S((C, C), f32),
            S((C,), f32),
            S((C,), f32),
            S((C,), f32),
            S((C, HID), f32),
            S((HID,), f32),
            S((C, HID), f32),
            S((C,), f32),
            S((3, 3, C, C), f32),
            S((C,), f32),
        ),
        compiler_params=pltpu.CompilerParams(vmem_limit_bytes=32 * 1024 * 1024),
        name="finish",
    )(a, b, c)


def on_device(
    images, widths, norm1_gain, norm1_bias, qkv_weight, qv_bias, bias_table, proj_weight, proj_bias,
    norm2_gain, norm2_bias, fc1_weight, fc1_bias, fc2_weight, fc2_bias, conv_weight, conv_bias, cotangent,
):
    count, rows_here, width, chans = images.shape
    img = images.reshape(rows_here, width, chans)
    cot = cotangent.reshape(rows_here, width, chans)
    scal = lax.div(widths, WIN)
    res, ig, a, b, c = run_layer(
        lax.axis_size("rows"), lax.axis_size("imgs"),
        scal, img, cot, qkv_weight, proj_weight, fc1_weight, fc2_weight.T, conv_weight, bias_table.T,
        norm1_gain, norm1_bias, qv_bias, proj_bias, norm2_gain, norm2_bias, fc1_bias, fc2_bias, conv_bias,
    )
    grads = list(run_finish(a, b, c, bias_table.shape[0]))
    grads[4] = grads[4].T
    grads[11] = grads[11].T
    return (res[None], ig[None], *grads)


def solution(mesh):
    big = P("imgs", "rows", None, None)
    in_specs = (big, P("imgs")) + (P(),) * 15 + (big,)
    out_specs = (big, big) + (P(),) * 15
    return jax.shard_map(
        on_device, mesh=mesh, in_specs=in_specs, out_specs=out_specs, check_vma=False
    )
```

```python
import functools

import jax
import jax.numpy as jnp
import numpy as np
from jax import lax
from jax.experimental import pallas as pl
from jax.experimental.pallas import tpu as pltpu
from jax.sharding import PartitionSpec as P

HEADS = 6
HEAD_DIM = 30
WIN = 8
SHIFT = 4
C = 180
CP = 256
HID = 360
HP = 384
AREA = WIN * WIN
HI = HEADS * AREA
LOG2E = 1.4426950408889634
SCALE = HEAD_DIM ** (-0.5)

CR = 192
A_USED = 5 * CR
B_SMALL = 5 * CR
B_USED = B_SMALL + 32
C_MIX = 9 * CR
C_FC1 = C_MIX + 5 * CR
C_USED = C_FC1 + 2 * CR

f32 = jnp.float32
bf16 = jnp.bfloat16


def dot(a, b, ca=1, cb=0):
    return lax.dot_general(a, b, (((ca,), (cb,)), ((), ())), preferred_element_type=f32)


def lanes(shape):
    return lax.broadcasted_iota(jnp.int32, shape, len(shape) - 1)


def rows_of(shape):
    return lax.broadcasted_iota(jnp.int32, shape, len(shape) - 2)


def ln_fwd(x, gain, bias):
    real = (lanes((1, CP)) < C).astype(f32)
    mean = jnp.sum(x, axis=-1, keepdims=True) * (1.0 / C)
    xc = (x - mean) * real
    var = jnp.sum(xc * xc, axis=-1, keepdims=True) * (1.0 / C)
    rstd = lax.rsqrt(var + 1e-05)
    xhat = xc * rstd
    return xhat, rstd, xhat * gain + bias


def with_rstd(xhat, rstd):
    high = rstd.astype(bf16).astype(f32)
    lane = lanes((1, CP))
    return jnp.where(lane == 200, high, jnp.where(lane == 201, rstd - high, xhat))


def ln_bwd(dy, xhat, rstd, gain):
    a = dy * gain
    m1 = jnp.sum(a, axis=-1, keepdims=True) * (1.0 / C)
    m2 = jnp.sum(a * xhat, axis=-1, keepdims=True) * (1.0 / C)
    return rstd * (a - m1 - xhat * m2)


def gelu_pair(h):
    z = jnp.abs(h) * 0.7071067811865476
    d = 1.0 + 0.3275911 * z
    t = pl.reciprocal(d, approx=True)
    t = t * (2.0 - d * t)
    e = jnp.exp2(h * h * (-0.5 * LOG2E))
    poly = t * (
        0.254829592 + t * (-0.284496736 + t * (1.421413741 + t * (-1.453152027 + t * 1.061405429)))
    )
    q = 0.5 * poly * e
    phi = jnp.where(h >= 0, 1.0 - q, q)
    return h * phi, phi + h * (e * 0.3989422804014327)


def fold8(v):
    return jnp.sum(v.reshape(v.shape[0] // 8, 8, v.shape[1]), axis=0)


HP_DIM = 32


def by_rows(f, step, *arrays):
    rows = arrays[0].shape[0]
    parts = [f(*[a[i : i + step] for a in arrays]) for i in range(0, rows, step)]
    if not isinstance(parts[0], tuple):
        return jnp.concatenate(parts, axis=0)
    return tuple(jnp.concatenate(p, axis=0) for p in zip(*parts))


def added(values):
    return functools.reduce(jnp.add, values)


def head_mask(h):
    ln = lanes((1, 128))
    return (ln >= h * HP_DIM) & (ln < (h + 1) * HP_DIM)


def spread_heads(v, count):
    return jnp.concatenate(
        [jnp.where(head_mask(h), v, jnp.zeros_like(v)) for h in range(count)], axis=0
    )


def gather_heads(v, count):
    out = jnp.where(head_mask(0), v[:AREA], 0.0)
    for h in range(1, count):
        out = jnp.where(head_mask(h), v[h * AREA : (h + 1) * AREA], out)
    return out


GROUPS = ((0, 4), (4, 2))


def column_masks(width):
    return rows_of((256, CP)) < width


class SmallAllReduce:
    def __init__(self, sums, slots, ssem, rsem, chips, imgs):
        self.sums, self.ssem, self.rsem = [sums.at[n] for n in range(4)], ssem, rsem
        rows, z = lax.axis_index("rows"), lax.axis_index("imgs")
        core, chip = lax.rem(rows, 2), lax.div(rows, 2)
        self.stages = [
            [{"rows": chip * 2 + 1 - core}],
            [{"rows": lax.rem(chip + d, chips) * 2 + core} for d in range(1, chips)],
            [{"imgs": lax.rem(z + d, imgs)} for d in range(1, imgs)],
        ]
        self.first = [0, 1, chips]
        self.slots = slots

    def copies(self, n):
        return [
            pltpu.make_async_remote_copy(
                src_ref=self.sums[n],
                dst_ref=self.slots.at[self.first[n] + d],
                send_sem=self.ssem.at[self.first[n] + d],
                recv_sem=self.rsem.at[self.first[n] + d],
                device_id=to,
                device_id_type=pl.DeviceIdType.MESH,
            )
            for d, to in enumerate(self.stages[n])
        ]

    def begin(self, value):
        self.sums[0][...] = value
        for c in self.copies(0):
            c.start()

    def step(self, n):
        value = self.sums[n][...]
        for d, c in enumerate(self.copies(n)):
            c.wait()
            value += self.slots[self.first[n] + d]
        self.sums[n + 1][...] = value
        if n < 2:
            for c in self.copies(n + 1):
                c.start()


TURNS = ((1, (("a", 2), ("c", 1))), (5, (("a", 3),)), (7, (("c", 2),)))


class AllReduce:
    def __init__(self, buf, out, r1, r2, r3, ssem, rsem, pr, chips, imgs, zsplit):
        self.buf, self.out, self.r1, self.r2, self.r3 = buf, out, r1, r2, r3
        self.ssem, self.rsem, self.chips, self.imgs = ssem, rsem, chips, imgs
        self.zsplit = zsplit
        rows = lax.axis_index("rows")
        self.core = lax.rem(rows, 2)
        self.chip = lax.div(rows, 2)
        self.z = lax.axis_index("imgs")
        self.piece = pr
        self.group = pr * imgs if zsplit else pr
        self.half = self.group * chips
        self.used = 0

    def copy(self, src, dst, device, n):
        return pltpu.make_async_remote_copy(
            src_ref=src,
            dst_ref=dst,
            send_sem=self.ssem.at[n],
            recv_sem=self.rsem.at[n],
            device_id=device,
            device_id_type=pl.DeviceIdType.MESH,
        )

    def rows(self, ref, start, size):
        return ref.at[pl.ds(pl.multiple_of(start, 16), size)]

    def base_half(self, core):
        return core * self.half

    def base_group(self, chip):
        return self.core * self.half + chip * self.group

    def base_piece(self, z):
        return self.base_group(self.chip) + (z * self.piece if self.zsplit else 0)

    def core_copy(self, ref, dst, n, gather):
        side = self.core if gather else 1 - self.core
        src = self.rows(ref, self.base_half(side), self.half)
        dst = src if dst is None else dst
        return [self.copy(src, dst, {"rows": self.chip * 2 + 1 - self.core}, n)]

    def chip_copies(self, ref, dst, n, gather):
        out = []
        for d in range(1, self.chips):
            to = lax.rem(self.chip + d, self.chips)
            src = self.rows(ref, self.base_group(self.chip if gather else to), self.group)
            to_ref = src if gather else dst.at[pl.ds((d - 1) * self.group, self.group)]
            out.append(self.copy(src, to_ref, {"rows": to * 2 + self.core}, n + d - 1))
        return out

    def img_copies(self, ref, dst, n, gather):
        out = []
        for d in range(1, self.imgs):
            to = lax.rem(self.z + d, self.imgs)
            src = self.rows(ref, self.base_piece(self.z if gather else to), self.piece)
            to_ref = src if gather else dst.at[pl.ds((d - 1) * self.piece, self.piece)]
            out.append(self.copy(src, to_ref, {"imgs": to}, n + d - 1))
        return out

    def start(self, copies):
        for c in copies:
            c.start()
        return copies

    def wait(self, copies):
        for c in copies:
            c.wait()

    def add(self, base, size, extra, count, stride, target):
        step = min(size, 64)
        while size % step:
            step -= 16

        @pl.loop(0, size // step)
        def _(i):
            at = pl.ds(pl.multiple_of(base + i * step, 16), step)
            total = self.buf[at, :].astype(f32)
            for d in range(count):
                total += extra[pl.ds(pl.multiple_of(d * stride + i * step, 16), step), :].astype(f32)
            target[at, :] = total.astype(bf16)

    def step(self, k):
        n2 = 1
        n3 = n2 + self.chips - 1
        n4 = n3 + self.imgs - 1
        n5 = n4 + self.imgs - 1
        n6 = n5 + self.chips - 1
        first = lambda: self.core_copy(self.buf, self.r1, 0, False)
        second = lambda: self.chip_copies(self.buf, self.r2, n2, False)
        third = lambda: self.img_copies(self.buf, self.r3, n3, False)
        fourth = lambda: self.img_copies(self.out, None, n4, True) if self.zsplit else []
        fifth = lambda: self.chip_copies(self.out, None, n5, True)
        sixth = lambda: self.core_copy(self.out, None, n6, True)
        if k == 0:
            self.start(first())
        elif k == 1:
            self.wait(first())
            self.add(self.base_half(self.core), self.half, self.r1, 1, 0, self.buf)
            self.start(second())
        elif k == 2:
            self.wait(second())
            self.add(
                self.base_group(self.chip), self.group, self.r2, self.chips - 1, self.group, self.buf
            )
            self.start(third())
        elif k == 3:
            self.wait(third())
            self.add(
                self.base_piece(self.z), self.piece, self.r3, self.imgs - 1, self.piece, self.out
            )
            self.start(fourth() if self.zsplit else fifth())
        elif k == 4:
            if self.zsplit:
                self.wait(fourth())
                self.start(fifth())
        elif k == 5:
            self.wait(fifth())
            self.start(sixth())
        elif k == 6:
            self.wait(sixth())


def all_reduce_sems(chips, imgs):
    return 2 * (1 + chips - 1 + imgs - 1)


def layer_kernel(
    chips,
    imgs,
    pieces,
    scal,
    img,
    cot,
    r_qkv,
    r_proj,
    r_fc1,
    r_fc2t,
    r_conv,
    r_table,
    r_n1g,
    r_n1b,
    r_qvb,
    r_pb,
    r_n2g,
    r_n2b,
    r_f1b,
    r_f2b,
    r_cb,
    res_out,
    ig_out,
    a_out,
    b_out,
    c_out,
    d_out,
    wqkv,
    wproj,
    wfc1,
    wfc2t,
    wconv,
    vecs,
    extra,
    d_qkv,
    d_proj,
    d_fc1,
    d_fc2,
    d_conv,
    d_norm,
    d_rel,
    io1,
    io2,
    xband,
    gband,
    gcat,
    llbuf,
    xhat1,
    normed,
    qkv,
    probs,
    mixed,
    winf,
    fgrad,
    do_buf,
    ig_rows,
    edge,
    tmp,
    a_buf,
    a_r1,
    a_r2,
    a_r3,
    b_buf,
    b_r1,
    b_r2,
    b_r3,
    c_buf,
    c_r1,
    c_r2,
    c_r3,
    dd_sums,
    dd_slots,
    lsem,
    hs,
    hr,
    a_s,
    a_r,
    b_s,
    b_r,
    c_s,
    c_r,
    dd_s,
    dd_r,
):
    stripes = 2 * chips
    rank = lax.axis_index("rows")
    core = lax.rem(rank, 2)
    up = lax.rem(rank + stripes - 1, stripes)
    down = lax.rem(rank + 1, stripes)
    pa, pb, pc = pieces
    ara = AllReduce(a_buf, a_out, a_r1, a_r2, a_r3, a_s, a_r, pa, chips, imgs, True)
    arb = AllReduce(b_buf, b_out, b_r1, b_r2, b_r3, b_s, b_r, pb, chips, imgs, False)
    arc = AllReduce(c_buf, c_out, c_r1, c_r2, c_r3, c_s, c_r, pc, chips, imgs, True)

    ard = SmallAllReduce(dd_sums, dd_slots, dd_s, dd_r, chips, imgs)

    load_cot = pltpu.make_async_copy(cot, io1.at[pl.ds(0, 16)], lsem.at[0])
    load_img = pltpu.make_async_copy(img, io2.at[pl.ds(0, 16)], lsem.at[1])
    load_cot.start()
    load_img.start()

    barrier = pltpu.get_barrier_semaphore()
    peers = [{"rows": up}, {"rows": down}]
    peers += [{"rows": lax.rem(rank + 2 * d, stripes)} for d in range(1, chips)]
    peers += [{"imgs": lax.rem(ara.z + d, imgs)} for d in range(1, imgs)]
    for peer in peers:
        pl.semaphore_signal(barrier, inc=1, device_id=peer, device_id_type=pl.DeviceIdType.MESH)

    def remote(src, dst, to, n):
        return pltpu.make_async_remote_copy(
            src_ref=src,
            dst_ref=dst,
            send_sem=hs.at[n],
            recv_sem=hr.at[n],
            device_id={"rows": to},
            device_id_type=pl.DeviceIdType.MESH,
        )

    send_img = remote(img.at[pl.ds(0, 4)], io2.at[pl.ds(16, 4)], up, 0)
    send_cot = remote(cot.at[pl.ds(0, 5)], io1.at[pl.ds(16, 5)], up, 1)
    nb = scal[0]
    width = nb * WIN
    is_last = rank == stripes - 1
    joined = jnp.where(is_last, 0.0, 1.0)
    NW = 256 // WIN
    RM = 256

    def vec(i, n):
        return vecs[i : i + 1, 0:n]

    def row_at(pos, count=1):
        return pl.ds(pl.multiple_of(pos * 256, 256), count * 256)

    tmp[...] = jnp.zeros_like(tmp)
    for ref in (d_qkv, d_proj, d_fc1, d_fc2, d_conv, d_norm, d_rel):
        ref[...] = jnp.zeros_like(ref)
    for ref, size in ((a_buf, A_USED), (b_buf, B_USED), (c_buf, C_USED)):
        if ref.shape[0] > size:
            ref[size:, :] = jnp.zeros((ref.shape[0] - size, 128), bf16)

    col_in = rows_of((256, C)) < width
    col_in_p = rows_of((256, CP)) < width

    def put_g(pos, row, flag):
        g = jnp.where(col_in, row.astype(f32), 0.0) * flag
        tmp[8:264, 0:C] = g
        at = row_at(pos)
        gcat[at, 0:CP] = tmp[9:265, :].astype(bf16)
        gcat[at, CP : 2 * CP] = tmp[8:264, :].astype(bf16)
        gcat[at, 2 * CP : 3 * CP] = tmp[7:263, :].astype(bf16)

    def iota(shape, dim):
        return lax.broadcasted_iota(jnp.int32, shape, dim)

    def padded(v):
        return jnp.concatenate([v.astype(f32), jnp.zeros((CR - C, v.shape[1]), f32)], axis=0).astype(bf16)

    for ref in (wqkv, wproj, wfc1, wfc2t, wconv, vecs):
        ref[...] = jnp.zeros_like(ref)
    part = iota((3 * C, 3 * CP), 1)
    lane = part & (CP - 1)
    place = (part >> 8) * C + (lane >> 5) * HEAD_DIM + (lane & 31)
    used = ((lane & 31) < HEAD_DIM) & (lane < HEADS * HP_DIM)
    spread = (used & (iota((3 * C, 3 * CP), 0) == place)).astype(bf16)
    wqkv[0:CR, :] = padded(dot(r_qkv[...], spread))
    lane = iota((CP, C), 0)
    place = (lane >> 5) * HEAD_DIM + (lane & 31)
    used = ((lane & 31) < HEAD_DIM) & (lane < HEADS * HP_DIM)
    wproj[:, 0:C] = dot((used & (iota((CP, C), 1) == place)).astype(bf16), r_proj[...]).astype(bf16)
    wfc1[0:CR, 0:HID] = padded(r_fc1[...])
    wfc2t[0:CR, 0:HID] = padded(r_fc2t[...])
    for a in range(3):
        for b in range(3):
            wconv[a, 0:CR, b * CP : b * CP + C] = padded(r_conv[a, b])
    for n, ref in ((0, r_n1g), (1, r_n1b), (3, r_pb), (4, r_n2g), (5, r_n2b), (6, r_f1b), (7, r_f2b), (8, r_cb)):
        vecs[n : n + 1, 0 : ref.shape[0]] = ref[...].reshape(1, ref.shape[0])
    for n in (1, 5, 7):
        vecs[n : n + 1, C : C + 1] = jnp.ones((1, 1), f32)
    qvb = r_qvb[...].reshape(1, 2 * C)
    for h in range(HEADS):
        at = h * HP_DIM
        vecs[2:3, at : at + HEAD_DIM] = qvb[:, h * HEAD_DIM : (h + 1) * HEAD_DIM]
        vecs[2:3, 2 * CP + at : 2 * CP + at + HEAD_DIM] = qvb[
            :, C + h * HEAD_DIM : C + (h + 1) * HEAD_DIM
        ]
    score_terms(r_table[...], extra)

    load_cot.wait()

    @pl.loop(0, 13)
    def _(r):
        put_g(r, io1[r + 3], 1.0)

    put_g(14, io1[15], joined)
    pl.semaphore_wait(barrier, len(peers))
    send_cot.start()
    send_img.start()
    load_img.wait()

    pos_hi = rows_of((1, WIN, CP)) >= SHIFT

    def rolled(a, b):
        t = jnp.where(pos_hi, a, b)
        return pltpu.roll(t, SHIFT, 1)

    def to_win(ref, k):
        nxt = jnp.minimum(k + 1, NW - 1)
        a = ref[:, pl.ds(pl.multiple_of(k * WIN, WIN), WIN), :]
        b = ref[:, pl.ds(pl.multiple_of(nxt * WIN, WIN), WIN), :]
        b = jnp.where(k == nb - 1, ref[:, 0:WIN, :], b)
        return rolled(a, b).reshape(AREA, CP)

    def from_win(ref, band):
        def block(k):
            at = pl.multiple_of((band * NW + k) * AREA, AREA)
            return ref[pl.ds(at, AREA), :].reshape(WIN, WIN, CP)

        @pl.loop(0, NW, unroll=4)
        def _(k):
            b = block(k)
            edge[...] = jnp.where(k == nb - 1, b, edge[...])
            xband[:, pl.ds(pl.multiple_of(k * WIN, WIN), WIN), :] = rolled(
                block(jnp.maximum(k - 1, 0)), b
            )

        xband[:, 0:WIN, :] = rolled(edge[...], block(0))

    def win_rows(w):
        return pl.ds(pl.multiple_of(w * AREA, AREA), AREA)

    @pl.loop(0, 2)
    def _(band):
        @pl.when(band == 1)
        def _():
            send_cot.wait()
            send_img.wait()
            put_g(13, io1[16], joined)

            @pl.loop(0, 5)
            def _(r):
                put_g(15 + r, io1[16 + r], 1.0)

        xband[:, :, 128:256] = jnp.zeros((8, 256, 128), f32)

        @pl.loop(0, 8)
        def _(y):
            xband[y, :, 0:C] = io2[band * 8 + y + 4].astype(f32)

        @pl.loop(0, 4)
        def _(y):
            r = band * 8 + 2 * y
            pos = r + 1 + jnp.where(r >= 12, 2, 0)
            acc = None
            for a in range(3):
                d = dot(gcat[row_at(pos + 1 - a, 2), :], wconv[a], 1, 1)
                acc = d if acc is None else acc + d
            for n in range(2):
                gband[2 * y + n] = jnp.where(col_in_p, acc[n * 256 : (n + 1) * 256], 0.0)

        @pl.loop(0, 4)
        def _(gg):
            g = band * 4 + gg
            k0 = gg * 8
            gs = pl.ds(pl.multiple_of(g * 512, 512), 512)

            xs = [to_win(xband, k0 + w) for w in range(8)]
            for w in range(8):
                winf[win_rows(gg * 8 + w), :] = xs[w]
                fgrad[win_rows(g * 8 + w), :] = to_win(gband, k0 + w)
                xhat, rs_, ln_out = ln_fwd(xs[w], vec(0, CP), vec(1, CP))
                xhat1[win_rows(g * 8 + w), :] = with_rstd(xhat, rs_).astype(bf16)
                normed[win_rows(g * 8 + w), :] = ln_out.astype(bf16)

            for n in range(3):
                sl = slice(n * CP, (n + 1) * CP)
                qkv[gs, sl] = (dot(normed[gs, :], wqkv[:, sl]) + vecs[2:3, sl]).astype(bf16)

            i = 0
            if True:
                which = jnp.where((band == 1) & is_last, 2, 0)
                jobs = []
                for w in range(8):
                    rs = win_rows(g * 8 + i * 8 + w)
                    edge_win = k0 + i * 8 + w == nb - 1
                    for n, (h0, count) in enumerate(GROUPS):
                        jobs.append((rs, w, edge_win, n, count, slice(h0 * AREA, (h0 + count) * AREA)))
                qs = [qkv[rs, n * 128 : (n + 1) * 128] for rs, w, ew, n, count, hl in jobs]
                ks = [qkv[rs, CP + n * 128 : CP + (n + 1) * 128] for rs, w, ew, n, count, hl in jobs]
                vs = [qkv[rs, 2 * CP + n * 128 : 2 * CP + (n + 1) * 128] for rs, w, ew, n, count, hl in jobs]
                ss = [dot(k, spread_heads(q, job[4]), 1, 1) for q, k, job in zip(qs, ks, jobs)]
                ps = []
                for s, (rs, w, ew, n, count, hl) in zip(ss, jobs):
                    more = jnp.where(ew, extra[which + 1, :, hl], extra[which, :, hl])
                    s = s * (SCALE * LOG2E) + more
                    top = jnp.max(s, axis=0, keepdims=True)
                    e = jnp.exp2(s - top)
                    total = jnp.sum(e, axis=0, keepdims=True)
                    ps.append((e * (1.0 / total)).astype(bf16))
                os = [gather_heads(dot(p, v, 0, 0), job[4]) for p, v, job in zip(ps, vs, jobs)]
                for p, o, (rs, w, ew, n, count, hl) in zip(ps, os, jobs):
                    probs[rs, hl] = p
                    if n == 0:
                        o = jnp.where(lanes((1, 128)) == HEAD_DIM, 1.0, o)
                    mixed[win_rows(i * 8 + w), n * 128 : (n + 1) * 128] = o.astype(bf16)

            parts = range(0, 512, 256)
            at_rows = [pl.ds(pl.multiple_of(g * 512 + r, 256), 256) for r in parts]
            in_band = [pl.ds(pl.multiple_of(gg * 512 + r, 256), 256) for r in parts]
            mixes = [mixed[r : r + 256, :] for r in parts]
            firsts = [dot(m, wproj[...]) + vec(3, CP) + winf[rs, :] for m, rs in zip(mixes, in_band)]

            def norm2(v):
                xhat, rs_, ln_out = ln_fwd(v, vec(4, CP), vec(5, CP))
                return xhat, rs_, ln_out.astype(bf16)

            def activate(v):
                ac, dg = gelu_pair(v + vec(6, HP))
                return jnp.where(lanes((1, HP)) == HID, 1.0, ac).astype(bf16), dg.astype(bf16)

            norms = [by_rows(norm2, 64, v) for v in firsts]
            n2s = [n[2] for n in norms]
            acts = [by_rows(activate, 64, dot(n2, wfc1[...])) for n2 in n2s]
            for fs, (ac, dg), rs in zip(firsts, acts, in_band):
                winf[rs, :] = fs + dot(ac, wfc2t[...], 1, 1) + vec(7, CP)
            lgs = [fgrad[rs, :] for rs in at_rows]
            mgs = [lg.astype(bf16) for lg in lgs]
            hgs = [
                (dot(mg, wfc2t[...]).astype(bf16).astype(f32) * dg.astype(f32)).astype(bf16)
                for mg, (ac, dg) in zip(mgs, acts)
            ]
            dns = [dot(hg, wfc1[...], 1, 1).astype(bf16) for hg in hgs]

            def back2(dn2, xh, rs_, lg):
                dn2 = dn2.astype(f32)
                fg = lg + ln_bwd(dn2, xh, rs_, vec(4, CP))
                return fg, fg.astype(bf16), fold8(dn2 * xh), fold8(dn2)

            backs = [
                by_rows(back2, 64, dn, n[0], n[1], lg) for dn, n, lg in zip(dns, norms, lgs)
            ]
            ats = [b[1] for b in backs]
            for b, rs in zip(backs, at_rows):
                fgrad[rs, :] = b[0]
                do_buf[rs, :] = dot(b[1], wproj[...], 1, 1).astype(bf16)
            d_norm[0:8, :] += added([fold8(b[2]) for b in backs])
            d_norm[8:16, :] += added([fold8(b[3]) for b in backs])
            join = lambda vs: jnp.concatenate(vs, axis=0)
            mg = join(mgs)
            d_fc2[...] += dot(mg[:, 0:CR], join([ac for ac, dg in acts]), 0, 0)
            d_norm[32:40, :] += fold8(mg.astype(f32))
            d_fc1[...] += dot(join(n2s)[:, 0:CR], join(hgs), 0, 0)
            d_proj[...] += dot(mixed[:, 0:CR], join(ats), 0, 0)

        from_win(winf, 0)

        @pl.loop(0, 8)
        def _(y):
            r = band * 8 + y
            pos = r + 5 + jnp.where(r >= 12, 2, 0)
            llbuf[row_at(pos), :] = jnp.where(col_in_p, xband[y], 0.0).astype(bf16)

    joined_low = joined.astype(bf16)
    llbuf[17 * 256 : 18 * 256, :] = llbuf[19 * 256 : 20 * 256, :] * joined_low
    llbuf[18 * 256 : 19 * 256, :] = llbuf[16 * 256 : 17 * 256, :] * joined_low
    send_up = remote(llbuf.at[pl.ds(5 * 256, 256)], llbuf.at[pl.ds(23 * 256, 256)], up, 2)
    send_down = remote(llbuf.at[pl.ds(22 * 256, 256)], llbuf.at[pl.ds(4 * 256, 256)], down, 3)
    send_more = remote(llbuf.at[pl.ds(18 * 256, 1024)], llbuf.at[pl.ds(0, 1024)], down, 4)
    send_up.start()
    send_down.start()

    def wgrad_rows(n):
        start = 1 + 4 * n + jnp.where(n == 3, 2, 0)
        gs = gcat[row_at(start, 4), :]
        for a in range(3):
            d_conv[a] += dot(llbuf[row_at(start + a + 3, 4), 0:CR], gs, 0, 0)

    low_lanes = lanes((1, 128)) < 64

    def mix(p, q):
        return jnp.where(low_lanes, p, pltpu.roll(q, 64, 1)).astype(bf16)

    a_buf[0:CR, :] = d_fc1[:, CP:HP].astype(bf16)
    for n in range(3):
        a_buf[(n + 1) * CR : (n + 2) * CR, :] = d_fc2[:, n * 128 : (n + 1) * 128].astype(bf16)
    a_buf[4 * CR : 5 * CR, :] = d_proj[:, 0:128].astype(bf16)
    ara.step(0)

    @pl.loop(1, 3)
    def _(n):
        wgrad_rows(n)

    send_up.wait()
    send_down.wait()
    ara.step(1)

    @pl.loop(0, 2)
    def _(n):
        wgrad_rows(n * 3)

    tails = []
    for a in range(3):
        for b in range(3):
            at = (a * 3 + b) * CR
            c_buf[at : at + CR, :] = d_conv[a, :, b * CP : b * CP + 128].astype(bf16)
            tails.append((d_conv, a, slice(b * CP + 128, (b + 1) * CP)))
    tails = [ref[a, :, ln] for ref, a, ln in tails] + [d_proj[:, 128:256]]
    for n in range(5):
        at = C_MIX + n * CR
        c_buf[at : at + CR, :] = mix(tails[2 * n], tails[2 * n + 1])
    for n in range(2):
        at = C_FC1 + n * CR
        c_buf[at : at + CR, :] = d_fc1[:, n * 128 : (n + 1) * 128].astype(bf16)
    arc.step(0)

    def conv_rows(lo, hi):
        @pl.loop(lo // 2, hi // 2)
        def _(half):
            r = 2 * half
            acc = None
            for a in range(3):
                d = dot(llbuf[row_at(r + a, 2), :], wconv[a])
                acc = d if acc is None else acc + d
            for n in range(2):
                px = slice(n * 256, (n + 1) * 256)
                tmp[8:264, :] = acc[px, 0:CP]
                tmp[280:536, :] = acc[px, 2 * CP : 3 * CP]
                out = acc[px, CP : 2 * CP] + tmp[7:263, :] + tmp[281:537, :] + vec(8, CP)
                out = out[:, 0:C] + io2[r + n].astype(f32)
                io1[r + n] = jnp.where(col_in, out, 0.0).astype(bf16)

    def grad_rows(band):
        from_win(fgrad, band)

        @pl.loop(0, 8)
        def _(y):
            r = band * 8 + y
            pos = r + 1 + jnp.where(r >= 12, 2, 0)
            v = xband[y] + gcat[row_at(pos), CP : 2 * CP].astype(f32)
            ig_rows[r] = jnp.where(col_in_p, v, 0.0)[:, 0:C].astype(bf16)

    send_ig = remote(ig_rows.at[pl.ds(12, 4)], ig_out.at[pl.ds(0, 4)], down, 5)

    @pl.loop(0, 8)
    def _(turn):
        g = lax.rem(turn + 4, 8)
        gs = pl.ds(pl.multiple_of(g * 512, 512), 512)

        i = 0
        if True:
            jobs = []
            for w in range(8):
                rs = win_rows(g * 8 + i * 8 + w)
                for n, (h0, count) in enumerate(GROUPS):
                    jobs.append((rs, n, count, slice(h0 * AREA, (h0 + count) * AREA)))
            qs = [qkv[rs, n * 128 : (n + 1) * 128] for rs, n, count, hl in jobs]
            ks = [qkv[rs, CP + n * 128 : CP + (n + 1) * 128] for rs, n, count, hl in jobs]
            vs = [qkv[rs, 2 * CP + n * 128 : 2 * CP + (n + 1) * 128] for rs, n, count, hl in jobs]
            dos = [spread_heads(do_buf[rs, n * 128 : (n + 1) * 128], count) for rs, n, count, hl in jobs]
            pbs = [probs[rs, hl] for rs, n, count, hl in jobs]
            dps = [dot(v, d, 1, 1) for v, d in zip(vs, dos)]
            dvs = [dot(p, d) for p, d in zip(pbs, dos)]
            dss = []
            for dp, pb in zip(dps, pbs):
                p = pb.astype(f32)
                dss.append((p * (dp - jnp.sum(p * dp, axis=0, keepdims=True))).astype(bf16))
            dks = [dot(ds, spread_heads(q, job[2])) * SCALE for ds, q, job in zip(dss, qs, jobs)]
            dqs = [gather_heads(dot(ds, k, 0, 0), job[2]) * SCALE for ds, k, job in zip(dss, ks, jobs)]
            for n, (h0, count) in enumerate(GROUPS):
                hl = slice(h0 * AREA, (h0 + count) * AREA)
                d_rel[:, hl] += functools.reduce(jnp.add, [d.astype(f32) for d in dss[n::2]])
            for dq, dk, dv, (rs, n, count, hl) in zip(dqs, dks, dvs, jobs):
                qkv[rs, n * 128 : (n + 1) * 128] = dq.astype(bf16)
                qkv[rs, CP + n * 128 : CP + (n + 1) * 128] = dk.astype(bf16)
                qkv[rs, 2 * CP + n * 128 : 2 * CP + (n + 1) * 128] = dv.astype(bf16)

        d_qkv[...] += dot(normed[gs, 0:CR], qkv[gs, :], 0, 0)

        @pl.when(turn == 5)
        def _():
            send_more.start()

        for at, steps in TURNS:

            @pl.when(turn == at)
            def _(steps=steps):
                for which, k in steps:
                    {"a": ara, "c": arc}[which].step(k)

    for n in range(3):
        b_buf[n * CR : (n + 1) * CR, :] = d_qkv[:, n * CP : n * CP + 128].astype(bf16)
    b_buf[3 * CR : 4 * CR, :] = mix(d_qkv[:, 128:256], d_qkv[:, CP + 128 : 2 * CP])
    b_buf[4 * CR : 5 * CR, :] = mix(d_qkv[:, 2 * CP + 128 : 3 * CP], d_qkv[:, 2 * CP + 128 : 3 * CP])
    sums = jnp.sum(d_norm[...].reshape(5, 8, CP), axis=1)
    small = jnp.concatenate([table_sum(d_rel[...]), sums, jnp.zeros((3, CP), f32)], axis=0)
    b_buf[B_SMALL : B_SMALL + 16, :] = small[:, 0:128].astype(bf16)
    b_buf[B_SMALL + 16 : B_SMALL + 32, :] = small[:, 128:256].astype(bf16)
    arb.step(0)
    ara.step(4)

    def norm1_back(lo, hi):
        @pl.loop(lo, hi)
        def _(g):
            gs = pl.ds(pl.multiple_of(g * 512, 512), 512)
            dn1 = dot(qkv[gs, :], wqkv[...], 1, 1).astype(bf16)

            def back1(dn, xhat, fg):
                dn, xhat = dn.astype(f32), xhat.astype(f32)
                out = fg + ln_bwd(dn, xhat, xhat[:, 200:201] + xhat[:, 201:202], vec(0, CP))
                return out, fold8(dn * xhat), fold8(dn)

            back = by_rows(back1, 64, dn1, xhat1[gs, :], fgrad[gs, :])
            fgrad[gs, :] = back[0]
            d_norm[16:24, :] += fold8(back[1])
            d_norm[24:32, :] += fold8(back[2])

    norm1_back(4, 8)
    arb.step(1)
    grad_rows(1)
    send_ig.start()
    norm1_back(0, 4)
    sums = jnp.sum(d_norm[16:32, :].reshape(2, 8, CP), axis=1)
    sums = jnp.concatenate([sums[:, 0:128], sums[:, 128:256], jnp.zeros((4, 128), f32)], axis=0)
    ard.begin(sums)
    ara.step(5)
    arc.step(3)
    conv_rows(4, 8)
    arb.step(2)
    ara.step(6)
    ard.step(0)
    conv_rows(8, 16)
    arc.step(4)
    ard.step(1)
    send_more.wait()
    conv_rows(0, 4)
    store_res = pltpu.make_async_copy(io1.at[pl.ds(0, 16)], res_out, lsem.at[2])
    store_res.start()
    grad_rows(0)
    store_ig = pltpu.make_async_copy(ig_rows.at[pl.ds(0, 12)], ig_out.at[pl.ds(4, 12)], lsem.at[3])
    store_ig.start()
    arb.step(3)
    ard.step(2)
    d_out[...] = dd_sums[3]
    arc.step(5)
    arb.step(5)
    arc.step(6)
    arb.step(6)
    send_ig.wait()
    store_res.wait()
    store_ig.wait()


def finish_kernel(
    a_ref, b_ref, c_ref, d_ref, o_n1g, o_n1b, o_qkv, o_qvb, o_table, o_proj, o_pb, o_n2g, o_n2b, o_fc1, o_f1b, o_fc2t,
    o_f2b, o_conv, o_cb,
):
    def block(ref, at, rows=CR):
        return ref[at : at + rows, :].astype(f32)

    def halves(v):
        return v, pltpu.roll(v, 64, 1)

    tails = []
    for n in range(5):
        tails += halves(block(c_ref, C_MIX + n * CR))
    for a in range(3):
        for b in range(3):
            v = jnp.concatenate([block(c_ref, (a * 3 + b) * CR), tails[a * 3 + b]], axis=1)
            o_conv[a, b] = v[0:C, 0:C]
            if a == 1 and b == 1:
                o_cb[...] = v[C : C + 1, 0:C].reshape(C)
    fc1 = [block(c_ref, C_FC1), block(c_ref, C_FC1 + CR), block(a_ref, 0)]
    fc1 = jnp.concatenate(fc1, axis=1)
    o_fc1[...] = fc1[0:C, 0:HID]
    o_f1b[...] = fc1[C : C + 1, 0:HID].reshape(HID)
    fc2 = jnp.concatenate([block(a_ref, (n + 1) * CR) for n in range(3)], axis=1)
    o_fc2t[...] = fc2[0:C, 0:HID]
    proj = jnp.concatenate([block(a_ref, 4 * CR), tails[9]], axis=1)
    for h in range(HEADS):
        at = h * HP_DIM
        o_proj[h * HEAD_DIM : (h + 1) * HEAD_DIM, :] = proj[at : at + HEAD_DIM, 0:C]
    o_pb[...] = proj[HEAD_DIM : HEAD_DIM + 1, 0:C].reshape(C)
    wide = lax.broadcasted_iota(jnp.int32, (CP, CP), 0)
    dense = lax.broadcasted_iota(jnp.int32, (CP, CP), 1)
    heads_out = (wide == dense + lax.div(dense, HEAD_DIM) * (HP_DIM - HEAD_DIM)) & (dense < C)
    heads_out = heads_out.astype(bf16)
    rest = halves(block(b_ref, 3 * CR)) + halves(block(b_ref, 4 * CR))
    for n in range(3):
        v = jnp.concatenate([block(b_ref, n * CR), rest[n]], axis=1).astype(bf16)
        v = dot(v, heads_out)
        o_qkv[:, n * C : (n + 1) * C] = v[0:C, 0:C]
        if n != 1:
            o_qvb[n // 2 * C : (n // 2 + 1) * C] = v[C : C + 1, 0:C].reshape(C)
    small = jnp.concatenate([block(b_ref, B_SMALL, 16), block(b_ref, B_SMALL + 16, 16)], axis=1)
    o_table[...] = small[0:HEADS, 0 : o_table.shape[1]]
    for n, ref in ((0, o_n1g), (1, o_n1b)):
        v = jnp.concatenate([d_ref[n : n + 1, :], d_ref[n + 2 : n + 3, :]], axis=1)
        ref[...] = v[:, 0:C].reshape(C)
    for n, ref in ((8, o_n2g), (9, o_n2b), (12, o_f2b)):
        ref[...] = small[n : n + 1, 0:C].reshape(C)


def score_terms(table, extra):
    table = jnp.concatenate([table * LOG2E, jnp.zeros((2, table.shape[1]), f32)], axis=0)
    table = jnp.concatenate([table, jnp.zeros((8, CP - table.shape[1]), f32)], axis=1)
    shifted = [pltpu.roll(table, x, 1) if x else table for x in range(WIN)]
    row = lax.broadcasted_iota(jnp.int32, (AREA, CP), 0)
    lane = lax.broadcasted_iota(jnp.int32, (AREA, CP), 1)
    put = (lane == row + (row >> 3) * (WIN - 1)).astype(bf16)
    shape = (AREA, AREA)
    j = lax.broadcasted_iota(jnp.int32, shape, 0)
    i = lax.broadcasted_iota(jnp.int32, shape, 1)
    rows_differ = ((j >> 5) & 1) != ((i >> 5) & 1)
    cols_differ = ((j >> 2) & 1) != ((i >> 2) & 1)
    masks = [None, cols_differ, rows_differ, rows_differ | cols_differ]
    for h in range(HEADS):
        base = jnp.concatenate([t[h : h + 1] for t in shifted], axis=0)
        wide = jnp.concatenate(
            [pltpu.roll(base, CP - (112 - 15 * y), 1) for y in range(WIN)], axis=0
        )
        high = wide.astype(bf16)
        rest = wide - high.astype(f32)
        mid = rest.astype(bf16)
        low = (rest - mid.astype(f32)).astype(bf16)
        term = dot(high, put, 1, 1) + dot(mid, put, 1, 1) + dot(low, put, 1, 1)
        for n, mask in enumerate(masks):
            value = term if mask is None else term + jnp.where(mask, -100.0 * LOG2E, 0.0)
            extra[n, :, h * AREA : (h + 1) * AREA] = value


def table_sum(d_rel):
    row = lax.broadcasted_iota(jnp.int32, (AREA, CP), 0)
    lane = lax.broadcasted_iota(jnp.int32, (AREA, CP), 1)
    put = (lane == row + lax.div(row, WIN) * (WIN - 1)).astype(bf16)
    heads = []
    for h in range(HEADS):
        v = d_rel[:, h * AREA : (h + 1) * AREA]
        v1 = v.astype(bf16)
        v2 = (v - v1.astype(f32)).astype(bf16)
        wide = dot(v1, put) + dot(v2, put)
        total = None
        for y in range(WIN):
            part = pltpu.roll(wide[y * WIN : (y + 1) * WIN, :], 112 - 15 * y, 1)
            total = part if total is None else total + part
        heads.append(total)
    out = None
    for x in range(WIN):
        rows = jnp.concatenate([t[x : x + 1] for t in heads] + [jnp.zeros((2, CP), f32)], axis=0)
        rows = pltpu.roll(rows, CP - x, 1) if x else rows
        out = rows if out is None else out + rows
    return out


VM = pl.BlockSpec(memory_space=pltpu.VMEM)
SM = pl.BlockSpec(memory_space=pltpu.SMEM)
HB = pl.BlockSpec(memory_space=pl.ANY)


def up_to(n, m):
    return (n + m - 1) // m * m


def run_layer(stripes, imgs, *operands):
    S = jax.ShapeDtypeStruct
    V = pltpu.VMEM
    chips = stripes // 2
    dma = pltpu.SemaphoreType.DMA
    sems = 2 * (chips + imgs - 1)
    pieces, buffers, outs = [], [], []
    for used, zsplit in ((A_USED, True), (B_USED, False), (C_USED, True)):
        parts = stripes * imgs if zsplit else stripes
        piece = up_to(-(-used // parts), 16)
        group = piece * imgs if zsplit else piece
        pieces.append(piece)
        outs.append(S((stripes * group, 128), bf16))
        buffers += [
            V((stripes * group, 128), bf16),
            V((chips * group, 128), bf16),
            V(((chips - 1) * group, 128), bf16),
            V(((imgs - 1) * piece, 128), bf16),
        ]
    return pl.pallas_call(
        functools.partial(layer_kernel, chips, imgs, tuple(pieces)),
        out_shape=(S((16, 256, C), bf16), S((16, 256, C), bf16), *outs, S((8, 128), f32)),
        in_specs=[SM, HB, HB] + [VM] * 15,
        out_specs=[HB] * 2 + [VM] * 4,
        scratch_shapes=[
            V((CP, 3 * CP), bf16),
            V((CP, CP), bf16),
            V((CP, HP), bf16),
            V((CP, HP), bf16),
            V((3, CP, 3 * CP), bf16),
            V((16, 3 * CP), f32),
            V((4, AREA, HI), f32),
            V((CR, 3 * CP), f32),
            V((CR, CP), f32),
            V((CR, HP), f32),
            V((CR, HP), f32),
            V((3, CR, 3 * CP), f32),
            V((40, CP), f32),
            V((AREA, HI), f32),
            V((21, 256, C), bf16),
            V((20, 256, C), bf16),
            V((8, 256, CP), f32),
            V((8, 256, CP), f32),
            V((20 * 256, 3 * CP), bf16),
            V((24 * 256, CP), bf16),
            V((4096, CP), bf16),
            V((4096, CP), bf16),
            V((4096, 3 * CP), bf16),
            V((4096, HI), bf16),
            V((512, CP), bf16),
            V((2048, CP), f32),
            V((4096, CP), f32),
            V((4096, CP), bf16),
            V((16, 256, C), bf16),
            V((WIN, WIN, CP), f32),
            V((544, CP), f32),
            *buffers,
            V((4, 8, 128), f32),
            V((chips + imgs - 1, 8, 128), f32),
            dma((4,)),
            dma((6,)),
            dma((6,)),
        ]
        + [dma((sems,))] * 6
        + [dma((chips + imgs - 1,))] * 2,
        compiler_params=pltpu.CompilerParams(
            vmem_limit_bytes=63 * 1024 * 1024, collective_id=0, has_side_effects=True
        ),
        name="layer",
    )(*operands)


def run_finish(a, b, c, d, table):
    S = jax.ShapeDtypeStruct
    return pl.pallas_call(
        finish_kernel,
        out_shape=(
            S((C,), f32),
            S((C,), f32),
            S((C, 3 * C), f32),
            S((2 * C,), f32),
            S((HEADS, table), f32),
            S((C, C), f32),
            S((C,), f32),
            S((C,), f32),
            S((C,), f32),
            S((C, HID), f32),
            S((HID,), f32),
            S((C, HID), f32),
            S((C,), f32),
            S((3, 3, C, C), f32),
            S((C,), f32),
        ),
        compiler_params=pltpu.CompilerParams(vmem_limit_bytes=32 * 1024 * 1024),
        name="finish",
    )(a, b, c, d)


def on_device(
    images, widths, norm1_gain, norm1_bias, qkv_weight, qv_bias, bias_table, proj_weight, proj_bias,
    norm2_gain, norm2_bias, fc1_weight, fc1_bias, fc2_weight, fc2_bias, conv_weight, conv_bias, cotangent,
):
    count, rows_here, width, chans = images.shape
    img = images.reshape(rows_here, width, chans)
    cot = cotangent.reshape(rows_here, width, chans)
    scal = lax.div(widths, WIN)
    res, ig, a, b, c, d = run_layer(
        lax.axis_size("rows"), lax.axis_size("imgs"),
        scal, img, cot, qkv_weight, proj_weight, fc1_weight, fc2_weight.T, conv_weight, bias_table.T,
        norm1_gain, norm1_bias, qv_bias, proj_bias, norm2_gain, norm2_bias, fc1_bias, fc2_bias, conv_bias,
    )
    grads = list(run_finish(a, b, c, d, bias_table.shape[0]))
    grads[4] = grads[4].T
    grads[11] = grads[11].T
    return (res[None], ig[None], *grads)


def solution(mesh):
    big = P("imgs", "rows", None, None)
    in_specs = (big, P("imgs")) + (P(),) * 15 + (big,)
    out_specs = (big, big) + (P(),) * 15
    return jax.shard_map(
        on_device, mesh=mesh, in_specs=in_specs, out_specs=out_specs, check_vma=False
    )
```

```python
import functools

import jax
import jax.numpy as jnp
import numpy as np
from jax import lax
from jax.experimental import pallas as pl
from jax.experimental.pallas import tpu as pltpu
from jax.sharding import PartitionSpec as P

HEADS = 6
HEAD_DIM = 30
WIN = 8
SHIFT = 4
C = 180
CP = 256
HID = 360
HP = 384
AREA = WIN * WIN
HI = HEADS * AREA
LOG2E = 1.4426950408889634
SCALE = HEAD_DIM ** (-0.5)

CR = 192
A_USED = 5 * CR
B_SMALL = 5 * CR
B_USED = B_SMALL + 32
C_MIX = 9 * CR
C_FC1 = C_MIX + 5 * CR
C_USED = C_FC1 + 2 * CR

f32 = jnp.float32
bf16 = jnp.bfloat16


def dot(a, b, ca=1, cb=0):
    return lax.dot_general(a, b, (((ca,), (cb,)), ((), ())), preferred_element_type=f32)


def lanes(shape):
    return lax.broadcasted_iota(jnp.int32, shape, len(shape) - 1)


def rows_of(shape):
    return lax.broadcasted_iota(jnp.int32, shape, len(shape) - 2)


def ln_fwd(x, gain, bias):
    real = (lanes((1, CP)) < C).astype(f32)
    mean = jnp.sum(x, axis=-1, keepdims=True) * (1.0 / C)
    xc = (x - mean) * real
    var = jnp.sum(xc * xc, axis=-1, keepdims=True) * (1.0 / C)
    rstd = lax.rsqrt(var + 1e-05)
    xhat = xc * rstd
    return xhat, rstd, xhat * gain + bias


def with_rstd(xhat, rstd):
    high = rstd.astype(bf16).astype(f32)
    lane = lanes((1, CP))
    return jnp.where(lane == 200, high, jnp.where(lane == 201, rstd - high, xhat))


def ln_bwd(dy, xhat, rstd, gain):
    a = dy * gain
    m1 = jnp.sum(a, axis=-1, keepdims=True) * (1.0 / C)
    m2 = jnp.sum(a * xhat, axis=-1, keepdims=True) * (1.0 / C)
    return rstd * (a - m1 - xhat * m2)


def gelu_pair(h):
    z = jnp.abs(h) * 0.7071067811865476
    d = 1.0 + 0.3275911 * z
    t = pl.reciprocal(d, approx=True)
    t = t * (2.0 - d * t)
    e = jnp.exp2(h * h * (-0.5 * LOG2E))
    poly = t * (
        0.254829592 + t * (-0.284496736 + t * (1.421413741 + t * (-1.453152027 + t * 1.061405429)))
    )
    q = 0.5 * poly * e
    phi = jnp.where(h >= 0, 1.0 - q, q)
    return h * phi, phi + h * (e * 0.3989422804014327)


def fold8(v):
    return jnp.sum(v.reshape(v.shape[0] // 8, 8, v.shape[1]), axis=0)


HP_DIM = 32


def by_rows(f, step, *arrays):
    rows = arrays[0].shape[0]
    parts = [f(*[a[i : i + step] for a in arrays]) for i in range(0, rows, step)]
    if not isinstance(parts[0], tuple):
        return jnp.concatenate(parts, axis=0)
    return tuple(jnp.concatenate(p, axis=0) for p in zip(*parts))


def added(values):
    return functools.reduce(jnp.add, values)


def head_mask(h):
    ln = lanes((1, 128))
    return (ln >= h * HP_DIM) & (ln < (h + 1) * HP_DIM)


def spread_heads(v, count):
    return jnp.concatenate(
        [jnp.where(head_mask(h), v, jnp.zeros_like(v)) for h in range(count)], axis=0
    )


def gather_heads(v, count):
    out = jnp.where(head_mask(0), v[:AREA], 0.0)
    for h in range(1, count):
        out = jnp.where(head_mask(h), v[h * AREA : (h + 1) * AREA], out)
    return out


GROUPS = ((0, 4), (4, 2))


def column_masks(width):
    return rows_of((256, CP)) < width


class SmallAllReduce:
    def __init__(self, sums, slots, ssem, rsem, chips, imgs):
        self.sums, self.ssem, self.rsem = [sums.at[n] for n in range(4)], ssem, rsem
        rows, z = lax.axis_index("rows"), lax.axis_index("imgs")
        core, chip = lax.rem(rows, 2), lax.div(rows, 2)
        self.stages = [
            [{"rows": chip * 2 + 1 - core}],
            [{"rows": lax.rem(chip + d, chips) * 2 + core} for d in range(1, chips)],
            [{"imgs": lax.rem(z + d, imgs)} for d in range(1, imgs)],
        ]
        self.first = [0, 1, chips]
        self.slots = slots

    def copies(self, n):
        return [
            pltpu.make_async_remote_copy(
                src_ref=self.sums[n],
                dst_ref=self.slots.at[self.first[n] + d],
                send_sem=self.ssem.at[self.first[n] + d],
                recv_sem=self.rsem.at[self.first[n] + d],
                device_id=to,
                device_id_type=pl.DeviceIdType.MESH,
            )
            for d, to in enumerate(self.stages[n])
        ]

    def begin(self, value):
        self.sums[0][...] = value
        for c in self.copies(0):
            c.start()

    def step(self, n):
        value = self.sums[n][...]
        for d, c in enumerate(self.copies(n)):
            c.wait()
            value += self.slots[self.first[n] + d]
        self.sums[n + 1][...] = value
        if n < 2:
            for c in self.copies(n + 1):
                c.start()


TURNS = ((0, (("a", 1),)), (1, (("c", 1),)), (4, (("a", 2),)), (7, (("c", 2),)))


class AllReduce:
    def __init__(self, buf, out, r1, r2, r3, ssem, rsem, pr, chips, imgs, zsplit):
        self.buf, self.out, self.r1, self.r2, self.r3 = buf, out, r1, r2, r3
        self.ssem, self.rsem, self.chips, self.imgs = ssem, rsem, chips, imgs
        self.zsplit = zsplit
        rows = lax.axis_index("rows")
        self.core = lax.rem(rows, 2)
        self.chip = lax.div(rows, 2)
        self.z = lax.axis_index("imgs")
        self.piece = pr
        self.group = pr * imgs if zsplit else pr
        self.half = self.group * chips
        self.used = 0

    def copy(self, src, dst, device, n):
        return pltpu.make_async_remote_copy(
            src_ref=src,
            dst_ref=dst,
            send_sem=self.ssem.at[n],
            recv_sem=self.rsem.at[n],
            device_id=device,
            device_id_type=pl.DeviceIdType.MESH,
        )

    def rows(self, ref, start, size):
        return ref.at[pl.ds(pl.multiple_of(start, 16), size)]

    def base_half(self, core):
        return core * self.half

    def base_group(self, chip):
        return self.core * self.half + chip * self.group

    def base_piece(self, z):
        return self.base_group(self.chip) + (z * self.piece if self.zsplit else 0)

    def core_copy(self, ref, dst, n, gather):
        side = self.core if gather else 1 - self.core
        src = self.rows(ref, self.base_half(side), self.half)
        dst = src if dst is None else dst
        return [self.copy(src, dst, {"rows": self.chip * 2 + 1 - self.core}, n)]

    def chip_copies(self, ref, dst, n, gather):
        out = []
        for d in range(1, self.chips):
            to = lax.rem(self.chip + d, self.chips)
            src = self.rows(ref, self.base_group(self.chip if gather else to), self.group)
            to_ref = src if gather else dst.at[pl.ds((d - 1) * self.group, self.group)]
            out.append(self.copy(src, to_ref, {"rows": to * 2 + self.core}, n + d - 1))
        return out

    def img_copies(self, ref, dst, n, gather):
        out = []
        for d in range(1, self.imgs):
            to = lax.rem(self.z + d, self.imgs)
            src = self.rows(ref, self.base_piece(self.z if gather else to), self.piece)
            to_ref = src if gather else dst.at[pl.ds((d - 1) * self.piece, self.piece)]
            out.append(self.copy(src, to_ref, {"imgs": to}, n + d - 1))
        return out

    def start(self, copies):
        for c in copies:
            c.start()
        return copies

    def wait(self, copies):
        for c in copies:
            c.wait()

    def add(self, base, size, extra, count, stride, target):
        step = min(size, 64)
        while size % step:
            step -= 16

        @pl.loop(0, size // step)
        def _(i):
            at = pl.ds(pl.multiple_of(base + i * step, 16), step)
            total = self.buf[at, :].astype(f32)
            for d in range(count):
                total += extra[pl.ds(pl.multiple_of(d * stride + i * step, 16), step), :].astype(f32)
            target[at, :] = total.astype(bf16)

    def step(self, k):
        n2 = 1
        n3 = n2 + self.chips - 1
        n4 = n3 + self.imgs - 1
        n5 = n4 + self.imgs - 1
        n6 = n5 + self.chips - 1
        first = lambda: self.core_copy(self.buf, self.r1, 0, False)
        second = lambda: self.chip_copies(self.buf, self.r2, n2, False)
        third = lambda: self.img_copies(self.buf, self.r3, n3, False)
        fourth = lambda: self.img_copies(self.out, None, n4, True) if self.zsplit else []
        fifth = lambda: self.chip_copies(self.out, None, n5, True)
        sixth = lambda: self.core_copy(self.out, None, n6, True)
        if k == 0:
            self.start(first())
        elif k == 1:
            self.wait(first())
            self.add(self.base_half(self.core), self.half, self.r1, 1, 0, self.buf)
            self.start(second())
        elif k == 2:
            self.wait(second())
            self.add(
                self.base_group(self.chip), self.group, self.r2, self.chips - 1, self.group, self.buf
            )
            self.start(third())
        elif k == 3:
            self.wait(third())
            self.add(
                self.base_piece(self.z), self.piece, self.r3, self.imgs - 1, self.piece, self.out
            )
            self.start(fourth() if self.zsplit else fifth())
        elif k == 4:
            if self.zsplit:
                self.wait(fourth())
                self.start(fifth())
        elif k == 5:
            self.wait(fifth())
            self.start(sixth())
        elif k == 6:
            self.wait(sixth())


def all_reduce_sems(chips, imgs):
    return 2 * (1 + chips - 1 + imgs - 1)


def layer_kernel(
    chips,
    imgs,
    pieces,
    splits,
    scal,
    img,
    cot,
    r_qkv,
    r_proj,
    r_fc1,
    r_fc2t,
    r_conv,
    r_table,
    r_n1g,
    r_n1b,
    r_qvb,
    r_pb,
    r_n2g,
    r_n2b,
    r_f1b,
    r_f2b,
    r_cb,
    res_out,
    ig_out,
    a_out,
    b_out,
    c_out,
    d_out,
    wqkv,
    wproj,
    wfc1,
    wfc2t,
    wconv,
    vecs,
    extra,
    d_qkv,
    d_proj,
    d_fc1,
    d_fc2,
    d_conv,
    d_norm,
    d_rel,
    io1,
    io2,
    xband,
    gband,
    gcat,
    llbuf,
    xhat1,
    normed,
    qkv,
    probs,
    mixed,
    winf,
    fgrad,
    do_buf,
    ig_rows,
    edge,
    tmp_eye,
    planes,
    tmp,
    a_buf,
    a_r1,
    a_r2,
    a_r3,
    b_buf,
    b_r1,
    b_r2,
    b_r3,
    c_buf,
    c_r1,
    c_r2,
    c_r3,
    dd_sums,
    dd_slots,
    lsem,
    hs,
    hr,
    a_s,
    a_r,
    b_s,
    b_r,
    c_s,
    c_r,
    dd_s,
    dd_r,
):
    stripes = 2 * chips
    rank = lax.axis_index("rows")
    core = lax.rem(rank, 2)
    up = lax.rem(rank + stripes - 1, stripes)
    down = lax.rem(rank + 1, stripes)
    pa, pb, pc = pieces
    ara = AllReduce(a_buf, a_out, a_r1, a_r2, a_r3, a_s, a_r, pa, chips, imgs, splits[0])
    arb = AllReduce(b_buf, b_out, b_r1, b_r2, b_r3, b_s, b_r, pb, chips, imgs, splits[1])
    arc = AllReduce(c_buf, c_out, c_r1, c_r2, c_r3, c_s, c_r, pc, chips, imgs, splits[2])

    ard = SmallAllReduce(dd_sums, dd_slots, dd_s, dd_r, chips, imgs)

    flat = C * 16
    load_cot = pltpu.make_async_copy(cot, qkv.at[pl.ds(0, flat), pl.ds(CP, CP)], lsem.at[0])
    load_img = pltpu.make_async_copy(img, qkv.at[pl.ds(0, flat), pl.ds(0, CP)], lsem.at[1])
    load_cot.start()
    load_img.start()

    barrier = pltpu.get_barrier_semaphore()
    peers = [{"rows": up}, {"rows": down}]
    peers += [{"rows": lax.rem(rank + 2 * d, stripes)} for d in range(1, chips)]
    peers += [{"imgs": lax.rem(ara.z + d, imgs)} for d in range(1, imgs)]
    for peer in peers:
        pl.semaphore_signal(barrier, inc=1, device_id=peer, device_id_type=pl.DeviceIdType.MESH)

    def remote(src, dst, to, n):
        return pltpu.make_async_remote_copy(
            src_ref=src,
            dst_ref=dst,
            send_sem=hs.at[n],
            recv_sem=hr.at[n],
            device_id={"rows": to},
            device_id_type=pl.DeviceIdType.MESH,
        )

    send_img = remote(io2.at[pl.ds(0, 4)], io2.at[pl.ds(16, 4)], up, 0)
    send_cot = remote(io1.at[pl.ds(0, 5)], io1.at[pl.ds(16, 5)], up, 1)
    nb = scal[0]
    width = nb * WIN
    is_last = rank == stripes - 1
    joined = jnp.where(is_last, 0.0, 1.0)
    NW = 256 // WIN
    RM = 256

    def vec(i, n):
        return vecs[i : i + 1, 0:n]

    def row_at(pos, count=1):
        return pl.ds(pl.multiple_of(pos * 256, 256), count * 256)

    tmp[...] = jnp.zeros_like(tmp)
    for ref in (d_qkv, d_proj, d_fc1, d_fc2, d_conv, d_norm, d_rel):
        ref[...] = jnp.zeros_like(ref)
    for ref, size in ((a_buf, A_USED), (b_buf, B_USED), (c_buf, C_USED)):
        if ref.shape[0] > size:
            ref[size:, :] = jnp.zeros((ref.shape[0] - size, 128), bf16)

    col_in = rows_of((256, C)) < width
    col_in_p = rows_of((256, CP)) < width

    def put_g(pos, row, flag):
        g = jnp.where(col_in, row.astype(f32), 0.0) * flag
        tmp[8:264, 0:C] = g
        at = row_at(pos)
        gcat[at, 0:CP] = tmp[9:265, :].astype(bf16)
        gcat[at, CP : 2 * CP] = tmp[8:264, :].astype(bf16)
        gcat[at, 2 * CP : 3 * CP] = tmp[7:263, :].astype(bf16)

    def iota(shape, dim):
        return lax.broadcasted_iota(jnp.int32, shape, dim)

    def padded(v):
        return jnp.concatenate([v.astype(f32), jnp.zeros((CR - C, v.shape[1]), f32)], axis=0).astype(bf16)

    for ref in (wqkv, wproj, wfc1, wfc2t, wconv, vecs):
        ref[...] = jnp.zeros_like(ref)
    part = iota((3 * C, 3 * CP), 1)
    lane = part & (CP - 1)
    place = (part >> 8) * C + (lane >> 5) * HEAD_DIM + (lane & 31)
    used = ((lane & 31) < HEAD_DIM) & (lane < HEADS * HP_DIM)
    spread = (used & (iota((3 * C, 3 * CP), 0) == place)).astype(bf16)
    wqkv[0:CR, :] = padded(dot(r_qkv[...], spread))
    lane = iota((CP, C), 0)
    place = (lane >> 5) * HEAD_DIM + (lane & 31)
    used = ((lane & 31) < HEAD_DIM) & (lane < HEADS * HP_DIM)
    wproj[:, 0:C] = dot((used & (iota((CP, C), 1) == place)).astype(bf16), r_proj[...]).astype(bf16)
    wfc1[0:CR, 0:HID] = padded(r_fc1[...])
    wfc2t[0:CR, 0:HID] = padded(r_fc2t[...])
    for a in range(3):
        for b in range(3):
            wconv[a, 0:CR, b * CP : b * CP + C] = padded(r_conv[a, b])
    for n, ref in ((0, r_n1g), (1, r_n1b), (3, r_pb), (4, r_n2g), (5, r_n2b), (6, r_f1b), (7, r_f2b), (8, r_cb)):
        vecs[n : n + 1, 0 : ref.shape[0]] = ref[...].reshape(1, ref.shape[0])
    for n in (1, 5, 7):
        vecs[n : n + 1, C : C + 1] = jnp.ones((1, 1), f32)
    qvb = r_qvb[...].reshape(1, 2 * C)
    for h in range(HEADS):
        at = h * HP_DIM
        vecs[2:3, at : at + HEAD_DIM] = qvb[:, h * HEAD_DIM : (h + 1) * HEAD_DIM]
        vecs[2:3, 2 * CP + at : 2 * CP + at + HEAD_DIM] = qvb[
            :, C + h * HEAD_DIM : C + (h + 1) * HEAD_DIM
        ]
    score_terms(r_table[...], extra)

    tmp_eye[...] = (iota((128, 128), 0) == iota((128, 128), 1)).astype(bf16)

    def to_rows(lane0, dst):
        for m in range(2):
            half = slice(m * 128, (m + 1) * 128)

            @pl.loop(0, flat // 96, unroll=2)
            def _(n):
                at = pl.ds(pl.multiple_of(n * 96, 96), 96)
                planes[at, :] = qkv[at, lane0 + m * 128 : lane0 + (m + 1) * 128].astype(f32)

            for r in range(16):
                x = planes[pl.ds(r, C, stride=16), :].astype(bf16)
                dst[r, half, :] = dot(tmp_eye[...], x, 1, 1).astype(bf16)

    load_cot.wait()
    to_rows(CP, io1)
    load_img.wait()
    to_rows(0, io2)

    @pl.loop(0, 13)
    def _(r):
        put_g(r, io1[r + 3], 1.0)

    put_g(14, io1[15], joined)
    pl.semaphore_wait(barrier, len(peers))
    send_cot.start()
    send_img.start()

    pos_hi = rows_of((1, WIN, CP)) >= SHIFT

    def rolled(a, b):
        t = jnp.where(pos_hi, a, b)
        return pltpu.roll(t, SHIFT, 1)

    def to_win(ref, k):
        nxt = jnp.minimum(k + 1, NW - 1)
        a = ref[:, pl.ds(pl.multiple_of(k * WIN, WIN), WIN), :]
        b = ref[:, pl.ds(pl.multiple_of(nxt * WIN, WIN), WIN), :]
        b = jnp.where(k == nb - 1, ref[:, 0:WIN, :], b)
        return rolled(a, b).reshape(AREA, CP)

    def from_win(ref, band):
        def block(k):
            at = pl.multiple_of((band * NW + k) * AREA, AREA)
            return ref[pl.ds(at, AREA), :].reshape(WIN, WIN, CP)

        @pl.loop(0, NW, unroll=4)
        def _(k):
            b = block(k)
            edge[...] = jnp.where(k == nb - 1, b, edge[...])
            xband[:, pl.ds(pl.multiple_of(k * WIN, WIN), WIN), :] = rolled(
                block(jnp.maximum(k - 1, 0)), b
            )

        xband[:, 0:WIN, :] = rolled(edge[...], block(0))

    def win_rows(w):
        return pl.ds(pl.multiple_of(w * AREA, AREA), AREA)

    send_up = remote(llbuf.at[pl.ds(5 * 256, 256)], llbuf.at[pl.ds(23 * 256, 256)], up, 2)

    @pl.loop(0, 2)
    def _(band):
        @pl.when(band == 1)
        def _():
            send_cot.wait()
            send_img.wait()
            put_g(13, io1[16], joined)

            @pl.loop(0, 5)
            def _(r):
                put_g(15 + r, io1[16 + r], 1.0)

        xband[:, :, 128:256] = jnp.zeros((8, 256, 128), f32)

        @pl.loop(0, 8)
        def _(y):
            xband[y, :, 0:C] = io2[band * 8 + y + 4].astype(f32)

        @pl.loop(0, 4)
        def _(y):
            r = band * 8 + 2 * y
            pos = r + 1 + jnp.where(r >= 12, 2, 0)
            acc = None
            for a in range(3):
                d = dot(gcat[row_at(pos + 1 - a, 2), :], wconv[a], 1, 1)
                acc = d if acc is None else acc + d
            for n in range(2):
                gband[2 * y + n] = jnp.where(col_in_p, acc[n * 256 : (n + 1) * 256], 0.0)

        @pl.loop(0, 4)
        def _(gg):
            g = band * 4 + gg
            k0 = gg * 8
            gs = pl.ds(pl.multiple_of(g * 512, 512), 512)

            xs = [to_win(xband, k0 + w) for w in range(8)]
            for w in range(8):
                winf[win_rows(gg * 8 + w), :] = xs[w]
                fgrad[win_rows(g * 8 + w), :] = to_win(gband, k0 + w)
                xhat, rs_, ln_out = ln_fwd(xs[w], vec(0, CP), vec(1, CP))
                xhat1[win_rows(g * 8 + w), :] = with_rstd(xhat, rs_).astype(bf16)
                normed[win_rows(g * 8 + w), :] = ln_out.astype(bf16)

            for n in range(3):
                sl = slice(n * CP, (n + 1) * CP)
                qkv[gs, sl] = (dot(normed[gs, :], wqkv[:, sl]) + vecs[2:3, sl]).astype(bf16)

            i = 0
            if True:
                which = jnp.where((band == 1) & is_last, 2, 0)
                jobs = []
                for w in range(8):
                    rs = win_rows(g * 8 + i * 8 + w)
                    edge_win = k0 + i * 8 + w == nb - 1
                    for n, (h0, count) in enumerate(GROUPS):
                        jobs.append((rs, w, edge_win, n, count, slice(h0 * AREA, (h0 + count) * AREA)))
                qs = [qkv[rs, n * 128 : (n + 1) * 128] for rs, w, ew, n, count, hl in jobs]
                ks = [qkv[rs, CP + n * 128 : CP + (n + 1) * 128] for rs, w, ew, n, count, hl in jobs]
                vs = [qkv[rs, 2 * CP + n * 128 : 2 * CP + (n + 1) * 128] for rs, w, ew, n, count, hl in jobs]
                ss = [dot(k, spread_heads(q, job[4]), 1, 1) for q, k, job in zip(qs, ks, jobs)]
                ps = []
                for s, (rs, w, ew, n, count, hl) in zip(ss, jobs):
                    more = jnp.where(ew, extra[which + 1, :, hl], extra[which, :, hl])
                    s = s * (SCALE * LOG2E) + more
                    top = jnp.max(s, axis=0, keepdims=True)
                    e = jnp.exp2(s - top)
                    total = jnp.sum(e, axis=0, keepdims=True)
                    ps.append((e * (1.0 / total)).astype(bf16))
                os = [gather_heads(dot(p, v, 0, 0), job[4]) for p, v, job in zip(ps, vs, jobs)]
                for p, o, (rs, w, ew, n, count, hl) in zip(ps, os, jobs):
                    probs[rs, hl] = p
                    if n == 0:
                        o = jnp.where(lanes((1, 128)) == HEAD_DIM, 1.0, o)
                    mixed[win_rows(i * 8 + w), n * 128 : (n + 1) * 128] = o.astype(bf16)

            parts = range(0, 512, 256)
            at_rows = [pl.ds(pl.multiple_of(g * 512 + r, 256), 256) for r in parts]
            in_band = [pl.ds(pl.multiple_of(gg * 512 + r, 256), 256) for r in parts]
            mixes = [mixed[r : r + 256, :] for r in parts]
            firsts = [dot(m, wproj[...]) + vec(3, CP) + winf[rs, :] for m, rs in zip(mixes, in_band)]

            def norm2(v):
                xhat, rs_, ln_out = ln_fwd(v, vec(4, CP), vec(5, CP))
                return xhat, rs_, ln_out.astype(bf16)

            def activate(v):
                ac, dg = gelu_pair(v + vec(6, HP))
                return jnp.where(lanes((1, HP)) == HID, 1.0, ac).astype(bf16), dg.astype(bf16)

            norms = [by_rows(norm2, 64, v) for v in firsts]
            n2s = [n[2] for n in norms]
            acts = [by_rows(activate, 64, dot(n2, wfc1[...])) for n2 in n2s]
            for fs, (ac, dg), rs in zip(firsts, acts, in_band):
                winf[rs, :] = fs + dot(ac, wfc2t[...], 1, 1) + vec(7, CP)
            lgs = [fgrad[rs, :] for rs in at_rows]
            mgs = [lg.astype(bf16) for lg in lgs]
            hgs = [
                (dot(mg, wfc2t[...]).astype(bf16).astype(f32) * dg.astype(f32)).astype(bf16)
                for mg, (ac, dg) in zip(mgs, acts)
            ]
            dns = [dot(hg, wfc1[...], 1, 1).astype(bf16) for hg in hgs]

            def back2(dn2, xh, rs_, lg):
                dn2 = dn2.astype(f32)
                fg = lg + ln_bwd(dn2, xh, rs_, vec(4, CP))
                return fg, fg.astype(bf16), fold8(dn2 * xh), fold8(dn2)

            backs = [
                by_rows(back2, 64, dn, n[0], n[1], lg) for dn, n, lg in zip(dns, norms, lgs)
            ]
            ats = [b[1] for b in backs]
            for b, rs in zip(backs, at_rows):
                fgrad[rs, :] = b[0]
                do_buf[rs, :] = dot(b[1], wproj[...], 1, 1).astype(bf16)
            d_norm[0:8, :] += added([fold8(b[2]) for b in backs])
            d_norm[8:16, :] += added([fold8(b[3]) for b in backs])
            join = lambda vs: jnp.concatenate(vs, axis=0)
            mg = join(mgs)
            d_fc2[...] += dot(mg[:, 0:CR], join([ac for ac, dg in acts]), 0, 0)
            d_norm[32:40, :] += fold8(mg.astype(f32))
            d_fc1[...] += dot(join(n2s)[:, 0:CR], join(hgs), 0, 0)
            d_proj[...] += dot(mixed[:, 0:CR], join(ats), 0, 0)

        from_win(winf, 0)

        @pl.loop(0, 8)
        def _(y):
            r = band * 8 + y
            pos = r + 5 + jnp.where(r >= 12, 2, 0)
            llbuf[row_at(pos), :] = jnp.where(col_in_p, xband[y], 0.0).astype(bf16)

        @pl.when(band == 0)
        def _():
            send_up.start()

    joined_low = joined.astype(bf16)
    llbuf[17 * 256 : 18 * 256, :] = llbuf[19 * 256 : 20 * 256, :] * joined_low
    llbuf[18 * 256 : 19 * 256, :] = llbuf[16 * 256 : 17 * 256, :] * joined_low
    send_down = remote(llbuf.at[pl.ds(22 * 256, 256)], llbuf.at[pl.ds(4 * 256, 256)], down, 3)
    send_more = remote(llbuf.at[pl.ds(18 * 256, 1024)], llbuf.at[pl.ds(0, 1024)], down, 4)
    send_down.start()

    def wgrad_rows(n):
        start = 1 + 4 * n + jnp.where(n == 3, 2, 0)
        gs = gcat[row_at(start, 4), :]
        for a in range(3):
            d_conv[a] += dot(llbuf[row_at(start + a + 3, 4), 0:CR], gs, 0, 0)

    low_lanes = lanes((1, 128)) < 64

    def mix(p, q):
        return jnp.where(low_lanes, p, pltpu.roll(q, 64, 1)).astype(bf16)

    a_buf[0:CR, :] = d_fc1[:, CP:HP].astype(bf16)
    for n in range(3):
        a_buf[(n + 1) * CR : (n + 2) * CR, :] = d_fc2[:, n * 128 : (n + 1) * 128].astype(bf16)
    a_buf[4 * CR : 5 * CR, :] = d_proj[:, 0:128].astype(bf16)
    ara.step(0)

    @pl.loop(1, 3)
    def _(n):
        wgrad_rows(n)

    send_up.wait()
    wgrad_rows(3)
    send_down.wait()
    wgrad_rows(0)

    tails = []
    for a in range(3):
        for b in range(3):
            at = (a * 3 + b) * CR
            c_buf[at : at + CR, :] = d_conv[a, :, b * CP : b * CP + 128].astype(bf16)
            tails.append((d_conv, a, slice(b * CP + 128, (b + 1) * CP)))
    tails = [ref[a, :, ln] for ref, a, ln in tails] + [d_proj[:, 128:256]]
    for n in range(5):
        at = C_MIX + n * CR
        c_buf[at : at + CR, :] = mix(tails[2 * n], tails[2 * n + 1])
    for n in range(2):
        at = C_FC1 + n * CR
        c_buf[at : at + CR, :] = d_fc1[:, n * 128 : (n + 1) * 128].astype(bf16)
    arc.step(0)

    def conv_rows(lo, hi):
        @pl.loop(lo // 2, hi // 2)
        def _(half):
            r = 2 * half
            acc = None
            for a in range(3):
                d = dot(llbuf[row_at(r + a, 2), :], wconv[a])
                acc = d if acc is None else acc + d
            for n in range(2):
                px = slice(n * 256, (n + 1) * 256)
                tmp[8:264, :] = acc[px, 0:CP]
                tmp[280:536, :] = acc[px, 2 * CP : 3 * CP]
                out = acc[px, CP : 2 * CP] + tmp[7:263, :] + tmp[281:537, :] + vec(8, CP)
                out = out[:, 0:C] + io2[r + n].astype(f32)
                io1[r + n] = jnp.where(col_in, out, 0.0).astype(bf16)

    def grad_rows(band):
        from_win(fgrad, band)

        @pl.loop(0, 8)
        def _(y):
            r = band * 8 + y
            pos = r + 1 + jnp.where(r >= 12, 2, 0)
            v = xband[y] + gcat[row_at(pos), CP : 2 * CP].astype(f32)
            ig_rows[r] = jnp.where(col_in_p, v, 0.0)[:, 0:C].astype(bf16)

    send_ig = remote(ig_rows.at[pl.ds(12, 4)], ig_out.at[pl.ds(0, 4)], down, 5)

    @pl.loop(0, 8)
    def _(turn):
        g = lax.rem(turn + 4, 8)
        gs = pl.ds(pl.multiple_of(g * 512, 512), 512)

        i = 0
        if True:
            jobs = []
            for w in range(8):
                rs = win_rows(g * 8 + i * 8 + w)
                for n, (h0, count) in enumerate(GROUPS):
                    jobs.append((rs, n, count, slice(h0 * AREA, (h0 + count) * AREA)))
            qs = [qkv[rs, n * 128 : (n + 1) * 128] for rs, n, count, hl in jobs]
            ks = [qkv[rs, CP + n * 128 : CP + (n + 1) * 128] for rs, n, count, hl in jobs]
            vs = [qkv[rs, 2 * CP + n * 128 : 2 * CP + (n + 1) * 128] for rs, n, count, hl in jobs]
            dos = [spread_heads(do_buf[rs, n * 128 : (n + 1) * 128], count) for rs, n, count, hl in jobs]
            pbs = [probs[rs, hl] for rs, n, count, hl in jobs]
            dps = [dot(v, d, 1, 1) for v, d in zip(vs, dos)]
            dvs = [dot(p, d) for p, d in zip(pbs, dos)]
            dss = []
            for dp, pb in zip(dps, pbs):
                p = pb.astype(f32)
                dss.append((p * (dp - jnp.sum(p * dp, axis=0, keepdims=True))).astype(bf16))
            dks = [dot(ds, spread_heads(q, job[2])) * SCALE for ds, q, job in zip(dss, qs, jobs)]
            dqs = [gather_heads(dot(ds, k, 0, 0), job[2]) * SCALE for ds, k, job in zip(dss, ks, jobs)]
            for n, (h0, count) in enumerate(GROUPS):
                hl = slice(h0 * AREA, (h0 + count) * AREA)
                d_rel[:, hl] += functools.reduce(jnp.add, [d.astype(f32) for d in dss[n::2]])
            for dq, dk, dv, (rs, n, count, hl) in zip(dqs, dks, dvs, jobs):
                qkv[rs, n * 128 : (n + 1) * 128] = dq.astype(bf16)
                qkv[rs, CP + n * 128 : CP + (n + 1) * 128] = dk.astype(bf16)
                qkv[rs, 2 * CP + n * 128 : 2 * CP + (n + 1) * 128] = dv.astype(bf16)

        d_qkv[...] += dot(normed[gs, 0:CR], qkv[gs, :], 0, 0)

        @pl.when(turn == 5)
        def _():
            send_more.start()

        for at, steps in TURNS:

            @pl.when(turn == at)
            def _(steps=steps):
                for which, k in steps:
                    {"a": ara, "c": arc}[which].step(k)

    for n in range(3):
        b_buf[n * CR : (n + 1) * CR, :] = d_qkv[:, n * CP : n * CP + 128].astype(bf16)
    b_buf[3 * CR : 4 * CR, :] = mix(d_qkv[:, 128:256], d_qkv[:, CP + 128 : 2 * CP])
    b_buf[4 * CR : 5 * CR, :] = mix(d_qkv[:, 2 * CP + 128 : 3 * CP], d_qkv[:, 2 * CP + 128 : 3 * CP])
    sums = jnp.sum(d_norm[...].reshape(5, 8, CP), axis=1)
    small = jnp.concatenate([table_sum(d_rel[...]), sums, jnp.zeros((3, CP), f32)], axis=0)
    b_buf[B_SMALL : B_SMALL + 16, :] = small[:, 0:128].astype(bf16)
    b_buf[B_SMALL + 16 : B_SMALL + 32, :] = small[:, 128:256].astype(bf16)
    arb.step(0)
    ara.step(3)

    def norm1_back(lo, hi):
        @pl.loop(lo, hi)
        def _(g):
            gs = pl.ds(pl.multiple_of(g * 512, 512), 512)
            dn1 = dot(qkv[gs, :], wqkv[...], 1, 1).astype(bf16)

            def back1(dn, xhat, fg):
                dn, xhat = dn.astype(f32), xhat.astype(f32)
                out = fg + ln_bwd(dn, xhat, xhat[:, 200:201] + xhat[:, 201:202], vec(0, CP))
                return out, fold8(dn * xhat), fold8(dn)

            back = by_rows(back1, 64, dn1, xhat1[gs, :], fgrad[gs, :])
            fgrad[gs, :] = back[0]
            d_norm[16:24, :] += fold8(back[1])
            d_norm[24:32, :] += fold8(back[2])

    norm1_back(4, 8)
    arb.step(1)
    grad_rows(1)
    send_ig.start()
    norm1_back(0, 4)
    sums = jnp.sum(d_norm[16:32, :].reshape(2, 8, CP), axis=1)
    sums = jnp.concatenate([sums[:, 0:128], sums[:, 128:256], jnp.zeros((4, 128), f32)], axis=0)
    ard.begin(sums)
    ara.step(4)
    arc.step(3)
    conv_rows(4, 8)
    arb.step(2)
    ard.step(0)
    conv_rows(8, 16)
    arc.step(4)
    ard.step(1)
    ara.step(5)
    send_more.wait()
    conv_rows(0, 4)
    store_res = pltpu.make_async_copy(io1.at[pl.ds(0, 16)], res_out, lsem.at[2])
    store_res.start()
    grad_rows(0)
    store_ig = pltpu.make_async_copy(ig_rows.at[pl.ds(0, 12)], ig_out.at[pl.ds(4, 12)], lsem.at[3])
    store_ig.start()
    arb.step(3)
    ara.step(6)
    ard.step(2)
    d_out[...] = dd_sums[3]
    arc.step(5)
    arb.step(5)
    arc.step(6)
    arb.step(6)
    send_ig.wait()
    store_res.wait()
    store_ig.wait()


def finish_kernel(
    a_ref, b_ref, c_ref, d_ref, o_n1g, o_n1b, o_qkv, o_qvb, o_table, o_proj, o_pb, o_n2g, o_n2b, o_fc1, o_f1b, o_fc2t,
    o_f2b, o_conv, o_cb,
):
    def block(ref, at, rows=CR):
        return ref[at : at + rows, :].astype(f32)

    def halves(v):
        return v, pltpu.roll(v, 64, 1)

    tails = []
    for n in range(5):
        tails += halves(block(c_ref, C_MIX + n * CR))
    for a in range(3):
        for b in range(3):
            v = jnp.concatenate([block(c_ref, (a * 3 + b) * CR), tails[a * 3 + b]], axis=1)
            o_conv[a, b] = v[0:C, 0:C]
            if a == 1 and b == 1:
                o_cb[...] = v[C : C + 1, 0:C].reshape(C)
    fc1 = [block(c_ref, C_FC1), block(c_ref, C_FC1 + CR), block(a_ref, 0)]
    fc1 = jnp.concatenate(fc1, axis=1)
    o_fc1[...] = fc1[0:C, 0:HID]
    o_f1b[...] = fc1[C : C + 1, 0:HID].reshape(HID)
    fc2 = jnp.concatenate([block(a_ref, (n + 1) * CR) for n in range(3)], axis=1)
    o_fc2t[...] = fc2[0:C, 0:HID]
    proj = jnp.concatenate([block(a_ref, 4 * CR), tails[9]], axis=1)
    for h in range(HEADS):
        at = h * HP_DIM
        o_proj[h * HEAD_DIM : (h + 1) * HEAD_DIM, :] = proj[at : at + HEAD_DIM, 0:C]
    o_pb[...] = proj[HEAD_DIM : HEAD_DIM + 1, 0:C].reshape(C)
    wide = lax.broadcasted_iota(jnp.int32, (CP, CP), 0)
    dense = lax.broadcasted_iota(jnp.int32, (CP, CP), 1)
    heads_out = (wide == dense + lax.div(dense, HEAD_DIM) * (HP_DIM - HEAD_DIM)) & (dense < C)
    heads_out = heads_out.astype(bf16)
    rest = halves(block(b_ref, 3 * CR)) + halves(block(b_ref, 4 * CR))
    for n in range(3):
        v = jnp.concatenate([block(b_ref, n * CR), rest[n]], axis=1).astype(bf16)
        v = dot(v, heads_out)
        o_qkv[:, n * C : (n + 1) * C] = v[0:C, 0:C]
        if n != 1:
            o_qvb[n // 2 * C : (n // 2 + 1) * C] = v[C : C + 1, 0:C].reshape(C)
    small = jnp.concatenate([block(b_ref, B_SMALL, 16), block(b_ref, B_SMALL + 16, 16)], axis=1)
    o_table[...] = small[0:HEADS, 0 : o_table.shape[1]]
    for n, ref in ((0, o_n1g), (1, o_n1b)):
        v = jnp.concatenate([d_ref[n : n + 1, :], d_ref[n + 2 : n + 3, :]], axis=1)
        ref[...] = v[:, 0:C].reshape(C)
    for n, ref in ((8, o_n2g), (9, o_n2b), (12, o_f2b)):
        ref[...] = small[n : n + 1, 0:C].reshape(C)


def score_terms(table, extra):
    table = jnp.concatenate([table * LOG2E, jnp.zeros((2, table.shape[1]), f32)], axis=0)
    table = jnp.concatenate([table, jnp.zeros((8, CP - table.shape[1]), f32)], axis=1)
    shifted = [pltpu.roll(table, x, 1) if x else table for x in range(WIN)]
    row = lax.broadcasted_iota(jnp.int32, (AREA, CP), 0)
    lane = lax.broadcasted_iota(jnp.int32, (AREA, CP), 1)
    put = (lane == row + (row >> 3) * (WIN - 1)).astype(bf16)
    shape = (AREA, AREA)
    j = lax.broadcasted_iota(jnp.int32, shape, 0)
    i = lax.broadcasted_iota(jnp.int32, shape, 1)
    rows_differ = ((j >> 5) & 1) != ((i >> 5) & 1)
    cols_differ = ((j >> 2) & 1) != ((i >> 2) & 1)
    masks = [None, cols_differ, rows_differ, rows_differ | cols_differ]
    for h in range(HEADS):
        base = jnp.concatenate([t[h : h + 1] for t in shifted], axis=0)
        wide = jnp.concatenate(
            [pltpu.roll(base, CP - (112 - 15 * y), 1) for y in range(WIN)], axis=0
        )
        high = wide.astype(bf16)
        rest = wide - high.astype(f32)
        mid = rest.astype(bf16)
        low = (rest - mid.astype(f32)).astype(bf16)
        term = dot(high, put, 1, 1) + dot(mid, put, 1, 1) + dot(low, put, 1, 1)
        for n, mask in enumerate(masks):
            value = term if mask is None else term + jnp.where(mask, -100.0 * LOG2E, 0.0)
            extra[n, :, h * AREA : (h + 1) * AREA] = value


def table_sum(d_rel):
    row = lax.broadcasted_iota(jnp.int32, (AREA, CP), 0)
    lane = lax.broadcasted_iota(jnp.int32, (AREA, CP), 1)
    put = (lane == row + lax.div(row, WIN) * (WIN - 1)).astype(bf16)
    heads = []
    for h in range(HEADS):
        v = d_rel[:, h * AREA : (h + 1) * AREA]
        v1 = v.astype(bf16)
        v2 = (v - v1.astype(f32)).astype(bf16)
        wide = dot(v1, put) + dot(v2, put)
        total = None
        for y in range(WIN):
            part = pltpu.roll(wide[y * WIN : (y + 1) * WIN, :], 112 - 15 * y, 1)
            total = part if total is None else total + part
        heads.append(total)
    out = None
    for x in range(WIN):
        rows = jnp.concatenate([t[x : x + 1] for t in heads] + [jnp.zeros((2, CP), f32)], axis=0)
        rows = pltpu.roll(rows, CP - x, 1) if x else rows
        out = rows if out is None else out + rows
    return out


VM = pl.BlockSpec(memory_space=pltpu.VMEM)
SM = pl.BlockSpec(memory_space=pltpu.SMEM)
HB = pl.BlockSpec(memory_space=pl.ANY)


def up_to(n, m):
    return (n + m - 1) // m * m


def run_layer(stripes, imgs, *operands):
    S = jax.ShapeDtypeStruct
    V = pltpu.VMEM
    chips = stripes // 2
    dma = pltpu.SemaphoreType.DMA
    sems = 2 * (chips + imgs - 1)
    pieces, splits, buffers, outs = [], [], [], []
    for used, zsplit in ((A_USED, True), (B_USED, False), (C_USED, True)):
        zsplit = zsplit and stripes * imgs * 16 <= 2 * used
        splits.append(zsplit)
        parts = stripes * imgs if zsplit else stripes
        piece = up_to(-(-used // parts), 16)
        group = piece * imgs if zsplit else piece
        pieces.append(piece)
        outs.append(S((stripes * group, 128), bf16))
        buffers += [
            V((stripes * group, 128), bf16),
            V((chips * group, 128), bf16),
            V(((chips - 1) * group, 128), bf16),
            V(((imgs - 1) * piece, 128), bf16),
        ]
    return pl.pallas_call(
        functools.partial(layer_kernel, chips, imgs, tuple(pieces), tuple(splits)),
        out_shape=(S((16, 256, C), bf16), S((16, 256, C), bf16), *outs, S((8, 128), f32)),
        in_specs=[SM, HB, HB] + [VM] * 15,
        out_specs=[HB] * 2 + [VM] * 4,
        scratch_shapes=[
            V((CP, 3 * CP), bf16),
            V((CP, CP), bf16),
            V((CP, HP), bf16),
            V((CP, HP), bf16),
            V((3, CP, 3 * CP), bf16),
            V((16, 3 * CP), f32),
            V((4, AREA, HI), f32),
            V((CR, 3 * CP), f32),
            V((CR, CP), f32),
            V((CR, HP), f32),
            V((CR, HP), f32),
            V((3, CR, 3 * CP), f32),
            V((40, CP), f32),
            V((AREA, HI), f32),
            V((21, 256, C), bf16),
            V((20, 256, C), bf16),
            V((8, 256, CP), f32),
            V((8, 256, CP), f32),
            V((20 * 256, 3 * CP), bf16),
            V((24 * 256, CP), bf16),
            V((4096, CP), bf16),
            V((4096, CP), bf16),
            V((4096, 3 * CP), bf16),
            V((4096, HI), bf16),
            V((512, CP), bf16),
            V((2048, CP), f32),
            V((4096, CP), f32),
            V((4096, CP), bf16),
            V((16, 256, C), bf16),
            V((WIN, WIN, CP), f32),
            V((128, 128), bf16),
            V((16 * C, 128), f32),
            V((544, CP), f32),
            *buffers,
            V((4, 8, 128), f32),
            V((chips + imgs - 1, 8, 128), f32),
            dma((4,)),
            dma((6,)),
            dma((6,)),
        ]
        + [dma((sems,))] * 6
        + [dma((chips + imgs - 1,))] * 2,
        compiler_params=pltpu.CompilerParams(
            vmem_limit_bytes=63 * 1024 * 1024, collective_id=0, has_side_effects=True
        ),
        name="layer",
    )(*operands)


def run_finish(a, b, c, d, table):
    S = jax.ShapeDtypeStruct
    return pl.pallas_call(
        finish_kernel,
        out_shape=(
            S((C,), f32),
            S((C,), f32),
            S((C, 3 * C), f32),
            S((2 * C,), f32),
            S((HEADS, table), f32),
            S((C, C), f32),
            S((C,), f32),
            S((C,), f32),
            S((C,), f32),
            S((C, HID), f32),
            S((HID,), f32),
            S((C, HID), f32),
            S((C,), f32),
            S((3, 3, C, C), f32),
            S((C,), f32),
        ),
        compiler_params=pltpu.CompilerParams(vmem_limit_bytes=32 * 1024 * 1024),
        name="finish",
    )(a, b, c, d)


def on_device(
    images, widths, norm1_gain, norm1_bias, qkv_weight, qv_bias, bias_table, proj_weight, proj_bias,
    norm2_gain, norm2_bias, fc1_weight, fc1_bias, fc2_weight, fc2_bias, conv_weight, conv_bias, cotangent,
):
    count, rows_here, width, chans = images.shape
    img, cot = [
        v.reshape(rows_here, width, chans).transpose(2, 0, 1).reshape(chans * rows_here, width)
        for v in (images, cotangent)
    ]
    scal = lax.div(widths, WIN)
    res, ig, a, b, c, d = run_layer(
        lax.axis_size("rows"), lax.axis_size("imgs"),
        scal, img, cot, qkv_weight, proj_weight, fc1_weight, fc2_weight.T, conv_weight, bias_table.T,
        norm1_gain, norm1_bias, qv_bias, proj_bias, norm2_gain, norm2_bias, fc1_bias, fc2_bias, conv_bias,
    )
    grads = list(run_finish(a, b, c, d, bias_table.shape[0]))
    grads[4] = grads[4].T
    grads[11] = grads[11].T
    return (res[None], ig[None], *grads)


def solution(mesh):
    big = P("imgs", "rows", None, None)
    in_specs = (big, P("imgs")) + (P(),) * 15 + (big,)
    out_specs = (big, big) + (P(),) * 15
    return jax.shard_map(
        on_device, mesh=mesh, in_specs=in_specs, out_specs=out_specs, check_vma=False
    )
```

```python
import functools

import jax
import jax.numpy as jnp
import numpy as np
from jax import lax
from jax.experimental import pallas as pl
from jax.experimental.pallas import tpu as pltpu
from jax.sharding import PartitionSpec as P

HEADS = 6
HEAD_DIM = 30
WIN = 8
SHIFT = 4
C = 180
CP = 256
HID = 360
HP = 384
AREA = WIN * WIN
HI = HEADS * AREA
LOG2E = 1.4426950408889634
SCALE = HEAD_DIM ** (-0.5)

CR = 192
A_USED = 5 * CR
B_SMALL = 5 * CR
B_USED = B_SMALL + 32
C_MIX = 9 * CR
C_FC1 = C_MIX + 5 * CR
C_USED = C_FC1 + 2 * CR

f32 = jnp.float32
bf16 = jnp.bfloat16


def dot(a, b, ca=1, cb=0):
    return lax.dot_general(a, b, (((ca,), (cb,)), ((), ())), preferred_element_type=f32)


def lanes(shape):
    return lax.broadcasted_iota(jnp.int32, shape, len(shape) - 1)


def rows_of(shape):
    return lax.broadcasted_iota(jnp.int32, shape, len(shape) - 2)


def ln_fwd(x, gain, bias):
    real = (lanes((1, CP)) < C).astype(f32)
    mean = jnp.sum(x, axis=-1, keepdims=True) * (1.0 / C)
    xc = (x - mean) * real
    var = jnp.sum(xc * xc, axis=-1, keepdims=True) * (1.0 / C)
    rstd = lax.rsqrt(var + 1e-05)
    xhat = xc * rstd
    return xhat, rstd, xhat * gain + bias


def with_rstd(xhat, rstd):
    high = rstd.astype(bf16).astype(f32)
    lane = lanes((1, CP))
    return jnp.where(lane == 200, high, jnp.where(lane == 201, rstd - high, xhat))


def ln_bwd(dy, xhat, rstd, gain):
    a = dy * gain
    m1 = jnp.sum(a, axis=-1, keepdims=True) * (1.0 / C)
    m2 = jnp.sum(a * xhat, axis=-1, keepdims=True) * (1.0 / C)
    return rstd * (a - m1 - xhat * m2)


def gelu_pair(h):
    z = jnp.abs(h) * 0.7071067811865476
    d = 1.0 + 0.3275911 * z
    t = pl.reciprocal(d, approx=True)
    t = t * (2.0 - d * t)
    e = jnp.exp2(h * h * (-0.5 * LOG2E))
    poly = t * (
        0.254829592 + t * (-0.284496736 + t * (1.421413741 + t * (-1.453152027 + t * 1.061405429)))
    )
    q = 0.5 * poly * e
    phi = jnp.where(h >= 0, 1.0 - q, q)
    return h * phi, phi + h * (e * 0.3989422804014327)


def fold8(v):
    return jnp.sum(v.reshape(v.shape[0] // 8, 8, v.shape[1]), axis=0)


HP_DIM = 32


def by_rows(f, step, *arrays):
    rows = arrays[0].shape[0]
    parts = [f(*[a[i : i + step] for a in arrays]) for i in range(0, rows, step)]
    if not isinstance(parts[0], tuple):
        return jnp.concatenate(parts, axis=0)
    return tuple(jnp.concatenate(p, axis=0) for p in zip(*parts))


def added(values):
    return functools.reduce(jnp.add, values)


def head_mask(h):
    ln = lanes((1, 128))
    return (ln >= h * HP_DIM) & (ln < (h + 1) * HP_DIM)


def spread_heads(v, count):
    return jnp.concatenate(
        [jnp.where(head_mask(h), v, jnp.zeros_like(v)) for h in range(count)], axis=0
    )


def gather_heads(v, count):
    out = jnp.where(head_mask(0), v[:AREA], 0.0)
    for h in range(1, count):
        out = jnp.where(head_mask(h), v[h * AREA : (h + 1) * AREA], out)
    return out


GROUPS = ((0, 4), (4, 2))


def column_masks(width):
    return rows_of((256, CP)) < width


class SmallAllReduce:
    def __init__(self, sums, slots, ssem, rsem, chips, imgs):
        self.sums, self.ssem, self.rsem = [sums.at[n] for n in range(4)], ssem, rsem
        rows, z = lax.axis_index("rows"), lax.axis_index("imgs")
        core, chip = lax.rem(rows, 2), lax.div(rows, 2)
        self.stages = [
            [{"rows": chip * 2 + 1 - core}],
            [{"rows": lax.rem(chip + d, chips) * 2 + core} for d in range(1, chips)],
            [{"imgs": lax.rem(z + d, imgs)} for d in range(1, imgs)],
        ]
        self.first = [0, 1, chips]
        self.slots = slots

    def copies(self, n):
        return [
            pltpu.make_async_remote_copy(
                src_ref=self.sums[n],
                dst_ref=self.slots.at[self.first[n] + d],
                send_sem=self.ssem.at[self.first[n] + d],
                recv_sem=self.rsem.at[self.first[n] + d],
                device_id=to,
                device_id_type=pl.DeviceIdType.MESH,
            )
            for d, to in enumerate(self.stages[n])
        ]

    def begin(self, value):
        self.sums[0][...] = value
        for c in self.copies(0):
            c.start()

    def step(self, n):
        value = self.sums[n][...]
        for d, c in enumerate(self.copies(n)):
            c.wait()
            value += self.slots[self.first[n] + d]
        self.sums[n + 1][...] = value
        if n < 2:
            for c in self.copies(n + 1):
                c.start()


TURNS = ((0, (("a", 1),)), (1, (("c", 1),)), (4, (("a", 2),)), (7, (("c", 2),)))


class AllReduce:
    def __init__(self, buf, out, r1, r2, r3, ssem, rsem, pr, chips, imgs, zsplit):
        self.buf, self.out, self.r1, self.r2, self.r3 = buf, out, r1, r2, r3
        self.ssem, self.rsem, self.chips, self.imgs = ssem, rsem, chips, imgs
        self.zsplit = zsplit
        rows = lax.axis_index("rows")
        self.core = lax.rem(rows, 2)
        self.chip = lax.div(rows, 2)
        self.z = lax.axis_index("imgs")
        self.piece = pr
        self.group = pr * imgs if zsplit else pr
        self.half = self.group * chips
        self.used = 0

    def copy(self, src, dst, device, n):
        return pltpu.make_async_remote_copy(
            src_ref=src,
            dst_ref=dst,
            send_sem=self.ssem.at[n],
            recv_sem=self.rsem.at[n],
            device_id=device,
            device_id_type=pl.DeviceIdType.MESH,
        )

    def rows(self, ref, start, size):
        return ref.at[pl.ds(pl.multiple_of(start, 16), size)]

    def base_half(self, core):
        return core * self.half

    def base_group(self, chip):
        return self.core * self.half + chip * self.group

    def base_piece(self, z):
        return self.base_group(self.chip) + (z * self.piece if self.zsplit else 0)

    def core_copy(self, ref, dst, n, gather):
        side = self.core if gather else 1 - self.core
        src = self.rows(ref, self.base_half(side), self.half)
        dst = src if dst is None else dst
        return [self.copy(src, dst, {"rows": self.chip * 2 + 1 - self.core}, n)]

    def chip_copies(self, ref, dst, n, gather):
        out = []
        for d in range(1, self.chips):
            to = lax.rem(self.chip + d, self.chips)
            src = self.rows(ref, self.base_group(self.chip if gather else to), self.group)
            to_ref = src if gather else dst.at[pl.ds((d - 1) * self.group, self.group)]
            out.append(self.copy(src, to_ref, {"rows": to * 2 + self.core}, n + d - 1))
        return out

    def img_copies(self, ref, dst, n, gather):
        out = []
        for d in range(1, self.imgs):
            to = lax.rem(self.z + d, self.imgs)
            src = self.rows(ref, self.base_piece(self.z if gather else to), self.piece)
            to_ref = src if gather else dst.at[pl.ds((d - 1) * self.piece, self.piece)]
            out.append(self.copy(src, to_ref, {"imgs": to}, n + d - 1))
        return out

    def start(self, copies):
        for c in copies:
            c.start()
        return copies

    def wait(self, copies):
        for c in copies:
            c.wait()

    def add(self, base, size, extra, count, stride, target):
        step = min(size, 64)
        while size % step:
            step -= 16

        @pl.loop(0, size // step)
        def _(i):
            at = pl.ds(pl.multiple_of(base + i * step, 16), step)
            total = self.buf[at, :].astype(f32)
            for d in range(count):
                total += extra[pl.ds(pl.multiple_of(d * stride + i * step, 16), step), :].astype(f32)
            target[at, :] = total.astype(bf16)

    def step(self, k):
        n2 = 1
        n3 = n2 + self.chips - 1
        n4 = n3 + self.imgs - 1
        n5 = n4 + self.imgs - 1
        n6 = n5 + self.chips - 1
        first = lambda: self.core_copy(self.buf, self.r1, 0, False)
        second = lambda: self.chip_copies(self.buf, self.r2, n2, False)
        third = lambda: self.img_copies(self.buf, self.r3, n3, False)
        fourth = lambda: self.img_copies(self.out, None, n4, True) if self.zsplit else []
        fifth = lambda: self.chip_copies(self.out, None, n5, True)
        sixth = lambda: self.core_copy(self.out, None, n6, True)
        if k == 0:
            self.start(first())
        elif k == 1:
            self.wait(first())
            self.add(self.base_half(self.core), self.half, self.r1, 1, 0, self.buf)
            self.start(second())
        elif k == 2:
            self.wait(second())
            self.add(
                self.base_group(self.chip), self.group, self.r2, self.chips - 1, self.group, self.buf
            )
            self.start(third())
        elif k == 3:
            self.wait(third())
            self.add(
                self.base_piece(self.z), self.piece, self.r3, self.imgs - 1, self.piece, self.out
            )
            self.start(fourth() if self.zsplit else fifth())
        elif k == 4:
            if self.zsplit:
                self.wait(fourth())
                self.start(fifth())
        elif k == 5:
            self.wait(fifth())
            self.start(sixth())
        elif k == 6:
            self.wait(sixth())


def all_reduce_sems(chips, imgs):
    return 2 * (1 + chips - 1 + imgs - 1)


def layer_kernel(
    chips,
    imgs,
    pieces,
    splits,
    scal,
    img,
    cot,
    r_qkv,
    r_proj,
    r_fc1,
    r_fc2t,
    r_conv,
    r_table,
    r_n1g,
    r_n1b,
    r_qvb,
    r_pb,
    r_n2g,
    r_n2b,
    r_f1b,
    r_f2b,
    r_cb,
    res_out,
    ig_out,
    a_out,
    b_out,
    c_out,
    d_out,
    wqkv,
    wproj,
    wfc1,
    wfc2t,
    wconv,
    vecs,
    extra,
    d_qkv,
    d_proj,
    d_fc1,
    d_fc2,
    d_conv,
    d_norm,
    d_rel,
    io1,
    io2,
    xband,
    gband,
    gcat,
    llbuf,
    xhat1,
    normed,
    qkv,
    probs,
    mixed,
    winf,
    fgrad,
    do_buf,
    ig_rows,
    edge,
    tmp_eye,
    eye_c,
    planes,
    tmp,
    a_buf,
    a_r1,
    a_r2,
    a_r3,
    b_buf,
    b_r1,
    b_r2,
    b_r3,
    c_buf,
    c_r1,
    c_r2,
    c_r3,
    dd_sums,
    dd_slots,
    lsem,
    hs,
    hr,
    a_s,
    a_r,
    b_s,
    b_r,
    c_s,
    c_r,
    dd_s,
    dd_r,
):
    stripes = 2 * chips
    rank = lax.axis_index("rows")
    core = lax.rem(rank, 2)
    up = lax.rem(rank + stripes - 1, stripes)
    down = lax.rem(rank + 1, stripes)
    pa, pb, pc = pieces
    ara = AllReduce(a_buf, a_out, a_r1, a_r2, a_r3, a_s, a_r, pa, chips, imgs, splits[0])
    arb = AllReduce(b_buf, b_out, b_r1, b_r2, b_r3, b_s, b_r, pb, chips, imgs, splits[1])
    arc = AllReduce(c_buf, c_out, c_r1, c_r2, c_r3, c_s, c_r, pc, chips, imgs, splits[2])

    ard = SmallAllReduce(dd_sums, dd_slots, dd_s, dd_r, chips, imgs)

    flat = C * 16
    load_cot = pltpu.make_async_copy(cot, qkv.at[pl.ds(0, flat), pl.ds(CP, CP)], lsem.at[0])
    load_img = pltpu.make_async_copy(img, qkv.at[pl.ds(0, flat), pl.ds(0, CP)], lsem.at[1])
    load_cot.start()
    load_img.start()

    barrier = pltpu.get_barrier_semaphore()
    peers = [{"rows": up}, {"rows": down}]
    peers += [{"rows": lax.rem(rank + 2 * d, stripes)} for d in range(1, chips)]
    peers += [{"imgs": lax.rem(ara.z + d, imgs)} for d in range(1, imgs)]
    for peer in peers:
        pl.semaphore_signal(barrier, inc=1, device_id=peer, device_id_type=pl.DeviceIdType.MESH)

    def remote(src, dst, to, n):
        return pltpu.make_async_remote_copy(
            src_ref=src,
            dst_ref=dst,
            send_sem=hs.at[n],
            recv_sem=hr.at[n],
            device_id={"rows": to},
            device_id_type=pl.DeviceIdType.MESH,
        )

    send_img = remote(io2.at[pl.ds(0, 4)], io2.at[pl.ds(16, 4)], up, 0)
    send_cot = remote(io1.at[pl.ds(0, 5)], io1.at[pl.ds(16, 5)], up, 1)
    nb = scal[0]
    width = nb * WIN
    is_last = rank == stripes - 1
    joined = jnp.where(is_last, 0.0, 1.0)
    NW = 256 // WIN
    RM = 256

    def vec(i, n):
        return vecs[i : i + 1, 0:n]

    def row_at(pos, count=1):
        return pl.ds(pl.multiple_of(pos * 256, 256), count * 256)

    tmp[...] = jnp.zeros_like(tmp)
    for ref in (d_qkv, d_proj, d_fc1, d_fc2, d_conv, d_norm, d_rel):
        ref[...] = jnp.zeros_like(ref)
    for ref, size in ((a_buf, A_USED), (b_buf, B_USED), (c_buf, C_USED)):
        if ref.shape[0] > size:
            ref[size:, :] = jnp.zeros((ref.shape[0] - size, 128), bf16)

    col_in = rows_of((256, C)) < width
    col_in_p = rows_of((256, CP)) < width

    def put_g(pos, row, flag):
        g = jnp.where(col_in, row.astype(f32), 0.0) * flag
        tmp[8:264, 0:C] = g
        at = row_at(pos)
        gcat[at, 0:CP] = tmp[9:265, :].astype(bf16)
        gcat[at, CP : 2 * CP] = tmp[8:264, :].astype(bf16)
        gcat[at, 2 * CP : 3 * CP] = tmp[7:263, :].astype(bf16)

    def iota(shape, dim):
        return lax.broadcasted_iota(jnp.int32, shape, dim)

    def padded(v):
        return jnp.concatenate([v.astype(f32), jnp.zeros((CR - C, v.shape[1]), f32)], axis=0).astype(bf16)

    for ref in (wqkv, wproj, wfc1, wfc2t, wconv, vecs):
        ref[...] = jnp.zeros_like(ref)
    part = iota((3 * C, 3 * CP), 1)
    lane = part & (CP - 1)
    place = (part >> 8) * C + (lane >> 5) * HEAD_DIM + (lane & 31)
    used = ((lane & 31) < HEAD_DIM) & (lane < HEADS * HP_DIM)
    spread = (used & (iota((3 * C, 3 * CP), 0) == place)).astype(bf16)
    wqkv[0:CR, :] = padded(dot(r_qkv[...], spread))
    lane = iota((CP, C), 0)
    place = (lane >> 5) * HEAD_DIM + (lane & 31)
    used = ((lane & 31) < HEAD_DIM) & (lane < HEADS * HP_DIM)
    wproj[:, 0:C] = dot((used & (iota((CP, C), 1) == place)).astype(bf16), r_proj[...]).astype(bf16)
    wfc1[0:CR, 0:HID] = padded(r_fc1[...])
    wfc2t[0:CR, 0:HID] = padded(r_fc2t[...])
    for a in range(3):
        for b in range(3):
            wconv[a, 0:CR, b * CP : b * CP + C] = padded(r_conv[a, b])
    for n, ref in ((0, r_n1g), (1, r_n1b), (3, r_pb), (4, r_n2g), (5, r_n2b), (6, r_f1b), (7, r_f2b), (8, r_cb)):
        vecs[n : n + 1, 0 : ref.shape[0]] = ref[...].reshape(1, ref.shape[0])
    for n in (1, 5, 7):
        vecs[n : n + 1, C : C + 1] = jnp.ones((1, 1), f32)
    qvb = r_qvb[...].reshape(1, 2 * C)
    for h in range(HEADS):
        at = h * HP_DIM
        vecs[2:3, at : at + HEAD_DIM] = qvb[:, h * HEAD_DIM : (h + 1) * HEAD_DIM]
        vecs[2:3, 2 * CP + at : 2 * CP + at + HEAD_DIM] = qvb[
            :, C + h * HEAD_DIM : C + (h + 1) * HEAD_DIM
        ]
    score_terms(r_table[...], extra)

    tmp_eye[...] = (iota((128, 128), 0) == iota((128, 128), 1)).astype(bf16)

    eye_c[...] = (iota((C, C), 0) == iota((C, C), 1)).astype(bf16)

    def to_rows(lane0, dst):
        for m in range(2):
            half = slice(m * 128, (m + 1) * 128)

            @pl.loop(0, flat // 96, unroll=2)
            def _(n):
                at = pl.ds(pl.multiple_of(n * 96, 96), 96)
                planes[at, :] = qkv[at, lane0 + m * 128 : lane0 + (m + 1) * 128].astype(f32)

            for r in range(16):
                x = planes[pl.ds(r, C, stride=16), :].astype(bf16)
                dst[r, half, :] = dot(tmp_eye[...], x, 1, 1).astype(bf16)

    load_cot.wait()
    to_rows(CP, io1)
    load_img.wait()
    to_rows(0, io2)

    @pl.loop(0, 13)
    def _(r):
        put_g(r, io1[r + 3], 1.0)

    put_g(14, io1[15], joined)
    pl.semaphore_wait(barrier, len(peers))
    send_cot.start()
    send_img.start()

    pos_hi = rows_of((1, WIN, CP)) >= SHIFT

    def rolled(a, b):
        t = jnp.where(pos_hi, a, b)
        return pltpu.roll(t, SHIFT, 1)

    def to_win(ref, k):
        nxt = jnp.minimum(k + 1, NW - 1)
        a = ref[:, pl.ds(pl.multiple_of(k * WIN, WIN), WIN), :]
        b = ref[:, pl.ds(pl.multiple_of(nxt * WIN, WIN), WIN), :]
        b = jnp.where(k == nb - 1, ref[:, 0:WIN, :], b)
        return rolled(a, b).reshape(AREA, CP)

    def from_win(ref, band):
        def block(k):
            at = pl.multiple_of((band * NW + k) * AREA, AREA)
            return ref[pl.ds(at, AREA), :].reshape(WIN, WIN, CP)

        @pl.loop(0, NW, unroll=4)
        def _(k):
            b = block(k)
            edge[...] = jnp.where(k == nb - 1, b, edge[...])
            xband[:, pl.ds(pl.multiple_of(k * WIN, WIN), WIN), :] = rolled(
                block(jnp.maximum(k - 1, 0)), b
            )

        xband[:, 0:WIN, :] = rolled(edge[...], block(0))

    def win_rows(w):
        return pl.ds(pl.multiple_of(w * AREA, AREA), AREA)

    send_up = remote(llbuf.at[pl.ds(5 * 256, 256)], llbuf.at[pl.ds(23 * 256, 256)], up, 2)

    @pl.loop(0, 2)
    def _(band):
        @pl.when(band == 1)
        def _():
            send_cot.wait()
            send_img.wait()
            put_g(13, io1[16], joined)

            @pl.loop(0, 5)
            def _(r):
                put_g(15 + r, io1[16 + r], 1.0)

        xband[:, :, 128:256] = jnp.zeros((8, 256, 128), f32)

        @pl.loop(0, 8)
        def _(y):
            xband[y, :, 0:C] = io2[band * 8 + y + 4].astype(f32)

        @pl.loop(0, 4)
        def _(y):
            r = band * 8 + 2 * y
            pos = r + 1 + jnp.where(r >= 12, 2, 0)
            acc = None
            for a in range(3):
                d = dot(gcat[row_at(pos + 1 - a, 2), :], wconv[a], 1, 1)
                acc = d if acc is None else acc + d
            for n in range(2):
                gband[2 * y + n] = jnp.where(col_in_p, acc[n * 256 : (n + 1) * 256], 0.0)

        @pl.loop(0, 4)
        def _(gg):
            g = band * 4 + gg
            k0 = gg * 8
            gs = pl.ds(pl.multiple_of(g * 512, 512), 512)

            xs = [to_win(xband, k0 + w) for w in range(8)]
            for w in range(8):
                winf[win_rows(gg * 8 + w), :] = xs[w]
                fgrad[win_rows(g * 8 + w), :] = to_win(gband, k0 + w)
                xhat, rs_, ln_out = ln_fwd(xs[w], vec(0, CP), vec(1, CP))
                xhat1[win_rows(g * 8 + w), :] = with_rstd(xhat, rs_).astype(bf16)
                normed[win_rows(g * 8 + w), :] = ln_out.astype(bf16)

            for n in range(3):
                sl = slice(n * CP, (n + 1) * CP)
                qkv[gs, sl] = (dot(normed[gs, :], wqkv[:, sl]) + vecs[2:3, sl]).astype(bf16)

            i = 0
            if True:
                which = jnp.where((band == 1) & is_last, 2, 0)
                jobs = []
                for w in range(8):
                    rs = win_rows(g * 8 + i * 8 + w)
                    edge_win = k0 + i * 8 + w == nb - 1
                    for n, (h0, count) in enumerate(GROUPS):
                        jobs.append((rs, w, edge_win, n, count, slice(h0 * AREA, (h0 + count) * AREA)))
                qs = [qkv[rs, n * 128 : (n + 1) * 128] for rs, w, ew, n, count, hl in jobs]
                ks = [qkv[rs, CP + n * 128 : CP + (n + 1) * 128] for rs, w, ew, n, count, hl in jobs]
                vs = [qkv[rs, 2 * CP + n * 128 : 2 * CP + (n + 1) * 128] for rs, w, ew, n, count, hl in jobs]
                ss = [dot(k, spread_heads(q, job[4]), 1, 1) for q, k, job in zip(qs, ks, jobs)]
                ps = []
                for s, (rs, w, ew, n, count, hl) in zip(ss, jobs):
                    more = jnp.where(ew, extra[which + 1, :, hl], extra[which, :, hl])
                    s = s * (SCALE * LOG2E) + more
                    top = jnp.max(s, axis=0, keepdims=True)
                    e = jnp.exp2(s - top)
                    total = jnp.sum(e, axis=0, keepdims=True)
                    ps.append((e * (1.0 / total)).astype(bf16))
                os = [gather_heads(dot(p, v, 0, 0), job[4]) for p, v, job in zip(ps, vs, jobs)]
                for p, o, (rs, w, ew, n, count, hl) in zip(ps, os, jobs):
                    probs[rs, hl] = p
                    if n == 0:
                        o = jnp.where(lanes((1, 128)) == HEAD_DIM, 1.0, o)
                    mixed[win_rows(i * 8 + w), n * 128 : (n + 1) * 128] = o.astype(bf16)

            parts = range(0, 512, 256)
            at_rows = [pl.ds(pl.multiple_of(g * 512 + r, 256), 256) for r in parts]
            in_band = [pl.ds(pl.multiple_of(gg * 512 + r, 256), 256) for r in parts]
            mixes = [mixed[r : r + 256, :] for r in parts]
            firsts = [dot(m, wproj[...]) + vec(3, CP) + winf[rs, :] for m, rs in zip(mixes, in_band)]

            def norm2(v):
                xhat, rs_, ln_out = ln_fwd(v, vec(4, CP), vec(5, CP))
                return xhat, rs_, ln_out.astype(bf16)

            def activate(v):
                ac, dg = gelu_pair(v + vec(6, HP))
                return jnp.where(lanes((1, HP)) == HID, 1.0, ac).astype(bf16), dg.astype(bf16)

            norms = [by_rows(norm2, 64, v) for v in firsts]
            n2s = [n[2] for n in norms]
            acts = [by_rows(activate, 64, dot(n2, wfc1[...])) for n2 in n2s]
            for fs, (ac, dg), rs in zip(firsts, acts, in_band):
                winf[rs, :] = fs + dot(ac, wfc2t[...], 1, 1) + vec(7, CP)
            lgs = [fgrad[rs, :] for rs in at_rows]
            mgs = [lg.astype(bf16) for lg in lgs]
            hgs = [
                (dot(mg, wfc2t[...]).astype(bf16).astype(f32) * dg.astype(f32)).astype(bf16)
                for mg, (ac, dg) in zip(mgs, acts)
            ]
            dns = [dot(hg, wfc1[...], 1, 1).astype(bf16) for hg in hgs]

            def back2(dn2, xh, rs_, lg):
                dn2 = dn2.astype(f32)
                fg = lg + ln_bwd(dn2, xh, rs_, vec(4, CP))
                return fg, fg.astype(bf16), fold8(dn2 * xh), fold8(dn2)

            backs = [
                by_rows(back2, 64, dn, n[0], n[1], lg) for dn, n, lg in zip(dns, norms, lgs)
            ]
            ats = [b[1] for b in backs]
            for b, rs in zip(backs, at_rows):
                fgrad[rs, :] = b[0]
                do_buf[rs, :] = dot(b[1], wproj[...], 1, 1).astype(bf16)
            d_norm[0:8, :] += added([fold8(b[2]) for b in backs])
            d_norm[8:16, :] += added([fold8(b[3]) for b in backs])
            join = lambda vs: jnp.concatenate(vs, axis=0)
            mg = join(mgs)
            d_fc2[...] += dot(mg[:, 0:CR], join([ac for ac, dg in acts]), 0, 0)
            d_norm[32:40, :] += fold8(mg.astype(f32))
            d_fc1[...] += dot(join(n2s)[:, 0:CR], join(hgs), 0, 0)
            d_proj[...] += dot(mixed[:, 0:CR], join(ats), 0, 0)

        from_win(winf, 0)

        @pl.loop(0, 8)
        def _(y):
            r = band * 8 + y
            pos = r + 5 + jnp.where(r >= 12, 2, 0)
            llbuf[row_at(pos), :] = jnp.where(col_in_p, xband[y], 0.0).astype(bf16)

        @pl.when(band == 0)
        def _():
            send_up.start()

    joined_low = joined.astype(bf16)
    llbuf[17 * 256 : 18 * 256, :] = llbuf[19 * 256 : 20 * 256, :] * joined_low
    llbuf[18 * 256 : 19 * 256, :] = llbuf[16 * 256 : 17 * 256, :] * joined_low
    send_down = remote(llbuf.at[pl.ds(22 * 256, 256)], llbuf.at[pl.ds(4 * 256, 256)], down, 3)
    send_more = remote(llbuf.at[pl.ds(18 * 256, 1024)], llbuf.at[pl.ds(0, 1024)], down, 4)
    send_down.start()

    def wgrad_rows(n):
        start = 1 + 4 * n + jnp.where(n == 3, 2, 0)
        gs = gcat[row_at(start, 4), :]
        for a in range(3):
            d_conv[a] += dot(llbuf[row_at(start + a + 3, 4), 0:CR], gs, 0, 0)

    low_lanes = lanes((1, 128)) < 64

    def mix(p, q):
        return jnp.where(low_lanes, p, pltpu.roll(q, 64, 1)).astype(bf16)

    a_buf[0:CR, :] = d_fc1[:, CP:HP].astype(bf16)
    for n in range(3):
        a_buf[(n + 1) * CR : (n + 2) * CR, :] = d_fc2[:, n * 128 : (n + 1) * 128].astype(bf16)
    a_buf[4 * CR : 5 * CR, :] = d_proj[:, 0:128].astype(bf16)
    ara.step(0)

    @pl.loop(1, 3)
    def _(n):
        wgrad_rows(n)

    send_up.wait()
    wgrad_rows(3)
    send_down.wait()
    wgrad_rows(0)

    tails = []
    for a in range(3):
        for b in range(3):
            at = (a * 3 + b) * CR
            c_buf[at : at + CR, :] = d_conv[a, :, b * CP : b * CP + 128].astype(bf16)
            tails.append((d_conv, a, slice(b * CP + 128, (b + 1) * CP)))
    tails = [ref[a, :, ln] for ref, a, ln in tails] + [d_proj[:, 128:256]]
    for n in range(5):
        at = C_MIX + n * CR
        c_buf[at : at + CR, :] = mix(tails[2 * n], tails[2 * n + 1])
    for n in range(2):
        at = C_FC1 + n * CR
        c_buf[at : at + CR, :] = d_fc1[:, n * 128 : (n + 1) * 128].astype(bf16)
    arc.step(0)

    def conv_rows(lo, hi):
        @pl.loop(lo // 2, hi // 2)
        def _(half):
            r = 2 * half
            acc = None
            for a in range(3):
                d = dot(llbuf[row_at(r + a, 2), :], wconv[a])
                acc = d if acc is None else acc + d
            for n in range(2):
                px = slice(n * 256, (n + 1) * 256)
                tmp[8:264, :] = acc[px, 0:CP]
                tmp[280:536, :] = acc[px, 2 * CP : 3 * CP]
                out = acc[px, CP : 2 * CP] + tmp[7:263, :] + tmp[281:537, :] + vec(8, CP)
                out = out[:, 0:C] + io2[r + n].astype(f32)
                io1[r + n] = jnp.where(col_in, out, 0.0).astype(bf16)

    def grad_rows(band):
        from_win(fgrad, band)

        @pl.loop(0, 8)
        def _(y):
            r = band * 8 + y
            pos = r + 1 + jnp.where(r >= 12, 2, 0)
            v = xband[y] + gcat[row_at(pos), CP : 2 * CP].astype(f32)
            ig_rows[r] = jnp.where(col_in_p, v, 0.0)[:, 0:C].astype(bf16)

    send_ig = remote(ig_rows.at[pl.ds(12, 4)], ig_rows.at[pl.ds(16, 4)], down, 5)

    @pl.loop(0, 8)
    def _(turn):
        g = lax.rem(turn + 4, 8)
        gs = pl.ds(pl.multiple_of(g * 512, 512), 512)

        i = 0
        if True:
            jobs = []
            for w in range(8):
                rs = win_rows(g * 8 + i * 8 + w)
                for n, (h0, count) in enumerate(GROUPS):
                    jobs.append((rs, n, count, slice(h0 * AREA, (h0 + count) * AREA)))
            qs = [qkv[rs, n * 128 : (n + 1) * 128] for rs, n, count, hl in jobs]
            ks = [qkv[rs, CP + n * 128 : CP + (n + 1) * 128] for rs, n, count, hl in jobs]
            vs = [qkv[rs, 2 * CP + n * 128 : 2 * CP + (n + 1) * 128] for rs, n, count, hl in jobs]
            dos = [spread_heads(do_buf[rs, n * 128 : (n + 1) * 128], count) for rs, n, count, hl in jobs]
            pbs = [probs[rs, hl] for rs, n, count, hl in jobs]
            dps = [dot(v, d, 1, 1) for v, d in zip(vs, dos)]
            dvs = [dot(p, d) for p, d in zip(pbs, dos)]
            dss = []
            for dp, pb in zip(dps, pbs):
                p = pb.astype(f32)
                dss.append((p * (dp - jnp.sum(p * dp, axis=0, keepdims=True))).astype(bf16))
            dks = [dot(ds, spread_heads(q, job[2])) * SCALE for ds, q, job in zip(dss, qs, jobs)]
            dqs = [gather_heads(dot(ds, k, 0, 0), job[2]) * SCALE for ds, k, job in zip(dss, ks, jobs)]
            for n, (h0, count) in enumerate(GROUPS):
                hl = slice(h0 * AREA, (h0 + count) * AREA)
                d_rel[:, hl] += functools.reduce(jnp.add, [d.astype(f32) for d in dss[n::2]])
            for dq, dk, dv, (rs, n, count, hl) in zip(dqs, dks, dvs, jobs):
                qkv[rs, n * 128 : (n + 1) * 128] = dq.astype(bf16)
                qkv[rs, CP + n * 128 : CP + (n + 1) * 128] = dk.astype(bf16)
                qkv[rs, 2 * CP + n * 128 : 2 * CP + (n + 1) * 128] = dv.astype(bf16)

        d_qkv[...] += dot(normed[gs, 0:CR], qkv[gs, :], 0, 0)

        @pl.when(turn == 5)
        def _():
            send_more.start()

        for at, steps in TURNS:

            @pl.when(turn == at)
            def _(steps=steps):
                for which, k in steps:
                    {"a": ara, "c": arc}[which].step(k)

    for n in range(3):
        b_buf[n * CR : (n + 1) * CR, :] = d_qkv[:, n * CP : n * CP + 128].astype(bf16)
    b_buf[3 * CR : 4 * CR, :] = mix(d_qkv[:, 128:256], d_qkv[:, CP + 128 : 2 * CP])
    b_buf[4 * CR : 5 * CR, :] = mix(d_qkv[:, 2 * CP + 128 : 3 * CP], d_qkv[:, 2 * CP + 128 : 3 * CP])
    sums = jnp.sum(d_norm[...].reshape(5, 8, CP), axis=1)
    small = jnp.concatenate([table_sum(d_rel[...]), sums, jnp.zeros((3, CP), f32)], axis=0)
    b_buf[B_SMALL : B_SMALL + 16, :] = small[:, 0:128].astype(bf16)
    b_buf[B_SMALL + 16 : B_SMALL + 32, :] = small[:, 128:256].astype(bf16)
    arb.step(0)
    ara.step(3)

    def norm1_back(lo, hi):
        @pl.loop(lo, hi)
        def _(g):
            gs = pl.ds(pl.multiple_of(g * 512, 512), 512)
            dn1 = dot(qkv[gs, :], wqkv[...], 1, 1).astype(bf16)

            def back1(dn, xhat, fg):
                dn, xhat = dn.astype(f32), xhat.astype(f32)
                out = fg + ln_bwd(dn, xhat, xhat[:, 200:201] + xhat[:, 201:202], vec(0, CP))
                return out, fold8(dn * xhat), fold8(dn)

            back = by_rows(back1, 64, dn1, xhat1[gs, :], fgrad[gs, :])
            fgrad[gs, :] = back[0]
            d_norm[16:24, :] += fold8(back[1])
            d_norm[24:32, :] += fold8(back[2])

    norm1_back(4, 8)
    arb.step(1)
    grad_rows(1)
    send_ig.start()
    norm1_back(0, 4)
    sums = jnp.sum(d_norm[16:32, :].reshape(2, 8, CP), axis=1)
    sums = jnp.concatenate([sums[:, 0:128], sums[:, 128:256], jnp.zeros((4, 128), f32)], axis=0)
    ard.begin(sums)
    ara.step(4)
    arc.step(3)
    def to_planes(src, lane0):
        for m in range(2):
            half = slice(m * 128, (m + 1) * 128)
            for i in range(16):
                planes[pl.ds(i, C, stride=16), :] = dot(eye_c[...], src(i)[half, :], 1, 1)

            @pl.loop(0, flat // 96, unroll=2)
            def _(n):
                at = pl.ds(pl.multiple_of(n * 96, 96), 96)
                qkv[at, lane0 + m * 128 : lane0 + (m + 1) * 128] = planes[at, :].astype(bf16)

    conv_rows(4, 8)
    arb.step(2)
    ard.step(0)
    conv_rows(8, 16)
    arc.step(4)
    ard.step(1)
    ara.step(5)
    send_more.wait()
    conv_rows(0, 4)
    to_planes(lambda i: io1[i], 0)
    store_res = pltpu.make_async_copy(qkv.at[pl.ds(0, flat), pl.ds(0, CP)], res_out, lsem.at[2])
    store_res.start()
    grad_rows(0)
    arb.step(3)
    ara.step(6)
    ard.step(2)
    d_out[...] = dd_sums[3]
    send_ig.wait()
    to_planes(lambda i: ig_rows[16 + i] if i < SHIFT else ig_rows[i - SHIFT], CP)
    store_ig = pltpu.make_async_copy(qkv.at[pl.ds(0, flat), pl.ds(CP, CP)], ig_out, lsem.at[3])
    store_ig.start()
    arc.step(5)
    arb.step(5)
    arc.step(6)
    arb.step(6)
    store_res.wait()
    store_ig.wait()


def finish_kernel(
    res_ref, ig_ref, a_hbm, b_hbm, c_hbm, d_ref, o_res, o_ig, o_n1g, o_n1b, o_qkv, o_qvb, o_table, o_proj, o_pb, o_n2g, o_n2b, o_fc1, o_f1b, o_fc2t,
    o_f2b, o_conv, o_cb, hold, a_ref, b_ref, c_ref, conv, sems, conv_sems,
):
    ins = [pltpu.make_async_copy(ref, hold.at[n], sems.at[n]) for n, ref in enumerate((res_ref, ig_ref))]
    moves = [pltpu.make_async_copy(hold.at[n], ref, sems.at[2 + n]) for n, ref in enumerate((o_res, o_ig))]
    sums = [
        pltpu.make_async_copy(src, dst, sems.at[4 + n])
        for n, (src, dst) in enumerate(((c_hbm, c_ref), (a_hbm, a_ref), (b_hbm, b_ref)))
    ]
    for m in sums + ins:
        m.start()
    sums[0].wait()

    def block(ref, at, rows=CR):
        return ref[at : at + rows, :].astype(f32)

    def halves(v):
        return v, pltpu.roll(v, 64, 1)

    tails = []
    for n in range(5):
        tails += halves(block(c_ref, C_MIX + n * CR))
    for a in range(3):
        for b in range(3):
            v = jnp.concatenate([block(c_ref, (a * 3 + b) * CR), tails[a * 3 + b]], axis=1)
            conv[a, b] = v[0:C, 0:C]
            moves.append(pltpu.make_async_copy(conv.at[a, b], o_conv.at[a, b], conv_sems.at[a * 3 + b]))
            moves[-1].start()
            if a == 1 and b == 1:
                o_cb[...] = v[C : C + 1, 0:C].reshape(C)
    sums[1].wait()
    sums[2].wait()
    for m, n in zip(ins, moves):
        m.wait()
        n.start()
    fc1 = [block(c_ref, C_FC1), block(c_ref, C_FC1 + CR), block(a_ref, 0)]
    fc1 = jnp.concatenate(fc1, axis=1)
    o_fc1[...] = fc1[0:C, 0:HID]
    o_f1b[...] = fc1[C : C + 1, 0:HID].reshape(HID)
    fc2 = jnp.concatenate([block(a_ref, (n + 1) * CR) for n in range(3)], axis=1)
    o_fc2t[...] = fc2[0:C, 0:HID]
    proj = jnp.concatenate([block(a_ref, 4 * CR), tails[9]], axis=1)
    for h in range(HEADS):
        at = h * HP_DIM
        o_proj[h * HEAD_DIM : (h + 1) * HEAD_DIM, :] = proj[at : at + HEAD_DIM, 0:C]
    o_pb[...] = proj[HEAD_DIM : HEAD_DIM + 1, 0:C].reshape(C)
    wide = lax.broadcasted_iota(jnp.int32, (CP, CP), 0)
    dense = lax.broadcasted_iota(jnp.int32, (CP, CP), 1)
    heads_out = (wide == dense + lax.div(dense, HEAD_DIM) * (HP_DIM - HEAD_DIM)) & (dense < C)
    heads_out = heads_out.astype(bf16)
    rest = halves(block(b_ref, 3 * CR)) + halves(block(b_ref, 4 * CR))
    for n in range(3):
        v = jnp.concatenate([block(b_ref, n * CR), rest[n]], axis=1).astype(bf16)
        v = dot(v, heads_out)
        o_qkv[:, n * C : (n + 1) * C] = v[0:C, 0:C]
        if n != 1:
            o_qvb[n // 2 * C : (n // 2 + 1) * C] = v[C : C + 1, 0:C].reshape(C)
    small = jnp.concatenate([block(b_ref, B_SMALL, 16), block(b_ref, B_SMALL + 16, 16)], axis=1)
    o_table[...] = small[0:HEADS, 0 : o_table.shape[1]]
    for n, ref in ((0, o_n1g), (1, o_n1b)):
        v = jnp.concatenate([d_ref[n : n + 1, :], d_ref[n + 2 : n + 3, :]], axis=1)
        ref[...] = v[:, 0:C].reshape(C)
    for n, ref in ((8, o_n2g), (9, o_n2b), (12, o_f2b)):
        ref[...] = small[n : n + 1, 0:C].reshape(C)
    for m in moves:
        m.wait()


def score_terms(table, extra):
    table = jnp.concatenate([table * LOG2E, jnp.zeros((2, table.shape[1]), f32)], axis=0)
    table = jnp.concatenate([table, jnp.zeros((8, CP - table.shape[1]), f32)], axis=1)
    shifted = [pltpu.roll(table, x, 1) if x else table for x in range(WIN)]
    row = lax.broadcasted_iota(jnp.int32, (AREA, CP), 0)
    lane = lax.broadcasted_iota(jnp.int32, (AREA, CP), 1)
    put = (lane == row + (row >> 3) * (WIN - 1)).astype(bf16)
    shape = (AREA, AREA)
    j = lax.broadcasted_iota(jnp.int32, shape, 0)
    i = lax.broadcasted_iota(jnp.int32, shape, 1)
    rows_differ = ((j >> 5) & 1) != ((i >> 5) & 1)
    cols_differ = ((j >> 2) & 1) != ((i >> 2) & 1)
    masks = [None, cols_differ, rows_differ, rows_differ | cols_differ]
    for h in range(HEADS):
        base = jnp.concatenate([t[h : h + 1] for t in shifted], axis=0)
        wide = jnp.concatenate(
            [pltpu.roll(base, CP - (112 - 15 * y), 1) for y in range(WIN)], axis=0
        )
        high = wide.astype(bf16)
        rest = wide - high.astype(f32)
        mid = rest.astype(bf16)
        low = (rest - mid.astype(f32)).astype(bf16)
        term = dot(high, put, 1, 1) + dot(mid, put, 1, 1) + dot(low, put, 1, 1)
        for n, mask in enumerate(masks):
            value = term if mask is None else term + jnp.where(mask, -100.0 * LOG2E, 0.0)
            extra[n, :, h * AREA : (h + 1) * AREA] = value


def table_sum(d_rel):
    row = lax.broadcasted_iota(jnp.int32, (AREA, CP), 0)
    lane = lax.broadcasted_iota(jnp.int32, (AREA, CP), 1)
    put = (lane == row + lax.div(row, WIN) * (WIN - 1)).astype(bf16)
    heads = []
    for h in range(HEADS):
        v = d_rel[:, h * AREA : (h + 1) * AREA]
        v1 = v.astype(bf16)
        v2 = (v - v1.astype(f32)).astype(bf16)
        wide = dot(v1, put) + dot(v2, put)
        total = None
        for y in range(WIN):
            part = pltpu.roll(wide[y * WIN : (y + 1) * WIN, :], 112 - 15 * y, 1)
            total = part if total is None else total + part
        heads.append(total)
    out = None
    for x in range(WIN):
        rows = jnp.concatenate([t[x : x + 1] for t in heads] + [jnp.zeros((2, CP), f32)], axis=0)
        rows = pltpu.roll(rows, CP - x, 1) if x else rows
        out = rows if out is None else out + rows
    return out


VM = pl.BlockSpec(memory_space=pltpu.VMEM)
SM = pl.BlockSpec(memory_space=pltpu.SMEM)
HB = pl.BlockSpec(memory_space=pl.ANY)


def up_to(n, m):
    return (n + m - 1) // m * m


def run_layer(stripes, imgs, *operands):
    S = jax.ShapeDtypeStruct
    V = pltpu.VMEM
    chips = stripes // 2
    dma = pltpu.SemaphoreType.DMA
    sems = 2 * (chips + imgs - 1)
    pieces, splits, buffers, outs = [], [], [], []
    for used, zsplit in ((A_USED, True), (B_USED, False), (C_USED, True)):
        zsplit = zsplit and stripes * imgs * 16 <= 2 * used
        splits.append(zsplit)
        parts = stripes * imgs if zsplit else stripes
        piece = up_to(-(-used // parts), 16)
        group = piece * imgs if zsplit else piece
        pieces.append(piece)
        outs.append(S((stripes * group, 128), bf16))
        buffers += [
            V((stripes * group, 128), bf16),
            V((chips * group, 128), bf16),
            V(((chips - 1) * group, 128), bf16),
            V(((imgs - 1) * piece, 128), bf16),
        ]
    return pl.pallas_call(
        functools.partial(layer_kernel, chips, imgs, tuple(pieces), tuple(splits)),
        out_shape=(S((16 * C, 256), bf16), S((16 * C, 256), bf16), *outs, S((8, 128), f32)),
        in_specs=[SM, HB, HB] + [VM] * 15,
        out_specs=[HB] * 2 + [VM] * 4,
        scratch_shapes=[
            V((CP, 3 * CP), bf16),
            V((CP, CP), bf16),
            V((CP, HP), bf16),
            V((CP, HP), bf16),
            V((3, CP, 3 * CP), bf16),
            V((16, 3 * CP), f32),
            V((4, AREA, HI), f32),
            V((CR, 3 * CP), f32),
            V((CR, CP), f32),
            V((CR, HP), f32),
            V((CR, HP), f32),
            V((3, CR, 3 * CP), f32),
            V((40, CP), f32),
            V((AREA, HI), f32),
            V((21, 256, C), bf16),
            V((20, 256, C), bf16),
            V((8, 256, CP), f32),
            V((8, 256, CP), f32),
            V((20 * 256, 3 * CP), bf16),
            V((24 * 256, CP), bf16),
            V((4096, CP), bf16),
            V((4096, CP), bf16),
            V((4096, 3 * CP), bf16),
            V((4096, HI), bf16),
            V((512, CP), bf16),
            V((2048, CP), f32),
            V((4096, CP), f32),
            V((4096, CP), bf16),
            V((20, 256, C), bf16),
            V((WIN, WIN, CP), f32),
            V((128, 128), bf16),
            V((C, C), bf16),
            V((16 * C, 128), f32),
            V((544, CP), f32),
            *buffers,
            V((4, 8, 128), f32),
            V((chips + imgs - 1, 8, 128), f32),
            dma((4,)),
            dma((6,)),
            dma((6,)),
        ]
        + [dma((sems,))] * 6
        + [dma((chips + imgs - 1,))] * 2,
        compiler_params=pltpu.CompilerParams(
            vmem_limit_bytes=63 * 1024 * 1024, collective_id=0, has_side_effects=True
        ),
        name="layer",
    )(*operands)


def run_finish(res, ig, a, b, c, d, table):
    S = jax.ShapeDtypeStruct
    return pl.pallas_call(
        finish_kernel,
        in_specs=[HB] * 5 + [VM],
        out_specs=(HB,) * 2 + (VM,) * 13 + (HB, VM),
        scratch_shapes=[
            pltpu.VMEM((2, *res.shape), bf16),
            *[pltpu.VMEM(v.shape, v.dtype) for v in (a, b, c)],
            pltpu.VMEM((3, 3, C, C), f32),
            pltpu.SemaphoreType.DMA((7,)),
            pltpu.SemaphoreType.DMA((9,)),
        ],
        out_shape=(
            S(res.shape, bf16),
            S(ig.shape, bf16),
            S((C,), f32),
            S((C,), f32),
            S((C, 3 * C), f32),
            S((2 * C,), f32),
            S((HEADS, table), f32),
            S((C, C), f32),
            S((C,), f32),
            S((C,), f32),
            S((C,), f32),
            S((C, HID), f32),
            S((HID,), f32),
            S((C, HID), f32),
            S((C,), f32),
            S((3, 3, C, C), f32),
            S((C,), f32),
        ),
        compiler_params=pltpu.CompilerParams(vmem_limit_bytes=63 * 1024 * 1024),
        name="finish",
    )(res, ig, a, b, c, d)


def on_device(
    images, widths, norm1_gain, norm1_bias, qkv_weight, qv_bias, bias_table, proj_weight, proj_bias,
    norm2_gain, norm2_bias, fc1_weight, fc1_bias, fc2_weight, fc2_bias, conv_weight, conv_bias, cotangent,
):
    count, rows_here, width, chans = images.shape
    img, cot = [
        v.reshape(rows_here, width, chans).transpose(2, 0, 1).reshape(chans * rows_here, width)
        for v in (images, cotangent)
    ]
    scal = lax.div(widths, WIN)
    res, ig, a, b, c, d = run_layer(
        lax.axis_size("rows"), lax.axis_size("imgs"),
        scal, img, cot, qkv_weight, proj_weight, fc1_weight, fc2_weight.T, conv_weight, bias_table.T,
        norm1_gain, norm1_bias, qv_bias, proj_bias, norm2_gain, norm2_bias, fc1_bias, fc2_bias, conv_bias,
    )
    res, ig, *grads = run_finish(res, ig, a, b, c, d, bias_table.shape[0])
    res, ig = [v.reshape(chans, rows_here, width).transpose(1, 2, 0) for v in (res, ig)]
    grads[4] = grads[4].T
    grads[11] = grads[11].T
    return (res[None], ig[None], *grads)


def solution(mesh):
    big = P("imgs", "rows", None, None)
    in_specs = (big, P("imgs")) + (P(),) * 15 + (big,)
    out_specs = (big, big) + (P(),) * 15
    return jax.shard_map(
        on_device, mesh=mesh, in_specs=in_specs, out_specs=out_specs, check_vma=False
    )
```

```python
import functools

import jax
import jax.numpy as jnp
import numpy as np
from jax import lax
from jax.experimental import pallas as pl
from jax.experimental.pallas import tpu as pltpu
from jax.sharding import PartitionSpec as P

HEADS = 6
HEAD_DIM = 30
WIN = 8
SHIFT = 4
C = 180
CP = 256
HID = 360
HP = 384
AREA = WIN * WIN
HI = HEADS * AREA
LOG2E = 1.4426950408889634
SCALE = HEAD_DIM ** (-0.5)

CR = 192
A_USED = 5 * CR
B_SMALL = 5 * CR
B_USED = B_SMALL + 32
C_MIX = 9 * CR
C_FC1 = C_MIX + 5 * CR
C_USED = C_FC1 + 2 * CR

f32 = jnp.float32
bf16 = jnp.bfloat16


def dot(a, b, ca=1, cb=0):
    return lax.dot_general(a, b, (((ca,), (cb,)), ((), ())), preferred_element_type=f32)


def lanes(shape):
    return lax.broadcasted_iota(jnp.int32, shape, len(shape) - 1)


def rows_of(shape):
    return lax.broadcasted_iota(jnp.int32, shape, len(shape) - 2)


def ln_fwd(x, gain, bias):
    real = (lanes((1, CP)) < C).astype(f32)
    mean = jnp.sum(x, axis=-1, keepdims=True) * (1.0 / C)
    xc = (x - mean) * real
    var = jnp.sum(xc * xc, axis=-1, keepdims=True) * (1.0 / C)
    rstd = lax.rsqrt(var + 1e-05)
    xhat = xc * rstd
    return xhat, rstd, xhat * gain + bias


def with_rstd(xhat, rstd):
    high = rstd.astype(bf16).astype(f32)
    lane = lanes((1, CP))
    return jnp.where(lane == 200, high, jnp.where(lane == 201, rstd - high, xhat))


def ln_bwd(dy, xhat, rstd, gain):
    a = dy * gain
    m1 = jnp.sum(a, axis=-1, keepdims=True) * (1.0 / C)
    m2 = jnp.sum(a * xhat, axis=-1, keepdims=True) * (1.0 / C)
    return rstd * (a - m1 - xhat * m2)


def gelu_pair(h):
    z = jnp.abs(h) * 0.7071067811865476
    d = 1.0 + 0.3275911 * z
    t = pl.reciprocal(d, approx=True)
    t = t * (2.0 - d * t)
    e = jnp.exp2(h * h * (-0.5 * LOG2E))
    poly = t * (
        0.254829592 + t * (-0.284496736 + t * (1.421413741 + t * (-1.453152027 + t * 1.061405429)))
    )
    q = 0.5 * poly * e
    phi = jnp.where(h >= 0, 1.0 - q, q)
    return h * phi, phi + h * (e * 0.3989422804014327)


def fold8(v):
    return jnp.sum(v.reshape(v.shape[0] // 8, 8, v.shape[1]), axis=0)


HP_DIM = 32


def by_rows(f, step, *arrays):
    rows = arrays[0].shape[0]
    parts = [f(*[a[i : i + step] for a in arrays]) for i in range(0, rows, step)]
    if not isinstance(parts[0], tuple):
        return jnp.concatenate(parts, axis=0)
    return tuple(jnp.concatenate(p, axis=0) for p in zip(*parts))


def added(values):
    return functools.reduce(jnp.add, values)


def head_mask(h):
    ln = lanes((1, 128))
    return (ln >= h * HP_DIM) & (ln < (h + 1) * HP_DIM)


def spread_heads(v, count):
    return jnp.concatenate(
        [jnp.where(head_mask(h), v, jnp.zeros_like(v)) for h in range(count)], axis=0
    )


def gather_heads(v, count):
    out = jnp.where(head_mask(0), v[:AREA], 0.0)
    for h in range(1, count):
        out = jnp.where(head_mask(h), v[h * AREA : (h + 1) * AREA], out)
    return out


GROUPS = ((0, 4), (4, 2))


def column_masks(width):
    return rows_of((256, CP)) < width


class SmallAllReduce:
    def __init__(self, sums, slots, ssem, rsem, chips, imgs):
        self.sums, self.ssem, self.rsem = [sums.at[n] for n in range(4)], ssem, rsem
        rows, z = lax.axis_index("rows"), lax.axis_index("imgs")
        core, chip = lax.rem(rows, 2), lax.div(rows, 2)
        self.stages = [
            [{"rows": chip * 2 + 1 - core}],
            [{"rows": lax.rem(chip + d, chips) * 2 + core} for d in range(1, chips)],
            [{"imgs": lax.rem(z + d, imgs)} for d in range(1, imgs)],
        ]
        self.first = [0, 1, chips]
        self.slots = slots

    def copies(self, n):
        return [
            pltpu.make_async_remote_copy(
                src_ref=self.sums[n],
                dst_ref=self.slots.at[self.first[n] + d],
                send_sem=self.ssem.at[self.first[n] + d],
                recv_sem=self.rsem.at[self.first[n] + d],
                device_id=to,
                device_id_type=pl.DeviceIdType.MESH,
            )
            for d, to in enumerate(self.stages[n])
        ]

    def begin(self, value):
        self.sums[0][...] = value
        for c in self.copies(0):
            c.start()

    def step(self, n):
        value = self.sums[n][...]
        for d, c in enumerate(self.copies(n)):
            c.wait()
            value += self.slots[self.first[n] + d]
        self.sums[n + 1][...] = value
        if n < 2:
            for c in self.copies(n + 1):
                c.start()


TURNS = ((0, (("a", 1),)), (1, (("c", 1),)), (4, (("a", 2),)), (7, (("c", 2),)))


class AllReduce:
    def __init__(self, buf, out, r1, r2, r3, ssem, rsem, pr, chips, imgs, zsplit):
        self.buf, self.out, self.r1, self.r2, self.r3 = buf, out, r1, r2, r3
        self.ssem, self.rsem, self.chips, self.imgs = ssem, rsem, chips, imgs
        self.zsplit = zsplit
        rows = lax.axis_index("rows")
        self.core = lax.rem(rows, 2)
        self.chip = lax.div(rows, 2)
        self.z = lax.axis_index("imgs")
        self.piece = pr
        self.group = pr * imgs if zsplit else pr
        self.half = self.group * chips
        self.used = 0

    def copy(self, src, dst, device, n):
        return pltpu.make_async_remote_copy(
            src_ref=src,
            dst_ref=dst,
            send_sem=self.ssem.at[n],
            recv_sem=self.rsem.at[n],
            device_id=device,
            device_id_type=pl.DeviceIdType.MESH,
        )

    def rows(self, ref, start, size):
        return ref.at[pl.ds(pl.multiple_of(start, 16), size)]

    def base_half(self, core):
        return core * self.half

    def base_group(self, chip):
        return self.core * self.half + chip * self.group

    def base_piece(self, z):
        return self.base_group(self.chip) + (z * self.piece if self.zsplit else 0)

    def core_copy(self, ref, dst, n, gather):
        side = self.core if gather else 1 - self.core
        src = self.rows(ref, self.base_half(side), self.half)
        dst = src if dst is None else dst
        return [self.copy(src, dst, {"rows": self.chip * 2 + 1 - self.core}, n)]

    def chip_copies(self, ref, dst, n, gather):
        out = []
        for d in range(1, self.chips):
            to = lax.rem(self.chip + d, self.chips)
            src = self.rows(ref, self.base_group(self.chip if gather else to), self.group)
            to_ref = src if gather else dst.at[pl.ds((d - 1) * self.group, self.group)]
            out.append(self.copy(src, to_ref, {"rows": to * 2 + self.core}, n + d - 1))
        return out

    def img_copies(self, ref, dst, n, gather):
        out = []
        for d in range(1, self.imgs):
            to = lax.rem(self.z + d, self.imgs)
            src = self.rows(ref, self.base_piece(self.z if gather else to), self.piece)
            to_ref = src if gather else dst.at[pl.ds((d - 1) * self.piece, self.piece)]
            out.append(self.copy(src, to_ref, {"imgs": to}, n + d - 1))
        return out

    def start(self, copies):
        for c in copies:
            c.start()
        return copies

    def wait(self, copies):
        for c in copies:
            c.wait()

    def add(self, base, size, extra, count, stride, target):
        step = min(size, 64)
        while size % step:
            step -= 16

        @pl.loop(0, size // step)
        def _(i):
            at = pl.ds(pl.multiple_of(base + i * step, 16), step)
            total = self.buf[at, :].astype(f32)
            for d in range(count):
                total += extra[pl.ds(pl.multiple_of(d * stride + i * step, 16), step), :].astype(f32)
            target[at, :] = total.astype(bf16)

    def step(self, k):
        n2 = 1
        n3 = n2 + self.chips - 1
        n4 = n3 + self.imgs - 1
        n5 = n4 + self.imgs - 1
        n6 = n5 + self.chips - 1
        first = lambda: self.core_copy(self.buf, self.r1, 0, False)
        second = lambda: self.chip_copies(self.buf, self.r2, n2, False)
        third = lambda: self.img_copies(self.buf, self.r3, n3, False)
        fourth = lambda: self.img_copies(self.out, None, n4, True) if self.zsplit else []
        fifth = lambda: self.chip_copies(self.out, None, n5, True)
        sixth = lambda: self.core_copy(self.out, None, n6, True)
        if k == 0:
            self.start(first())
        elif k == 1:
            self.wait(first())
            self.add(self.base_half(self.core), self.half, self.r1, 1, 0, self.buf)
            self.start(second())
        elif k == 2:
            self.wait(second())
            self.add(
                self.base_group(self.chip), self.group, self.r2, self.chips - 1, self.group, self.buf
            )
            self.start(third())
        elif k == 3:
            self.wait(third())
            self.add(
                self.base_piece(self.z), self.piece, self.r3, self.imgs - 1, self.piece, self.out
            )
            self.start(fourth() if self.zsplit else fifth())
        elif k == 4:
            if self.zsplit:
                self.wait(fourth())
                self.start(fifth())
        elif k == 5:
            self.wait(fifth())
            self.start(sixth())
        elif k == 6:
            self.wait(sixth())


def all_reduce_sems(chips, imgs):
    return 2 * (1 + chips - 1 + imgs - 1)


def layer_kernel(
    chips,
    imgs,
    pieces,
    splits,
    scal,
    img,
    cot,
    r_qkv,
    r_proj,
    r_fc1,
    r_fc2t,
    r_conv,
    r_table,
    r_n1g,
    r_n1b,
    r_qvb,
    r_pb,
    r_n2g,
    r_n2b,
    r_f1b,
    r_f2b,
    r_cb,
    res_out,
    ig_out,
    a_out,
    b_out,
    c_out,
    d_out,
    wqkv,
    wproj,
    wfc1,
    wfc2t,
    wconv,
    vecs,
    extra,
    d_qkv,
    d_proj,
    d_fc1,
    d_fc2,
    d_conv,
    d_norm,
    d_rel,
    io1,
    io2,
    xband,
    gband,
    gcat,
    llbuf,
    xhat1,
    normed,
    qkv,
    probs,
    mixed,
    winf,
    fgrad,
    do_buf,
    ig_rows,
    edge,
    tmp_eye,
    eye_c,
    planes,
    tmp,
    a_buf,
    a_r1,
    a_r2,
    a_r3,
    b_buf,
    b_r1,
    b_r2,
    b_r3,
    c_buf,
    c_r1,
    c_r2,
    c_r3,
    dd_sums,
    dd_slots,
    lsem,
    hs,
    hr,
    a_s,
    a_r,
    b_s,
    b_r,
    c_s,
    c_r,
    dd_s,
    dd_r,
):
    stripes = 2 * chips
    rank = lax.axis_index("rows")
    core = lax.rem(rank, 2)
    up = lax.rem(rank + stripes - 1, stripes)
    down = lax.rem(rank + 1, stripes)
    pa, pb, pc = pieces
    ara = AllReduce(a_buf, a_out, a_r1, a_r2, a_r3, a_s, a_r, pa, chips, imgs, splits[0])
    arb = AllReduce(b_buf, b_out, b_r1, b_r2, b_r3, b_s, b_r, pb, chips, imgs, splits[1])
    arc = AllReduce(c_buf, c_out, c_r1, c_r2, c_r3, c_s, c_r, pc, chips, imgs, splits[2])

    ard = SmallAllReduce(dd_sums, dd_slots, dd_s, dd_r, chips, imgs)

    flat = C * 16
    load_cot = pltpu.make_async_copy(cot, qkv.at[pl.ds(0, flat), pl.ds(CP, CP)], lsem.at[0])
    load_img = pltpu.make_async_copy(img, qkv.at[pl.ds(0, flat), pl.ds(0, CP)], lsem.at[1])
    load_cot.start()
    load_img.start()

    barrier = pltpu.get_barrier_semaphore()
    peers = [{"rows": up}, {"rows": down}]
    peers += [{"rows": lax.rem(rank + 2 * d, stripes)} for d in range(1, chips)]
    peers += [{"imgs": lax.rem(ara.z + d, imgs)} for d in range(1, imgs)]
    for peer in peers:
        pl.semaphore_signal(barrier, inc=1, device_id=peer, device_id_type=pl.DeviceIdType.MESH)

    def remote(src, dst, to, n):
        return pltpu.make_async_remote_copy(
            src_ref=src,
            dst_ref=dst,
            send_sem=hs.at[n],
            recv_sem=hr.at[n],
            device_id={"rows": to},
            device_id_type=pl.DeviceIdType.MESH,
        )

    send_img = remote(io2.at[pl.ds(0, 4)], io2.at[pl.ds(16, 4)], up, 0)
    send_cot = remote(io1.at[pl.ds(0, 5)], io1.at[pl.ds(16, 5)], up, 1)
    nb = scal[0]
    width = nb * WIN
    is_last = rank == stripes - 1
    joined = jnp.where(is_last, 0.0, 1.0)
    NW = 256 // WIN
    RM = 256

    def vec(i, n):
        return vecs[i : i + 1, 0:n]

    def row_at(pos, count=1):
        return pl.ds(pl.multiple_of(pos * 256, 256), count * 256)

    tmp[...] = jnp.zeros_like(tmp)
    for ref in (d_qkv, d_proj, d_fc1, d_fc2, d_conv, d_norm, d_rel):
        ref[...] = jnp.zeros_like(ref)
    for ref, size in ((a_buf, A_USED), (b_buf, B_USED), (c_buf, C_USED)):
        if ref.shape[0] > size:
            ref[size:, :] = jnp.zeros((ref.shape[0] - size, 128), bf16)

    col_in = rows_of((256, C)) < width
    col_in_p = rows_of((256, CP)) < width

    def put_g(pos, row, flag):
        g = jnp.where(col_in, row.astype(f32), 0.0) * flag
        tmp[8:264, 0:C] = g
        at = row_at(pos)
        gcat[at, 0:CP] = tmp[9:265, :].astype(bf16)
        gcat[at, CP : 2 * CP] = tmp[8:264, :].astype(bf16)
        gcat[at, 2 * CP : 3 * CP] = tmp[7:263, :].astype(bf16)

    def iota(shape, dim):
        return lax.broadcasted_iota(jnp.int32, shape, dim)

    def padded(v):
        return jnp.concatenate([v.astype(f32), jnp.zeros((CR - C, v.shape[1]), f32)], axis=0).astype(bf16)

    for ref in (wqkv, wproj, wfc1, wfc2t, wconv, vecs):
        ref[...] = jnp.zeros_like(ref)
    part = iota((3 * C, 3 * CP), 1)
    lane = part & (CP - 1)
    place = (part >> 8) * C + (lane >> 5) * HEAD_DIM + (lane & 31)
    used = ((lane & 31) < HEAD_DIM) & (lane < HEADS * HP_DIM)
    spread = (used & (iota((3 * C, 3 * CP), 0) == place)).astype(bf16)
    wqkv[0:CR, :] = padded(dot(r_qkv[...], spread))
    lane = iota((CP, C), 0)
    place = (lane >> 5) * HEAD_DIM + (lane & 31)
    used = ((lane & 31) < HEAD_DIM) & (lane < HEADS * HP_DIM)
    wproj[:, 0:C] = dot((used & (iota((CP, C), 1) == place)).astype(bf16), r_proj[...]).astype(bf16)
    wfc1[0:CR, 0:HID] = padded(r_fc1[...])
    wfc2t[0:CR, 0:HID] = padded(r_fc2t[...])
    for a in range(3):
        for b in range(3):
            wconv[a, 0:CR, b * CP : b * CP + C] = padded(r_conv[a, b])
    for n, ref in ((0, r_n1g), (1, r_n1b), (3, r_pb), (4, r_n2g), (5, r_n2b), (6, r_f1b), (7, r_f2b), (8, r_cb)):
        vecs[n : n + 1, 0 : ref.shape[0]] = ref[...].reshape(1, ref.shape[0])
    for n in (1, 5, 7):
        vecs[n : n + 1, C : C + 1] = jnp.ones((1, 1), f32)
    qvb = r_qvb[...].reshape(1, 2 * C)
    for h in range(HEADS):
        at = h * HP_DIM
        vecs[2:3, at : at + HEAD_DIM] = qvb[:, h * HEAD_DIM : (h + 1) * HEAD_DIM]
        vecs[2:3, 2 * CP + at : 2 * CP + at + HEAD_DIM] = qvb[
            :, C + h * HEAD_DIM : C + (h + 1) * HEAD_DIM
        ]
    score_terms(r_table[...], extra)

    tmp_eye[...] = (iota((128, 128), 0) == iota((128, 128), 1)).astype(bf16)

    eye_c[...] = (iota((C, C), 0) == iota((C, C), 1)).astype(bf16)

    def to_rows(lane0, dst):
        for m in range(2):
            half = slice(m * 128, (m + 1) * 128)

            @pl.loop(0, flat // 96, unroll=2)
            def _(n):
                at = pl.ds(pl.multiple_of(n * 96, 96), 96)
                planes[at, :] = qkv[at, lane0 + m * 128 : lane0 + (m + 1) * 128].astype(f32)

            for r in range(16):
                x = planes[pl.ds(r, C, stride=16), :].astype(bf16)
                dst[r, half, :] = dot(tmp_eye[...], x, 1, 1).astype(bf16)

    load_cot.wait()
    to_rows(CP, io1)
    load_img.wait()
    to_rows(0, io2)

    @pl.loop(0, 13)
    def _(r):
        put_g(r, io1[r + 3], 1.0)

    put_g(14, io1[15], joined)
    pl.semaphore_wait(barrier, len(peers))
    send_cot.start()
    send_img.start()

    pos_hi = rows_of((1, WIN, CP)) >= SHIFT

    def rolled(a, b):
        t = jnp.where(pos_hi, a, b)
        return pltpu.roll(t, SHIFT, 1)

    def to_win(ref, k):
        nxt = jnp.minimum(k + 1, NW - 1)
        a = ref[:, pl.ds(pl.multiple_of(k * WIN, WIN), WIN), :]
        b = ref[:, pl.ds(pl.multiple_of(nxt * WIN, WIN), WIN), :]
        b = jnp.where(k == nb - 1, ref[:, 0:WIN, :], b)
        return rolled(a, b).reshape(AREA, CP)

    def from_win(ref, band):
        def block(k):
            at = pl.multiple_of((band * NW + k) * AREA, AREA)
            return ref[pl.ds(at, AREA), :].reshape(WIN, WIN, CP)

        @pl.loop(0, NW, unroll=4)
        def _(k):
            b = block(k)
            edge[...] = jnp.where(k == nb - 1, b, edge[...])
            xband[:, pl.ds(pl.multiple_of(k * WIN, WIN), WIN), :] = rolled(
                block(jnp.maximum(k - 1, 0)), b
            )

        xband[:, 0:WIN, :] = rolled(edge[...], block(0))

    def win_rows(w):
        return pl.ds(pl.multiple_of(w * AREA, AREA), AREA)

    send_up = remote(llbuf.at[pl.ds(5 * 256, 256)], llbuf.at[pl.ds(23 * 256, 256)], up, 2)

    @pl.loop(0, 2)
    def _(band):
        @pl.when(band == 1)
        def _():
            send_cot.wait()
            send_img.wait()
            put_g(13, io1[16], joined)

            @pl.loop(0, 5)
            def _(r):
                put_g(15 + r, io1[16 + r], 1.0)

        xband[:, :, 128:256] = jnp.zeros((8, 256, 128), f32)

        @pl.loop(0, 8)
        def _(y):
            xband[y, :, 0:C] = io2[band * 8 + y + 4].astype(f32)

        @pl.loop(0, 2)
        def _(y):
            r = band * 8 + 4 * y
            pos = r + 1 + jnp.where(r >= 12, 2, 0)
            acc = None
            for a in range(3):
                d = dot(gcat[row_at(pos + 1 - a, 4), :], wconv[a], 1, 1)
                acc = d if acc is None else acc + d
            for n in range(4):
                gband[4 * y + n] = jnp.where(col_in_p, acc[n * 256 : (n + 1) * 256], 0.0)

        @pl.loop(0, 4)
        def _(gg):
            g = band * 4 + gg
            k0 = gg * 8
            gs = pl.ds(pl.multiple_of(g * 512, 512), 512)

            xs = [to_win(xband, k0 + w) for w in range(8)]
            for w in range(8):
                winf[win_rows(gg * 8 + w), :] = xs[w]
                fgrad[win_rows(g * 8 + w), :] = to_win(gband, k0 + w)
                xhat, rs_, ln_out = ln_fwd(xs[w], vec(0, CP), vec(1, CP))
                xhat1[win_rows(g * 8 + w), :] = with_rstd(xhat, rs_).astype(bf16)
                normed[win_rows(g * 8 + w), :] = ln_out.astype(bf16)

            for n in range(3):
                sl = slice(n * CP, (n + 1) * CP)
                qkv[gs, sl] = (dot(normed[gs, :], wqkv[:, sl]) + vecs[2:3, sl]).astype(bf16)

            i = 0
            if True:
                which = jnp.where((band == 1) & is_last, 2, 0)
                jobs = []
                for w in range(8):
                    rs = win_rows(g * 8 + i * 8 + w)
                    edge_win = k0 + i * 8 + w == nb - 1
                    for n, (h0, count) in enumerate(GROUPS):
                        jobs.append((rs, w, edge_win, n, count, slice(h0 * AREA, (h0 + count) * AREA)))
                qs = [qkv[rs, n * 128 : (n + 1) * 128] for rs, w, ew, n, count, hl in jobs]
                ks = [qkv[rs, CP + n * 128 : CP + (n + 1) * 128] for rs, w, ew, n, count, hl in jobs]
                vs = [qkv[rs, 2 * CP + n * 128 : 2 * CP + (n + 1) * 128] for rs, w, ew, n, count, hl in jobs]
                ss = [dot(k, spread_heads(q, job[4]), 1, 1) for q, k, job in zip(qs, ks, jobs)]
                ps = []
                for s, (rs, w, ew, n, count, hl) in zip(ss, jobs):
                    more = jnp.where(ew, extra[which + 1, :, hl], extra[which, :, hl])
                    s = s * (SCALE * LOG2E) + more
                    top = jnp.max(s, axis=0, keepdims=True)
                    e = jnp.exp2(s - top)
                    total = jnp.sum(e, axis=0, keepdims=True)
                    ps.append((e * (1.0 / total)).astype(bf16))
                os = [gather_heads(dot(p, v, 0, 0), job[4]) for p, v, job in zip(ps, vs, jobs)]
                for p, o, (rs, w, ew, n, count, hl) in zip(ps, os, jobs):
                    probs[rs, hl] = p
                    if n == 0:
                        o = jnp.where(lanes((1, 128)) == HEAD_DIM, 1.0, o)
                    mixed[win_rows(i * 8 + w), n * 128 : (n + 1) * 128] = o.astype(bf16)

            parts = range(0, 512, 256)
            at_rows = [pl.ds(pl.multiple_of(g * 512 + r, 256), 256) for r in parts]
            in_band = [pl.ds(pl.multiple_of(gg * 512 + r, 256), 256) for r in parts]
            mixes = [mixed[r : r + 256, :] for r in parts]
            firsts = [dot(m, wproj[...]) + vec(3, CP) + winf[rs, :] for m, rs in zip(mixes, in_band)]

            def norm2(v):
                xhat, rs_, ln_out = ln_fwd(v, vec(4, CP), vec(5, CP))
                return xhat, rs_, ln_out.astype(bf16)

            def activate(v):
                ac, dg = gelu_pair(v + vec(6, HP))
                return jnp.where(lanes((1, HP)) == HID, 1.0, ac).astype(bf16), dg.astype(bf16)

            norms = [by_rows(norm2, 64, v) for v in firsts]
            n2s = [n[2] for n in norms]
            acts = [by_rows(activate, 64, dot(n2, wfc1[...])) for n2 in n2s]
            for fs, (ac, dg), rs in zip(firsts, acts, in_band):
                winf[rs, :] = fs + dot(ac, wfc2t[...], 1, 1) + vec(7, CP)
            lgs = [fgrad[rs, :] for rs in at_rows]
            mgs = [lg.astype(bf16) for lg in lgs]
            hgs = [
                (dot(mg, wfc2t[...]).astype(bf16).astype(f32) * dg.astype(f32)).astype(bf16)
                for mg, (ac, dg) in zip(mgs, acts)
            ]
            dns = [dot(hg, wfc1[...], 1, 1).astype(bf16) for hg in hgs]

            def back2(dn2, xh, rs_, lg):
                dn2 = dn2.astype(f32)
                fg = lg + ln_bwd(dn2, xh, rs_, vec(4, CP))
                return fg, fg.astype(bf16), fold8(dn2 * xh), fold8(dn2)

            backs = [
                by_rows(back2, 64, dn, n[0], n[1], lg) for dn, n, lg in zip(dns, norms, lgs)
            ]
            ats = [b[1] for b in backs]
            for b, rs in zip(backs, at_rows):
                fgrad[rs, :] = b[0]
                do_buf[rs, :] = dot(b[1], wproj[...], 1, 1).astype(bf16)
            d_norm[0:8, :] += added([fold8(b[2]) for b in backs])
            d_norm[8:16, :] += added([fold8(b[3]) for b in backs])
            join = lambda vs: jnp.concatenate(vs, axis=0)
            mg = join(mgs)
            d_fc2[...] += dot(mg[:, 0:CR], join([ac for ac, dg in acts]), 0, 0)
            d_norm[32:40, :] += fold8(mg.astype(f32))
            d_fc1[...] += dot(join(n2s)[:, 0:CR], join(hgs), 0, 0)
            d_proj[...] += dot(mixed[:, 0:CR], join(ats), 0, 0)

        from_win(winf, 0)

        @pl.loop(0, 8)
        def _(y):
            r = band * 8 + y
            pos = r + 5 + jnp.where(r >= 12, 2, 0)
            llbuf[row_at(pos), :] = jnp.where(col_in_p, xband[y], 0.0).astype(bf16)

        @pl.when(band == 0)
        def _():
            send_up.start()

    joined_low = joined.astype(bf16)
    llbuf[17 * 256 : 18 * 256, :] = llbuf[19 * 256 : 20 * 256, :] * joined_low
    llbuf[18 * 256 : 19 * 256, :] = llbuf[16 * 256 : 17 * 256, :] * joined_low
    send_down = remote(llbuf.at[pl.ds(22 * 256, 256)], llbuf.at[pl.ds(4 * 256, 256)], down, 3)
    send_more = remote(llbuf.at[pl.ds(18 * 256, 1024)], llbuf.at[pl.ds(0, 1024)], down, 4)
    send_down.start()

    def wgrad_rows(n):
        start = 1 + 4 * n + jnp.where(n == 3, 2, 0)
        gs = gcat[row_at(start, 4), :]
        for a in range(3):
            d_conv[a] += dot(llbuf[row_at(start + a + 3, 4), 0:CR], gs, 0, 0)

    low_lanes = lanes((1, 128)) < 64

    def mix(p, q):
        return jnp.where(low_lanes, p, pltpu.roll(q, 64, 1)).astype(bf16)

    a_buf[0:CR, :] = d_fc1[:, CP:HP].astype(bf16)
    for n in range(3):
        a_buf[(n + 1) * CR : (n + 2) * CR, :] = d_fc2[:, n * 128 : (n + 1) * 128].astype(bf16)
    a_buf[4 * CR : 5 * CR, :] = d_proj[:, 0:128].astype(bf16)
    ara.step(0)

    @pl.loop(1, 3)
    def _(n):
        wgrad_rows(n)

    send_up.wait()
    wgrad_rows(3)
    send_down.wait()
    wgrad_rows(0)

    tails = []
    for a in range(3):
        for b in range(3):
            at = (a * 3 + b) * CR
            c_buf[at : at + CR, :] = d_conv[a, :, b * CP : b * CP + 128].astype(bf16)
            tails.append((d_conv, a, slice(b * CP + 128, (b + 1) * CP)))
    tails = [ref[a, :, ln] for ref, a, ln in tails] + [d_proj[:, 128:256]]
    for n in range(5):
        at = C_MIX + n * CR
        c_buf[at : at + CR, :] = mix(tails[2 * n], tails[2 * n + 1])
    for n in range(2):
        at = C_FC1 + n * CR
        c_buf[at : at + CR, :] = d_fc1[:, n * 128 : (n + 1) * 128].astype(bf16)
    arc.step(0)

    def conv_rows(lo, hi):
        @pl.loop(lo // 2, hi // 2)
        def _(half):
            r = 2 * half
            acc = None
            for a in range(3):
                d = dot(llbuf[row_at(r + a, 2), :], wconv[a])
                acc = d if acc is None else acc + d
            for n in range(2):
                px = slice(n * 256, (n + 1) * 256)
                tmp[8:264, :] = acc[px, 0:CP]
                tmp[280:536, :] = acc[px, 2 * CP : 3 * CP]
                out = acc[px, CP : 2 * CP] + tmp[7:263, :] + tmp[281:537, :] + vec(8, CP)
                out = out[:, 0:C] + io2[r + n].astype(f32)
                io1[r + n] = jnp.where(col_in, out, 0.0).astype(bf16)

    def grad_rows(band):
        from_win(fgrad, band)

        @pl.loop(0, 8)
        def _(y):
            r = band * 8 + y
            pos = r + 1 + jnp.where(r >= 12, 2, 0)
            v = xband[y] + gcat[row_at(pos), CP : 2 * CP].astype(f32)
            ig_rows[r] = jnp.where(col_in_p, v, 0.0)[:, 0:C].astype(bf16)

    send_ig = remote(ig_rows.at[pl.ds(12, 4)], ig_rows.at[pl.ds(16, 4)], down, 5)

    @pl.loop(0, 8)
    def _(turn):
        g = lax.rem(turn + 4, 8)
        gs = pl.ds(pl.multiple_of(g * 512, 512), 512)

        i = 0
        if True:
            jobs = []
            for w in range(8):
                rs = win_rows(g * 8 + i * 8 + w)
                for n, (h0, count) in enumerate(GROUPS):
                    jobs.append((rs, n, count, slice(h0 * AREA, (h0 + count) * AREA)))
            qs = [qkv[rs, n * 128 : (n + 1) * 128] for rs, n, count, hl in jobs]
            ks = [qkv[rs, CP + n * 128 : CP + (n + 1) * 128] for rs, n, count, hl in jobs]
            vs = [qkv[rs, 2 * CP + n * 128 : 2 * CP + (n + 1) * 128] for rs, n, count, hl in jobs]
            dos = [spread_heads(do_buf[rs, n * 128 : (n + 1) * 128], count) for rs, n, count, hl in jobs]
            pbs = [probs[rs, hl] for rs, n, count, hl in jobs]
            dps = [dot(v, d, 1, 1) for v, d in zip(vs, dos)]
            dvs = [dot(p, d) for p, d in zip(pbs, dos)]
            dss = []
            for dp, pb in zip(dps, pbs):
                p = pb.astype(f32)
                dss.append((p * (dp - jnp.sum(p * dp, axis=0, keepdims=True))).astype(bf16))
            dks = [dot(ds, spread_heads(q, job[2])) * SCALE for ds, q, job in zip(dss, qs, jobs)]
            dqs = [gather_heads(dot(ds, k, 0, 0), job[2]) * SCALE for ds, k, job in zip(dss, ks, jobs)]
            for n, (h0, count) in enumerate(GROUPS):
                hl = slice(h0 * AREA, (h0 + count) * AREA)
                d_rel[:, hl] += functools.reduce(jnp.add, [d.astype(f32) for d in dss[n::2]])
            for dq, dk, dv, (rs, n, count, hl) in zip(dqs, dks, dvs, jobs):
                qkv[rs, n * 128 : (n + 1) * 128] = dq.astype(bf16)
                qkv[rs, CP + n * 128 : CP + (n + 1) * 128] = dk.astype(bf16)
                qkv[rs, 2 * CP + n * 128 : 2 * CP + (n + 1) * 128] = dv.astype(bf16)

        d_qkv[...] += dot(normed[gs, 0:CR], qkv[gs, :], 0, 0)

        @pl.when(turn == 5)
        def _():
            send_more.start()

        for at, steps in TURNS:

            @pl.when(turn == at)
            def _(steps=steps):
                for which, k in steps:
                    {"a": ara, "c": arc}[which].step(k)

    for n in range(3):
        b_buf[n * CR : (n + 1) * CR, :] = d_qkv[:, n * CP : n * CP + 128].astype(bf16)
    b_buf[3 * CR : 4 * CR, :] = mix(d_qkv[:, 128:256], d_qkv[:, CP + 128 : 2 * CP])
    b_buf[4 * CR : 5 * CR, :] = mix(d_qkv[:, 2 * CP + 128 : 3 * CP], d_qkv[:, 2 * CP + 128 : 3 * CP])
    sums = jnp.sum(d_norm[...].reshape(5, 8, CP), axis=1)
    small = jnp.concatenate([table_sum(d_rel[...]), sums, jnp.zeros((3, CP), f32)], axis=0)
    b_buf[B_SMALL : B_SMALL + 16, :] = small[:, 0:128].astype(bf16)
    b_buf[B_SMALL + 16 : B_SMALL + 32, :] = small[:, 128:256].astype(bf16)
    arb.step(0)
    ara.step(3)

    def norm1_back(lo, hi):
        @pl.loop(lo, hi)
        def _(g):
            gs = pl.ds(pl.multiple_of(g * 512, 512), 512)
            dn1 = dot(qkv[gs, :], wqkv[...], 1, 1).astype(bf16)

            def back1(dn, xhat, fg):
                dn, xhat = dn.astype(f32), xhat.astype(f32)
                out = fg + ln_bwd(dn, xhat, xhat[:, 200:201] + xhat[:, 201:202], vec(0, CP))
                return out, fold8(dn * xhat), fold8(dn)

            back = by_rows(back1, 64, dn1, xhat1[gs, :], fgrad[gs, :])
            fgrad[gs, :] = back[0]
            d_norm[16:24, :] += fold8(back[1])
            d_norm[24:32, :] += fold8(back[2])

    norm1_back(4, 8)
    arb.step(1)
    grad_rows(1)
    send_ig.start()
    norm1_back(0, 4)
    sums = jnp.sum(d_norm[16:32, :].reshape(2, 8, CP), axis=1)
    sums = jnp.concatenate([sums[:, 0:128], sums[:, 128:256], jnp.zeros((4, 128), f32)], axis=0)
    ard.begin(sums)
    ara.step(4)
    arc.step(3)
    def to_planes(src, lane0):
        for m in range(2):
            half = slice(m * 128, (m + 1) * 128)
            for i in range(16):
                planes[pl.ds(i, C, stride=16), :] = dot(eye_c[...], src(i)[half, :], 1, 1)

            @pl.loop(0, flat // 96, unroll=2)
            def _(n):
                at = pl.ds(pl.multiple_of(n * 96, 96), 96)
                qkv[at, lane0 + m * 128 : lane0 + (m + 1) * 128] = planes[at, :].astype(bf16)

    conv_rows(4, 8)
    arb.step(2)
    ard.step(0)
    conv_rows(8, 16)
    arc.step(4)
    ard.step(1)
    ara.step(5)
    send_more.wait()
    conv_rows(0, 4)
    to_planes(lambda i: io1[i], 0)
    store_res = pltpu.make_async_copy(qkv.at[pl.ds(0, flat), pl.ds(0, CP)], res_out, lsem.at[2])
    store_res.start()
    grad_rows(0)
    arb.step(3)
    ara.step(6)
    ard.step(2)
    d_out[...] = dd_sums[3]
    send_ig.wait()
    to_planes(lambda i: ig_rows[16 + i] if i < SHIFT else ig_rows[i - SHIFT], CP)
    store_ig = pltpu.make_async_copy(qkv.at[pl.ds(0, flat), pl.ds(CP, CP)], ig_out, lsem.at[3])
    store_ig.start()
    arc.step(5)
    arb.step(5)
    arc.step(6)
    arb.step(6)
    store_res.wait()
    store_ig.wait()


def finish_kernel(
    res_ref, ig_ref, a_hbm, b_hbm, c_hbm, d_ref, o_res, o_ig, o_n1g, o_n1b, o_qkv, o_qvb, o_table, o_proj, o_pb, o_n2g, o_n2b, o_fc1, o_f1b, o_fc2t,
    o_f2b, o_conv, o_cb, hold, a_ref, b_ref, c_ref, conv, sems, conv_sems,
):
    ins = [pltpu.make_async_copy(ref, hold.at[n], sems.at[n]) for n, ref in enumerate((res_ref, ig_ref))]
    moves = [pltpu.make_async_copy(hold.at[n], ref, sems.at[2 + n]) for n, ref in enumerate((o_res, o_ig))]
    sums = [
        pltpu.make_async_copy(src, dst, sems.at[4 + n])
        for n, (src, dst) in enumerate(((c_hbm, c_ref), (a_hbm, a_ref), (b_hbm, b_ref)))
    ]
    for m in sums + ins:
        m.start()
    sums[0].wait()

    def block(ref, at, rows=CR):
        return ref[at : at + rows, :].astype(f32)

    def halves(v):
        return v, pltpu.roll(v, 64, 1)

    tails = []
    for n in range(5):
        tails += halves(block(c_ref, C_MIX + n * CR))
    for a in range(3):
        for b in range(3):
            v = jnp.concatenate([block(c_ref, (a * 3 + b) * CR), tails[a * 3 + b]], axis=1)
            conv[a, b] = v[0:C, 0:C]
            moves.append(pltpu.make_async_copy(conv.at[a, b], o_conv.at[a, b], conv_sems.at[a * 3 + b]))
            moves[-1].start()
            if a == 1 and b == 1:
                o_cb[...] = v[C : C + 1, 0:C].reshape(C)
    sums[1].wait()
    sums[2].wait()
    for m, n in zip(ins, moves):
        m.wait()
        n.start()
    fc1 = [block(c_ref, C_FC1), block(c_ref, C_FC1 + CR), block(a_ref, 0)]
    fc1 = jnp.concatenate(fc1, axis=1)
    o_fc1[...] = fc1[0:C, 0:HID]
    o_f1b[...] = fc1[C : C + 1, 0:HID].reshape(HID)
    fc2 = jnp.concatenate([block(a_ref, (n + 1) * CR) for n in range(3)], axis=1)
    o_fc2t[...] = fc2[0:C, 0:HID]
    proj = jnp.concatenate([block(a_ref, 4 * CR), tails[9]], axis=1)
    for h in range(HEADS):
        at = h * HP_DIM
        o_proj[h * HEAD_DIM : (h + 1) * HEAD_DIM, :] = proj[at : at + HEAD_DIM, 0:C]
    o_pb[...] = proj[HEAD_DIM : HEAD_DIM + 1, 0:C].reshape(C)
    wide = lax.broadcasted_iota(jnp.int32, (CP, CP), 0)
    dense = lax.broadcasted_iota(jnp.int32, (CP, CP), 1)
    heads_out = (wide == dense + lax.div(dense, HEAD_DIM) * (HP_DIM - HEAD_DIM)) & (dense < C)
    heads_out = heads_out.astype(bf16)
    rest = halves(block(b_ref, 3 * CR)) + halves(block(b_ref, 4 * CR))
    for n in range(3):
        v = jnp.concatenate([block(b_ref, n * CR), rest[n]], axis=1).astype(bf16)
        v = dot(v, heads_out)
        o_qkv[:, n * C : (n + 1) * C] = v[0:C, 0:C]
        if n != 1:
            o_qvb[n // 2 * C : (n // 2 + 1) * C] = v[C : C + 1, 0:C].reshape(C)
    small = jnp.concatenate([block(b_ref, B_SMALL, 16), block(b_ref, B_SMALL + 16, 16)], axis=1)
    o_table[...] = small[0:HEADS, 0 : o_table.shape[1]]
    for n, ref in ((0, o_n1g), (1, o_n1b)):
        v = jnp.concatenate([d_ref[n : n + 1, :], d_ref[n + 2 : n + 3, :]], axis=1)
        ref[...] = v[:, 0:C].reshape(C)
    for n, ref in ((8, o_n2g), (9, o_n2b), (12, o_f2b)):
        ref[...] = small[n : n + 1, 0:C].reshape(C)
    for m in moves:
        m.wait()


def score_terms(table, extra):
    table = jnp.concatenate([table * LOG2E, jnp.zeros((2, table.shape[1]), f32)], axis=0)
    table = jnp.concatenate([table, jnp.zeros((8, CP - table.shape[1]), f32)], axis=1)
    shifted = [pltpu.roll(table, x, 1) if x else table for x in range(WIN)]
    row = lax.broadcasted_iota(jnp.int32, (AREA, CP), 0)
    lane = lax.broadcasted_iota(jnp.int32, (AREA, CP), 1)
    put = (lane == row + (row >> 3) * (WIN - 1)).astype(bf16)
    shape = (AREA, AREA)
    j = lax.broadcasted_iota(jnp.int32, shape, 0)
    i = lax.broadcasted_iota(jnp.int32, shape, 1)
    rows_differ = ((j >> 5) & 1) != ((i >> 5) & 1)
    cols_differ = ((j >> 2) & 1) != ((i >> 2) & 1)
    masks = [None, cols_differ, rows_differ, rows_differ | cols_differ]
    for h in range(HEADS):
        base = jnp.concatenate([t[h : h + 1] for t in shifted], axis=0)
        wide = jnp.concatenate(
            [pltpu.roll(base, CP - (112 - 15 * y), 1) for y in range(WIN)], axis=0
        )
        high = wide.astype(bf16)
        rest = wide - high.astype(f32)
        mid = rest.astype(bf16)
        low = (rest - mid.astype(f32)).astype(bf16)
        term = dot(high, put, 1, 1) + dot(mid, put, 1, 1) + dot(low, put, 1, 1)
        for n, mask in enumerate(masks):
            value = term if mask is None else term + jnp.where(mask, -100.0 * LOG2E, 0.0)
            extra[n, :, h * AREA : (h + 1) * AREA] = value


def table_sum(d_rel):
    row = lax.broadcasted_iota(jnp.int32, (AREA, CP), 0)
    lane = lax.broadcasted_iota(jnp.int32, (AREA, CP), 1)
    put = (lane == row + lax.div(row, WIN) * (WIN - 1)).astype(bf16)
    heads = []
    for h in range(HEADS):
        v = d_rel[:, h * AREA : (h + 1) * AREA]
        v1 = v.astype(bf16)
        v2 = (v - v1.astype(f32)).astype(bf16)
        wide = dot(v1, put) + dot(v2, put)
        total = None
        for y in range(WIN):
            part = pltpu.roll(wide[y * WIN : (y + 1) * WIN, :], 112 - 15 * y, 1)
            total = part if total is None else total + part
        heads.append(total)
    out = None
    for x in range(WIN):
        rows = jnp.concatenate([t[x : x + 1] for t in heads] + [jnp.zeros((2, CP), f32)], axis=0)
        rows = pltpu.roll(rows, CP - x, 1) if x else rows
        out = rows if out is None else out + rows
    return out


VM = pl.BlockSpec(memory_space=pltpu.VMEM)
SM = pl.BlockSpec(memory_space=pltpu.SMEM)
HB = pl.BlockSpec(memory_space=pl.ANY)


def up_to(n, m):
    return (n + m - 1) // m * m


def run_layer(stripes, imgs, *operands):
    S = jax.ShapeDtypeStruct
    V = pltpu.VMEM
    chips = stripes // 2
    dma = pltpu.SemaphoreType.DMA
    sems = 2 * (chips + imgs - 1)
    pieces, splits, buffers, outs = [], [], [], []
    for used, zsplit in ((A_USED, True), (B_USED, False), (C_USED, True)):
        zsplit = zsplit and stripes * imgs * 16 <= 2 * used
        splits.append(zsplit)
        parts = stripes * imgs if zsplit else stripes
        piece = up_to(-(-used // parts), 16)
        group = piece * imgs if zsplit else piece
        pieces.append(piece)
        outs.append(S((stripes * group, 128), bf16))
        buffers += [
            V((stripes * group, 128), bf16),
            V((chips * group, 128), bf16),
            V(((chips - 1) * group, 128), bf16),
            V(((imgs - 1) * piece, 128), bf16),
        ]
    return pl.pallas_call(
        functools.partial(layer_kernel, chips, imgs, tuple(pieces), tuple(splits)),
        out_shape=(S((16 * C, 256), bf16), S((16 * C, 256), bf16), *outs, S((8, 128), f32)),
        in_specs=[SM, HB, HB] + [VM] * 15,
        out_specs=[HB] * 2 + [VM] * 4,
        scratch_shapes=[
            V((CP, 3 * CP), bf16),
            V((CP, CP), bf16),
            V((CP, HP), bf16),
            V((CP, HP), bf16),
            V((3, CP, 3 * CP), bf16),
            V((16, 3 * CP), f32),
            V((4, AREA, HI), f32),
            V((CR, 3 * CP), f32),
            V((CR, CP), f32),
            V((CR, HP), f32),
            V((CR, HP), f32),
            V((3, CR, 3 * CP), f32),
            V((40, CP), f32),
            V((AREA, HI), f32),
            V((21, 256, C), bf16),
            V((20, 256, C), bf16),
            V((8, 256, CP), f32),
            V((8, 256, CP), f32),
            V((20 * 256, 3 * CP), bf16),
            V((24 * 256, CP), bf16),
            V((4096, CP), bf16),
            V((4096, CP), bf16),
            V((4096, 3 * CP), bf16),
            V((4096, HI), bf16),
            V((512, CP), bf16),
            V((2048, CP), f32),
            V((4096, CP), f32),
            V((4096, CP), bf16),
            V((20, 256, C), bf16),
            V((WIN, WIN, CP), f32),
            V((128, 128), bf16),
            V((C, C), bf16),
            V((16 * C, 128), f32),
            V((544, CP), f32),
            *buffers,
            V((4, 8, 128), f32),
            V((chips + imgs - 1, 8, 128), f32),
            dma((4,)),
            dma((6,)),
            dma((6,)),
        ]
        + [dma((sems,))] * 6
        + [dma((chips + imgs - 1,))] * 2,
        compiler_params=pltpu.CompilerParams(
            vmem_limit_bytes=63 * 1024 * 1024, collective_id=0, has_side_effects=True
        ),
        name="layer",
    )(*operands)


def run_finish(res, ig, a, b, c, d, table):
    S = jax.ShapeDtypeStruct
    return pl.pallas_call(
        finish_kernel,
        in_specs=[HB] * 5 + [VM],
        out_specs=(HB,) * 2 + (VM,) * 13 + (HB, VM),
        scratch_shapes=[
            pltpu.VMEM((2, *res.shape), bf16),
            *[pltpu.VMEM(v.shape, v.dtype) for v in (a, b, c)],
            pltpu.VMEM((3, 3, C, C), f32),
            pltpu.SemaphoreType.DMA((7,)),
            pltpu.SemaphoreType.DMA((9,)),
        ],
        out_shape=(
            S(res.shape, bf16),
            S(ig.shape, bf16),
            S((C,), f32),
            S((C,), f32),
            S((C, 3 * C), f32),
            S((2 * C,), f32),
            S((HEADS, table), f32),
            S((C, C), f32),
            S((C,), f32),
            S((C,), f32),
            S((C,), f32),
            S((C, HID), f32),
            S((HID,), f32),
            S((C, HID), f32),
            S((C,), f32),
            S((3, 3, C, C), f32),
            S((C,), f32),
        ),
        compiler_params=pltpu.CompilerParams(vmem_limit_bytes=63 * 1024 * 1024),
        name="finish",
    )(res, ig, a, b, c, d)


def on_device(
    images, widths, norm1_gain, norm1_bias, qkv_weight, qv_bias, bias_table, proj_weight, proj_bias,
    norm2_gain, norm2_bias, fc1_weight, fc1_bias, fc2_weight, fc2_bias, conv_weight, conv_bias, cotangent,
):
    count, rows_here, width, chans = images.shape
    img, cot = [
        v.reshape(rows_here, width, chans).transpose(2, 0, 1).reshape(chans * rows_here, width)
        for v in (images, cotangent)
    ]
    scal = lax.div(widths, WIN)
    res, ig, a, b, c, d = run_layer(
        lax.axis_size("rows"), lax.axis_size("imgs"),
        scal, img, cot, qkv_weight, proj_weight, fc1_weight, fc2_weight.T, conv_weight, bias_table.T,
        norm1_gain, norm1_bias, qv_bias, proj_bias, norm2_gain, norm2_bias, fc1_bias, fc2_bias, conv_bias,
    )
    res, ig, *grads = run_finish(res, ig, a, b, c, d, bias_table.shape[0])
    res, ig = [v.reshape(chans, rows_here, width).transpose(1, 2, 0) for v in (res, ig)]
    grads[4] = grads[4].T
    grads[11] = grads[11].T
    return (res[None], ig[None], *grads)


def solution(mesh):
    big = P("imgs", "rows", None, None)
    in_specs = (big, P("imgs")) + (P(),) * 15 + (big,)
    out_specs = (big, big) + (P(),) * 15
    return jax.shard_map(
        on_device, mesh=mesh, in_specs=in_specs, out_specs=out_specs, check_vma=False
    )
```
